32 devices in a mesh: dp: 8 (over z, x), tp: 4 (over y, core).
Axes of the slice: x: 2, y: 2, z: 4, core: 2. Of those that a mesh axis runs over, the one named last changes fastest.
Arguments:
- tokens: bfloat16 [28416, 768], P(('dp', 'tp')), may hold values from -6 to 6
- cotangent: bfloat16 [28416, 768], P(('dp', 'tp')), may hold values from -6 to 6
- patch_rank: int32 [48, 577], P('dp'), may hold values from 0 to 576, as said below
- kept_counts: int32 [48], P('dp'), may hold values from 289 to 577, as said below
- norm1_gain: bfloat16 [768], replicated, may hold values from 0.5 to 1.5
- norm1_shift: bfloat16 [768], replicated, may hold values from -1 to 1
- qkv_weight: bfloat16 [768, 3, 768], P(None, None, 'tp'), may hold values from -0.21875 to 0.21875
- query_bias: bfloat16 [768], P('tp'), may hold values from -3 to 3
- value_bias: bfloat16 [768], P('tp'), may hold values from -3 to 3
- out_weight: bfloat16 [768, 768], P('tp'), may hold values from -2.5 to 2.5
- out_bias: bfloat16 [768], replicated, may hold values from -2 to 2
- router_weight: bfloat16 [768], replicated, may hold values from -0.21875 to 0.21875
- norm2_gain: bfloat16 [768], replicated, may hold values from 0.5 to 1.5
- norm2_shift: bfloat16 [768], replicated, may hold values from -1 to 1
- fc1_weight: bfloat16 [768, 3072], P(None, 'tp'), may hold values from -0.21875 to 0.21875
- fc1_bias: bfloat16 [3072], P('tp'), may hold values from -3 to 3
- fc2_weight: bfloat16 [3072, 768], P('tp'), may hold values from -0.109375 to 0.109375
- fc2_bias: bfloat16 [768], replicated, may hold values from -2 to 2
Outputs:
- block_out: bfloat16 [28416, 768], P(('dp', 'tp'))
- input_grad: float32 [28416, 768], P(('dp', 'tp'))
- norm1_gain_grad: float32 [768], replicated
- norm1_shift_grad: float32 [768], replicated
- qkv_weight_grad: float32 [768, 3, 768], P(None, None, 'tp')
- query_bias_grad: float32 [768], P('tp')
- value_bias_grad: float32 [768], P('tp')
- out_weight_grad: float32 [768, 768], P('tp')
- out_bias_grad: float32 [768], replicated
- router_grad: float32 [768], replicated
- norm2_gain_grad: float32 [768], replicated
- norm2_shift_grad: float32 [768], replicated
- fc1_weight_grad: float32 [768, 3072], P(None, 'tp')
- fc1_bias_grad: float32 [3072], P('tp')
- fc2_weight_grad: float32 [3072, 768], P('tp')
- fc2_bias_grad: float32 [768], replicated
The draws below stay inside these ranges and needn't reach their ends.
Inputs may be any that keep to these rules, and one draw needn't show every extreme that they name: `patch_rank`: each image's row holds every number 0 to 576 once. `kept_counts`: some image keeps all 577 patches.
All inputs are finite; a program needn't handle non-finite values.
Results may differ from the reference program's by a relative error of at most 0.012.
The reference program's roundings to bfloat16 on the way count: a program that leaves them out, or rounds other values in their place, can miss the bound.
Values may be sent and summed in bfloat16 or wider, within the bound.
No kernel may reach another device: no remote copies, remote signals or barrier semaphores. Data moves between devices by JAX's collectives and lax.ppermute only.
A program may use at most 192 MiB of HBM per device.

```python
import jax
import jax.numpy as jnp
from jax import lax

D = 768
HEADS = 12
HEAD = 64
FF = 3072
PATCHES = 577
SEQ = 592
IMAGES = 48
TOKENS = 28416


def draw_patch_rank(key, part):
    key = jax.random.fold_in(key, 11)
    image_keys = jax.random.split(key, IMAGES)
    return jax.vmap(lambda one_key: jax.random.permutation(one_key, PATCHES))(image_keys).astype(jnp.int32)


def draw_kept_counts(key, part):
    key = jax.random.fold_in(key, 23)
    first_key, second_key = jax.random.split(key)
    counts = jax.random.randint(first_key, (IMAGES,), PATCHES // 2 + 1, PATCHES + 1)
    chosen = jax.random.randint(second_key, (), 0, IMAGES)
    return counts.at[chosen].set(PATCHES).astype(jnp.int32)


def level_of(stream_key, shape, cuts, low, top_value):
    def one(dim, blocks):
        draws = jax.random.uniform(jax.random.fold_in(jax.random.fold_in(stream_key, 6), dim), (blocks,), jnp.float32, low / len(cuts), top_value / len(cuts))
        return jnp.repeat(jnp.exp(draws), shape[dim] // blocks).reshape((-1,) + (1,) * (len(shape) - dim - 1))

    loudness = one(*cuts[0])
    for cut in cuts[1:]:
        loudness = loudness * one(*cut)
    return loudness


def gaussian(key, dims, deviation, limit, pieces=(), held_as=jnp.bfloat16):
    gain = level_of(key, dims, pieces, -0.22, 0.18) if pieces else 1.0
    entries = jax.random.normal(key, dims, jnp.float32) * deviation * gain
    return jnp.minimum(jnp.maximum(entries, -limit), limit).astype(held_as)


def setup_inputs(seed: int = 0) -> dict:
    key_list = jax.random.split(jax.random.key(seed), 19)
    tokens = gaussian(key_list[0], (TOKENS, D), 1.0, 6.0, ((0, 32),))
    cotangent = gaussian(key_list[1], (TOKENS, D), 1.0, 6.0, ((0, 32),))
    patch_rank = draw_patch_rank(jax.random.fold_in(key_list[18], 71), 0)
    kept_counts = draw_kept_counts(jax.random.fold_in(key_list[18], 71), 0)
    norm1_gain = jnp.clip(1.0 + 0.1 * jax.random.normal(key_list[4], (D,), jnp.float32), 0.5, 1.5).astype(jnp.bfloat16)
    norm1_shift = gaussian(key_list[5], (D,), 0.2, 1.0)
    qkv_weight = gaussian(key_list[6], (D, 3, D), D ** -0.5, 0.21875, ((2, 4),))
    query_bias = gaussian(key_list[7], (D,), 0.5, 3.0, ((0, 4),))
    value_bias = gaussian(key_list[8], (D,), 0.5, 3.0, ((0, 4),))
    out_weight = gaussian(key_list[9], (D, D), (max(D // 128, 2)) ** -0.5, 2.5, ((0, 4),))
    out_bias = gaussian(key_list[10], (D,), 0.3, 2.0)
    router_weight = gaussian(key_list[11], (D,), D ** -0.5, 0.21875)
    norm2_gain = jnp.clip(1.0 + 0.1 * jax.random.normal(key_list[12], (D,), jnp.float32), 0.5, 1.5).astype(jnp.bfloat16)
    norm2_shift = gaussian(key_list[13], (D,), 0.2, 1.0)
    fc1_weight = gaussian(key_list[14], (D, FF), D ** -0.5, 0.21875, ((1, 4),))
    fc1_bias = gaussian(key_list[15], (FF,), 0.5, 3.0, ((0, 4),))
    fc2_weight = gaussian(key_list[16], (FF, D), FF ** -0.5, 0.109375, ((0, 4),))
    fc2_bias = gaussian(key_list[17], (D,), 0.3, 2.0)
    return dict(tokens=tokens, cotangent=cotangent, patch_rank=patch_rank, kept_counts=kept_counts, norm1_gain=norm1_gain, norm1_shift=norm1_shift, qkv_weight=qkv_weight, query_bias=query_bias, value_bias=value_bias, out_weight=out_weight, out_bias=out_bias, router_weight=router_weight, norm2_gain=norm2_gain, norm2_shift=norm2_shift, fc1_weight=fc1_weight, fc1_bias=fc1_bias, fc2_weight=fc2_weight, fc2_bias=fc2_bias)


@jax.custom_vjp
def low(v):
    return lax.optimization_barrier(v.astype(jnp.bfloat16)).astype(jnp.float32)

@jax.custom_vjp
def low_back(v):
    return v

def low_keep(v):
    return (low(v), None)

def low_pass(kept, grad):
    return (grad,)

def back_keep(v):
    return (v, None)

def back_low(kept, grad):
    return (low(grad),)
low.defvjp(low_keep, low_pass)
low_back.defvjp(back_keep, back_low)
pair_images = 2
highest = lax.Precision.HIGHEST

def layer_norm(values, gain_vec, shift_vec):
    centre = values - lax.optimization_barrier(jnp.mean(values, axis=-1, keepdims=True))
    spread = lax.optimization_barrier(jnp.mean(centre * centre, axis=-1, keepdims=True))
    return centre * lax.rsqrt(spread + 1e-06) * gain_vec + shift_vec

def forward(param_set, token_rows, live):
    gain1, shift1, qkv_w, q_bias, v_bias, out_w, out_b, router_w, gain2, shift2, fc1_w, fc1_b, fc2_w, fc2_b = param_set

    def one_group(operands):
        rows_in, live_in = operands
        normed_one = low(layer_norm(rows_in, gain1, shift1))
        packed = jnp.einsum('rd,dcj->rcj', normed_one, qkv_w, precision=highest)
        shape_four = (pair_images, SEQ, HEADS, HEAD)
        queries = low(low_back(packed[:, 0] + q_bias)).reshape(shape_four)
        key_rows = low(low_back(packed[:, 1])).reshape(shape_four)
        value_rows = low(low_back(packed[:, 2] + v_bias)).reshape(shape_four)
        scores = low_back(jnp.einsum('bqhe,bkhe->bhqk', queries, key_rows, precision=highest) * HEAD ** (-0.5))
        live_keys = live_in.reshape(pair_images, SEQ)[:, None, None, :]
        scores = jnp.where(live_keys > 0, scores, -1e+30)
        weights = jnp.exp(scores - lax.optimization_barrier(jnp.max(scores, axis=-1, keepdims=True)))
        probs = low(weights / lax.optimization_barrier(jnp.sum(weights, axis=-1, keepdims=True)))
        mixed = jnp.einsum('bhqk,bkhe->bqhe', probs, value_rows, precision=highest)
        mixed = low(low_back(mixed.reshape(pair_images * SEQ, D)))
        attention = low_back(jnp.dot(mixed, out_w, precision=highest) + out_b)
        router_gate = jax.nn.sigmoid(jnp.dot(rows_in, router_w, precision=highest))[:, None] * live_in[:, None]
        hidden = rows_in + router_gate * attention
        normed_two = low(layer_norm(hidden, gain2, shift2))
        pre_act = low_back(jnp.dot(normed_two, fc1_w, precision=highest) + fc1_b)
        activated = low(jax.nn.gelu(pre_act, approximate=False))
        mlp_out = low_back(jnp.dot(activated, fc2_w, precision=highest) + fc2_b)
        return hidden + router_gate * mlp_out
    grouped = (token_rows.reshape(-1, pair_images * SEQ, D), live.reshape(-1, pair_images * SEQ))
    return lax.map(jax.checkpoint(one_group), grouped).reshape(-1, D)

def reference(tokens, cotangent, patch_rank, kept_counts, norm1_gain, norm1_shift, qkv_weight, query_bias, value_bias, out_weight, out_bias, router_weight, norm2_gain, norm2_shift, fc1_weight, fc1_bias, fc2_weight, fc2_bias):
    padded = jnp.concatenate([patch_rank.astype(jnp.int32), jnp.full((IMAGES, SEQ - PATCHES), PATCHES, jnp.int32)], axis=1)
    live = (padded < kept_counts.astype(jnp.int32)[:, None]).astype(jnp.float32).reshape(-1)
    param_set = tuple((weight_arr.astype(jnp.float32) for weight_arr in (norm1_gain, norm1_shift, qkv_weight, query_bias, value_bias, out_weight, out_bias, router_weight, norm2_gain, norm2_shift, fc1_weight, fc1_bias, fc2_weight, fc2_bias)))
    token_rows = tokens.astype(jnp.float32)
    result, pullback = jax.vjp(lambda params_in, rows_in: forward(params_in, rows_in, live), param_set, token_rows)
    grad_params, input_grad = pullback(cotangent.astype(jnp.float32))
    g_gain1, g_shift1, g_qkv, g_qbias, g_vbias, g_out, g_outb, g_router, g_gain2, g_shift2, g_fc1, g_fc1b, g_fc2, g_fc2b = grad_params
    return (result.astype(jnp.bfloat16), input_grad, g_gain1, g_shift1, g_qkv, g_qbias, g_vbias, g_out, g_outb, g_router, g_gain2, g_shift2, g_fc1, g_fc1b, g_fc2, g_fc2b)
```

```python
import functools

import jax
import jax.numpy as jnp
from jax import lax
from jax.experimental import pallas as pl
from jax.experimental.pallas import tpu as pltpu
from jax.sharding import PartitionSpec as P

HEAD = 64
PATCHES = 577
SEQ = 592
EPS = 1e-06
F32 = jnp.float32
BF16 = jnp.bfloat16
VMEM_BYTES = 60 * 1024 * 1024
CORE_SWAP = [(0, 1), (1, 0), (2, 3), (3, 2)]
Y_SWAP = [(0, 2), (1, 3), (2, 0), (3, 1)]

NN = (((1,), (0,)), ((), ()))
NT = (((1,), (1,)), ((), ()))
TN = (((0,), (0,)), ((), ()))


def mm(left, right, dims):
    return lax.dot_general(left, right, dims, preferred_element_type=F32)


def params(*semantics):
    return pltpu.CompilerParams(vmem_limit_bytes=VMEM_BYTES)


def whole(shape):
    rank = len(shape)
    return pl.BlockSpec(shape, lambda *ids: (0,) * rank)


def norm_parts(values):
    centre = values - jnp.mean(values, axis=-1, keepdims=True)
    inv = lax.rsqrt(jnp.mean(centre * centre, axis=-1, keepdims=True) + EPS)
    return centre * inv, inv


def split_three(column):
    high = column.astype(BF16).astype(F32)
    rest = column - high
    middle = rest.astype(BF16).astype(F32)
    return high, middle, (rest - middle).astype(BF16).astype(F32)


def pick(lane, base, columns, other):
    out = other
    for place, column in enumerate(columns):
        out = jnp.where(lane == base + place, column, out)
    return out


def attend_kernel(first, *refs):
    if first:
        (x_ref, gain_ref, shift_ref, w_ref, qb_ref, vb_ref, live_ref, normed_ref, qkv_ref, mix_ref, lse_ref) = refs
        scaled, _ = norm_parts(x_ref[...].astype(F32))
        normed = (scaled * gain_ref[...] + shift_ref[...]).astype(BF16)
        normed_ref[...] = normed
    else:
        x_ref, w_ref, qb_ref, vb_ref, live_ref, qkv_ref, mix_ref, lse_ref = refs
        normed = x_ref[...]
    width = w_ref.shape[0] // 3
    rows = normed.shape[0]
    empty = jnp.zeros((rows, 256 - width), BF16)
    queries = (mm(normed, w_ref[:width, :], NT) + qb_ref[...]).astype(BF16)
    qkv_ref[:, 0:width] = (queries.astype(F32) * HEAD**-0.5).astype(BF16)
    qkv_ref[:, width:256] = empty
    qkv_ref[:, 256 : 256 + width] = mm(normed, w_ref[width : 2 * width, :], NT).astype(BF16)
    qkv_ref[:, 256 + width : 512] = empty
    qkv_ref[:, 512 : 512 + width] = (mm(normed, w_ref[2 * width :, :], NT) + vb_ref[...]).astype(BF16)
    qkv_ref[:, 512 + width : 768] = empty
    lane = lax.broadcasted_iota(jnp.int32, (rows, 128), 1)
    key_bias = jnp.where(live_ref[...] > 0, 0.0, -1e30)
    lse_all = jnp.zeros((rows, 128), F32)
    for pair in range(2):
        base = pair * 128
        q_pair = qkv_ref[:, base : base + 128].astype(F32)
        k_pair = qkv_ref[:, 256 + base : 384 + base].astype(F32)
        v_pair = qkv_ref[:, 512 + base : 640 + base].astype(F32)
        mixed = jnp.zeros((rows, 128), F32)
        for side in range(2 if pair == 0 else 1):
            inside = (lane >= side * 64) & (lane < side * 64 + 64)
            extra = 64 - side * 64
            q_ext = jnp.where(inside, q_pair, jnp.where(lane == extra, 1.0, 0.0)).astype(BF16)
            k_ext = jnp.where(inside, k_pair, jnp.where(lane == extra, key_bias, 0.0)).astype(BF16)
            v_own = jnp.where(inside, v_pair, 0.0).astype(BF16)
            scores = mm(q_ext, k_ext, NT)
            top = jnp.max(scores, axis=-1, keepdims=True)
            weights = jnp.exp(scores - top)
            total = jnp.sum(weights, axis=-1, keepdims=True)
            mixed = mixed + mm(weights.astype(BF16), v_own, NN) * (1.0 / total)
            lse_all = jnp.where(lane == pair * 2 + side, top + jnp.log(total), lse_all)
        mix_ref[:, base : base + 128] = mixed.astype(BF16)
    lse_ref[...] = lse_all


def attend_call(first, x, extras, weight, q_bias, v_bias, live_col):
    rows = x.shape[0]
    dim = x.shape[1]
    width = weight.shape[0] // 3
    block = lambda lanes: pl.BlockSpec((SEQ, lanes), lambda i: (i, 0))
    shapes = [((rows, 768), BF16), ((rows, 256), BF16), ((rows, 128), F32)]
    if first:
        shapes = [((rows, dim), BF16)] + shapes
    return pl.pallas_call(
        functools.partial(attend_kernel, first),
        grid=(rows // SEQ,),
        in_specs=[block(dim)]
        + [whole(e.shape) for e in extras]
        + [whole(weight.shape), whole((1, width)), whole((1, width)), block(1)],
        out_specs=[block(s[1]) for s, _ in shapes],
        out_shape=[jax.ShapeDtypeStruct(s, d) for s, d in shapes],
        compiler_params=params(),
        name="attend",
    )(x, *extras, weight, q_bias, v_bias, live_col)


def hidden_kernel(mix_ref, w_ref, bias_ref, x_ref, cot_ref, live_ref, router_ref, gain_ref, shift_ref,
                  attn_ref, hidden_ref, normed_ref, gm_ref, sig_ref):
    x = x_ref[...].astype(F32)
    attention = mm(mix_ref[...], w_ref[...], NN) + bias_ref[...]
    sig = jax.nn.sigmoid(jnp.sum(x * router_ref[...], axis=-1, keepdims=True))
    gate = live_ref[...] * sig
    hidden = x + gate * attention
    scaled, _ = norm_parts(hidden)
    pad = jnp.zeros((normed_ref.shape[0] - x.shape[0], x.shape[1]), F32)
    attn_ref[...] = attention
    hidden_ref[...] = hidden
    normed_ref[...] = jnp.concatenate([scaled * gain_ref[...] + shift_ref[...], pad], axis=0).astype(BF16)
    gm_ref[...] = jnp.concatenate([gate * cot_ref[...].astype(F32), pad], axis=0).astype(BF16)
    sig_ref[...] = sig


def hidden_call(mix, weight, bias, x, cot, live_col, router, gain, shift):
    rows, dim = x.shape
    padded = -(-rows // 16) * 16
    args = (mix, weight, bias, x, cot, live_col, router, gain, shift)
    shapes = [((rows, dim), F32), ((rows, dim), F32), ((padded, dim), BF16), ((padded, dim), BF16), ((rows, 1), F32)]
    return pl.pallas_call(
        hidden_kernel,
        in_specs=[whole(a.shape) for a in args],
        out_specs=[whole(s) for s, _ in shapes],
        grid=(1,),
        out_shape=[jax.ShapeDtypeStruct(s, d) for s, d in shapes],
        compiler_params=params(),
        name="hidden",
    )(*args)


def ff_kernel(chunk, has_acc, *refs):
    n2_ref, gm_ref, a1, b1, a2, b2, bias_ref = refs[:7]
    refs = refs[7:]
    if has_acc:
        mlp_in, gn2_in = refs[:2]
        refs = refs[2:]
    mlp_ref, gn2_ref, da1, db1, da2, db2, dbias_ref = refs
    step = pl.program_id(0)
    half = pl.num_programs(0) // 2

    @pl.when(step == 0)
    def _():
        if has_acc:
            mlp_ref[...] = mlp_in[...]
            gn2_ref[...] = gn2_in[...]
        else:
            mlp_ref[...] = jnp.zeros_like(mlp_ref)
            gn2_ref[...] = jnp.zeros_like(gn2_ref)

    def work(w1, w2, d1, d2):
        n2 = n2_ref[...]
        gm = gm_ref[...]
        pre = mm(n2, w1[...], NN) + bias_ref[0]
        g_act = mm(gm, w2[...], NT)
        cdf = 0.5 * (1.0 + lax.erf(pre * (0.5**0.5)))
        act = (pre * cdf).astype(BF16)
        slope = cdf + pre * (jnp.exp(-0.5 * pre * pre) * (0.5 / jnp.pi) ** 0.5)
        g_pre32 = g_act * slope
        g_pre = g_pre32.astype(BF16)
        mlp_ref[...] += mm(act, w2[...], NN)
        d2[...] = mm(act, gm, TN).astype(BF16)
        d1[...] = mm(n2, g_pre, TN).astype(BF16)
        dbias_ref[0] = jnp.sum(g_pre.astype(F32), axis=0, keepdims=True)
        gn2_ref[...] += mm(g_pre, w1[...], NT)

    @pl.when(step < half)
    def _():
        work(a1, a2, da1, da2)

    @pl.when(step >= half)
    def _():
        work(b1, b2, db1, db2)


def ff_call(n2, gm, a, b, acc):
    rows, dim = n2.shape
    units = a[0].shape[1]
    chunk = units // 2
    first = lambda j: jnp.minimum(j, 1)
    second = lambda j: jnp.maximum(j - 2, 0)
    bias = jnp.concatenate([a[1], b[1]]).astype(F32).reshape(4, 1, chunk)
    col = lambda f: pl.BlockSpec((dim, chunk), lambda j: (0, f(j)))
    row = lambda f: pl.BlockSpec((chunk, dim), lambda j: (f(j), 0))
    bias_spec = pl.BlockSpec((1, 1, chunk), lambda j: (j, 0, 0))
    acc_specs = [whole((rows, dim)), whole((rows, dim))]
    acc_shapes = [jax.ShapeDtypeStruct((rows, dim), F32)] * 2
    ins = [n2, gm, a[0], b[0], a[2], b[2], bias]
    in_specs = [whole(n2.shape), whole(gm.shape), col(first), col(second), row(first), row(second), bias_spec]
    if acc is not None:
        ins += list(acc)
        in_specs += acc_specs
    out = pl.pallas_call(
        functools.partial(ff_kernel, chunk, acc is not None),
        grid=(4,),
        in_specs=in_specs,
        out_specs=acc_specs + [col(first), col(second), row(first), row(second), bias_spec],
        out_shape=acc_shapes
        + [jax.ShapeDtypeStruct((dim, units), BF16)] * 2
        + [jax.ShapeDtypeStruct((units, dim), BF16)] * 2
        + [jax.ShapeDtypeStruct((4, 1, chunk), F32)],
        compiler_params=params(),
        name="feed",
    )(*ins)
    mlp, gn2, da1, db1, da2, db2, dbias = out
    dbias = dbias.reshape(2, units)
    return (mlp, gn2), (da1, dbias[0], da2), (db1, dbias[1], db2)


def middle_kernel(mlp_ref, gn2_ref, hidden_ref, attn_ref, x_ref, cot_ref, live_ref, sig_ref, gm_ref, mix_ref,
                  w_ref, bias_ref, gain_ref, router_ref, block_ref, carry_ref, gmix_ref, dw_ref, vec_ref):
    rows = x_ref.shape[0]
    x = x_ref[...].astype(F32)
    cot = cot_ref[...].astype(F32)
    sig = sig_ref[...]
    live = live_ref[...]
    gate = live * sig
    hidden = hidden_ref[...]
    mlp = mlp_ref[:rows, :] + bias_ref[...]
    block_ref[...] = (hidden + gate * mlp).astype(BF16)
    scaled, inv = norm_parts(hidden)
    gn2 = gn2_ref[:rows, :]
    e = gn2 * gain_ref[...]
    grad_hidden = cot + inv * (
        e - jnp.mean(e, axis=-1, keepdims=True) - scaled * jnp.mean(e * scaled, axis=-1, keepdims=True)
    )
    gate_grad = jnp.sum(grad_hidden * attn_ref[...] + cot * mlp, axis=-1, keepdims=True)
    logit = live * gate_grad * sig * (1.0 - sig)
    carry_ref[...] = grad_hidden + logit * router_ref[...]
    pad = jnp.zeros((gm_ref.shape[0] - rows, x.shape[1]), F32)
    grad_attn = jnp.concatenate([gate * grad_hidden, pad], axis=0).astype(BF16)
    gmix = mm(grad_attn, w_ref[...], NT)
    gmix_ref[...] = gmix[:rows, :].astype(BF16)
    mix = jnp.concatenate([mix_ref[...].astype(F32), pad], axis=0).astype(BF16)
    dw_ref[...] = mm(mix, grad_attn, TN).astype(BF16)
    add = lambda v: jnp.sum(v, axis=0, keepdims=True)
    vec_ref[0:1, :] = add(gn2 * scaled)
    vec_ref[1:2, :] = add(gn2)
    vec_ref[2:3, :] = add(grad_attn.astype(F32))
    vec_ref[3:4, :] = add(gm_ref[...].astype(F32))
    vec_ref[4:5, :] = add(x * logit)
    vec_ref[5:8, :] = jnp.zeros((3, x.shape[1]), F32)


def middle_call(*args):
    x = args[4]
    rows, dim = x.shape
    shapes = [((rows, dim), BF16), ((rows, dim), F32), ((rows, dim), BF16), ((dim, dim), BF16), ((8, dim), F32)]
    return pl.pallas_call(
        middle_kernel,
        in_specs=[whole(a.shape) for a in args],
        out_specs=[whole(s) for s, _ in shapes],
        grid=(1,),
        out_shape=[jax.ShapeDtypeStruct(s, d) for s, d in shapes],
        compiler_params=params(),
        name="middle",
    )(*args)


def attend_back_kernel(has_acc, *refs):
    qkv_ref, mix_ref, lse_ref, gmix_ref, live_ref, normed_ref, w_ref = refs[:7]
    refs = refs[7:]
    if has_acc:
        gn_in = refs[0]
        refs = refs[1:]
    dw_ref, gn_ref, bias_ref, gp_ref, acc_ref, bacc_ref = refs
    rows = qkv_ref.shape[0]
    width = w_ref.shape[0] // 3
    lane = lax.broadcasted_iota(jnp.int32, (rows, 128), 1)
    key_bias = jnp.where(live_ref[...] > 0, 0.0, -1e30)
    lse_all = lse_ref[...]
    for pair in range(2):
        base = pair * 128
        q_pair = qkv_ref[:, base : base + 128].astype(F32)
        k_pair = qkv_ref[:, 256 + base : 384 + base].astype(F32)
        v_pair = qkv_ref[:, 512 + base : 640 + base].astype(F32)
        m_pair = mix_ref[:, base : base + 128].astype(F32)
        if pair == 0:
            g_pair = gmix_ref[:, 0:128].astype(F32)
        else:
            g_pair = jnp.concatenate([gmix_ref[:, 128:192].astype(F32), jnp.zeros((rows, 64), F32)], axis=1)
        gq = jnp.zeros((rows, 128), F32)
        gk = jnp.zeros((rows, 128), F32)
        gv = jnp.zeros((rows, 128), F32)
        for side in range(2 if pair == 0 else 1):
            inside = (lane >= side * 64) & (lane < side * 64 + 64)
            extra = 64 - side * 64
            lse = jnp.sum(jnp.where(lane == pair * 2 + side, lse_all, 0.0), axis=-1, keepdims=True)
            delta = jnp.sum(jnp.where(inside, g_pair * m_pair, 0.0), axis=-1, keepdims=True)
            l0, l1, l2 = split_three(lse)
            d0, d1, d2 = split_three(delta)
            one = jnp.ones((rows, 1), F32)
            q_ext = jnp.where(inside, q_pair, pick(lane, extra, (-l0, -l1, -l2, one), 0.0)).astype(BF16)
            k_ext = jnp.where(inside, k_pair, pick(lane, extra, (one, one, one, key_bias), 0.0)).astype(BF16)
            g_ext = jnp.where(inside, g_pair, pick(lane, extra, (-d0, -d1, -d2), 0.0)).astype(BF16)
            v_ext = jnp.where(inside, v_pair, pick(lane, extra, (one, one, one), 0.0)).astype(BF16)
            q_own = jnp.where(inside, q_pair, 0.0).astype(BF16)
            k_own = jnp.where(inside, k_pair, 0.0).astype(BF16)
            g_own = jnp.where(inside, g_pair, 0.0).astype(BF16)
            probs = jnp.exp(mm(k_ext, q_ext, NT))
            grad_scores = (probs * mm(v_ext, g_ext, NT)).astype(BF16)
            gv = gv + mm(probs.astype(BF16), g_own, NN)
            gk = gk + mm(grad_scores, q_own, NN)
            gq = gq + mm(grad_scores, k_own, TN)
        gp_ref[:, base : base + 128] = (gq * HEAD**-0.5).astype(BF16)
        gp_ref[:, 256 + base : 384 + base] = gk.astype(BF16)
        gp_ref[:, 512 + base : 640 + base] = gv.astype(BF16)
    normed = normed_ref[...]
    step = pl.program_id(0)
    total = jnp.zeros((rows, normed.shape[1]), F32)
    if has_acc:
        total = gn_in[...]
    for part in range(3):
        piece = gp_ref[:, part * 256 : part * 256 + width]
        total = total + mm(piece, w_ref[part * width : (part + 1) * width, :], NN)
        update = mm(piece, normed, TN)
        sums = jnp.sum(piece.astype(F32), axis=0, keepdims=True)

        @pl.when(step == 0)
        def _():
            acc_ref[part * width : (part + 1) * width, :] = update
            bacc_ref[part : part + 1, :] = sums

        @pl.when(step > 0)
        def _():
            acc_ref[part * width : (part + 1) * width, :] += update
            bacc_ref[part : part + 1, :] += sums

    gn_ref[...] = total

    @pl.when(step == pl.num_programs(0) - 1)
    def _():
        dw_ref[...] = acc_ref[...].astype(BF16)
        bias_ref[...] = bacc_ref[...]


def attend_back_call(qkv, mix, lse, gmix, live_col, normed, weight, acc):
    rows, dim = normed.shape
    width = weight.shape[0] // 3
    block = lambda lanes: pl.BlockSpec((SEQ, lanes), lambda i: (i, 0))
    ins = [qkv, mix, lse, gmix, live_col, normed, weight]
    in_specs = [block(a.shape[1]) for a in ins[:6]] + [whole(weight.shape)]
    if acc is not None:
        ins.append(acc)
        in_specs.append(block(dim))
    return pl.pallas_call(
        functools.partial(attend_back_kernel, acc is not None),
        grid=(rows // SEQ,),
        in_specs=in_specs,
        out_specs=[whole(weight.shape), block(dim), whole((3, width))],
        out_shape=[
            jax.ShapeDtypeStruct(weight.shape, BF16),
            jax.ShapeDtypeStruct((rows, dim), F32),
            jax.ShapeDtypeStruct((3, width), F32),
        ],
        scratch_shapes=[
            pltpu.VMEM((SEQ, 768), BF16),
            pltpu.VMEM(weight.shape, F32),
            pltpu.VMEM((3, width), F32),
        ],
        compiler_params=params(),
        name="attend_back",
    )(*ins)


def last_kernel(own_ref, other_ref, x_ref, carry_ref, gain_ref, grad_ref, vec_ref):
    gn = own_ref[...] + other_ref[...].astype(F32)
    scaled, inv = norm_parts(x_ref[...].astype(F32))
    f = gn * gain_ref[...]
    grad_ref[...] = carry_ref[...] + inv * (
        f - jnp.mean(f, axis=-1, keepdims=True) - scaled * jnp.mean(f * scaled, axis=-1, keepdims=True)
    )
    vec_ref[0:1, :] = jnp.sum(gn * scaled, axis=0, keepdims=True)
    vec_ref[1:2, :] = jnp.sum(gn, axis=0, keepdims=True)
    vec_ref[2:8, :] = jnp.zeros((6, gn.shape[1]), F32)


def last_call(*args):
    rows, dim = args[0].shape
    shapes = [((rows, dim), F32), ((8, dim), F32)]
    return pl.pallas_call(
        last_kernel,
        in_specs=[whole(a.shape) for a in args],
        out_specs=[whole(s) for s, _ in shapes],
        grid=(1,),
        out_shape=[jax.ShapeDtypeStruct(s, d) for s, d in shapes],
        compiler_params=params(),
        name="last",
    )(*args)


def plus(a, b):
    return (a.astype(F32) + b.astype(F32)).astype(BF16)


def reduce_dp(value, dp_size, dp_index):
    bits = []
    bit = 1
    while bit < dp_size:
        bits.append(bit)
        bit *= 2
    swap = lambda v, b: lax.ppermute(v, "dp", [(i, i ^ b) for i in range(dp_size)])
    for b in bits:
        half = value.shape[0] // 2
        side = (dp_index // b) % 2
        send = lax.dynamic_slice_in_dim(value, (1 - side) * half, half)
        keep = lax.dynamic_slice_in_dim(value, side * half, half)
        value = plus(keep, swap(send, b))
    for b in reversed(bits):
        side = (dp_index // b) % 2
        other = swap(value, b)
        value = jnp.where(
            side == 0, jnp.concatenate([value, other]), jnp.concatenate([other, value])
        )
    return value


def sum_dp(value, dp_size):
    b = 1
    while b < dp_size:
        value = value + lax.ppermute(value, "dp", [(i, i ^ b) for i in range(dp_size)])
        b *= 2
    return value


def body(
    dp_size,
    tokens, cotangent, patch_rank, kept_counts, norm1_gain, norm1_shift, qkv_weight, query_bias, value_bias,
    out_weight, out_bias, router_weight, norm2_gain, norm2_shift, fc1_weight, fc1_bias, fc2_weight, fc2_bias,
):
    rows, dim = tokens.shape
    images = patch_rank.shape[0]
    tp_index = lax.axis_index("tp")
    dp_index = lax.axis_index("dp")
    core = tp_index % 2
    chip = tp_index // 2
    core_swap = lambda v: lax.ppermute(v, "tp", CORE_SWAP)
    y_swap = lambda v: lax.ppermute(v, "tp", Y_SWAP)
    row_vec = lambda v: v.astype(F32).reshape(1, -1)

    padded = jnp.concatenate([patch_rank, jnp.full((images, SEQ - PATCHES), PATCHES, jnp.int32)], axis=1)
    live_image = (padded < kept_counts[:, None]).astype(F32)
    live_chip = lax.dynamic_slice_in_dim(live_image, chip * (images // 2), images // 2).reshape(-1, 1)
    live_own = lax.dynamic_slice_in_dim(live_chip, core * rows, rows)

    qkv_own = jnp.transpose(qkv_weight, (1, 2, 0)).reshape(-1, dim)
    bias_own = jnp.stack([query_bias, value_bias])
    qkv_y = y_swap(qkv_own)
    bias_y = y_swap(bias_own)
    out_y = y_swap(out_weight)
    fc1_y, fc2_y, fb_y = y_swap(fc1_weight), y_swap(fc2_weight), y_swap(fc1_bias)
    out_core = core_swap(out_weight)
    fc1_core, fc2_core, fb_core = core_swap(fc1_weight), core_swap(fc2_weight), core_swap(fc1_bias)
    out_yd = core_swap(out_y)
    fc1_yd, fc2_yd, fb_yd = core_swap(fc1_y), core_swap(fc2_y), core_swap(fb_y)

    tokens_other = core_swap(tokens)
    tokens_chip = jnp.where(
        core == 0, jnp.concatenate([tokens, tokens_other]), jnp.concatenate([tokens_other, tokens])
    )
    normed, qkv_a, mix_a, lse_a = attend_call(
        True, tokens_chip, (row_vec(norm1_gain), row_vec(norm1_shift)), qkv_own,
        row_vec(bias_own[0]), row_vec(bias_own[1]), live_chip,
    )
    qkv_b, mix_b, lse_b = attend_call(
        False, normed, (), qkv_y, row_vec(bias_y[0]), row_vec(bias_y[1]), live_chip
    )
    width = out_weight.shape[0]
    part = lambda v, side: lax.dynamic_slice(v, (side * rows, 0), (rows, width))
    send_mix = jnp.concatenate([part(mix_a, 1 - core), part(mix_b, 1 - core)], axis=1)
    mix_rows = jnp.concatenate([part(mix_a, core), part(mix_b, core), core_swap(send_mix)], axis=1)
    out_all = jnp.concatenate([out_weight, out_y, out_core, out_yd], axis=0)

    attn, hidden, n2, gm, sig = hidden_call(
        mix_rows, out_all, row_vec(out_bias), tokens, cotangent, live_own, row_vec(router_weight),
        row_vec(norm2_gain), row_vec(norm2_shift),
    )
    acc, d_y, d_yd = ff_call(n2, gm, (fc1_y, fb_y, fc2_y), (fc1_yd, fb_yd, fc2_yd), None)
    acc, d_own, d_core = ff_call(
        n2, gm, (fc1_weight, fc1_bias, fc2_weight), (fc1_core, fb_core, fc2_core), acc
    )
    block_out, carry, gmix, d_out, vec2 = middle_call(
        acc[0], acc[1], hidden, attn, tokens, cotangent, live_own, sig, gm, mix_rows, out_all,
        row_vec(fc2_bias), row_vec(norm2_gain), row_vec(router_weight),
    )
    tail = lambda d: jnp.concatenate([d[0], d[2]], axis=0)
    ff_y = plus(tail(d_y), core_swap(tail(d_yd)))
    ff_own = plus(tail(d_own), core_swap(tail(d_core)))
    ff_own = plus(ff_own, y_swap(ff_y))
    fb_sum_y = d_y[1] + core_swap(d_yd[1])
    fb_sum = d_own[1] + core_swap(d_core[1]) + y_swap(fb_sum_y)
    ff_grad = reduce_dp(ff_own, dp_size, dp_index)

    gmix_other = core_swap(gmix[:, 2 * width :])
    join = lambda lo: jnp.where(
        core == 0,
        jnp.concatenate([gmix[:, lo : lo + width], gmix_other[:, lo : lo + width]]),
        jnp.concatenate([gmix_other[:, lo : lo + width], gmix[:, lo : lo + width]]),
    )
    dqkv_y, gn1, qv_y = attend_back_call(qkv_b, mix_b, lse_b, join(width), live_chip, normed, qkv_y, None)
    dqkv, gn1, qv_own = attend_back_call(qkv_a, mix_a, lse_a, join(0), live_chip, normed, qkv_own, gn1)

    d_out_half = plus(d_out[: 2 * width], core_swap(d_out[2 * width :]))
    qo_y = jnp.concatenate([dqkv_y, d_out_half[width:]], axis=0)
    qo_own = plus(jnp.concatenate([dqkv, d_out_half[:width]], axis=0), y_swap(qo_y))
    qo_grad = reduce_dp(qo_own, dp_size, dp_index)
    qv_sum = qv_own + y_swap(qv_y)

    send_gn = lax.dynamic_slice_in_dim(gn1, (1 - core) * rows, rows).astype(BF16)
    keep_gn = lax.dynamic_slice_in_dim(gn1, core * rows, rows)
    input_grad, vec1 = last_call(keep_gn, core_swap(send_gn), tokens, carry, row_vec(norm1_gain))

    vec = jnp.concatenate([vec2[:5], vec1[:2]], axis=0)
    vec = vec + core_swap(vec)
    vec = sum_dp(vec + y_swap(vec), dp_size)
    own_vec = sum_dp(jnp.concatenate([qv_sum.reshape(-1), fb_sum]), dp_size)
    qv_all = own_vec[: 3 * width].reshape(3, width)

    qkv_grad = jnp.transpose(qo_grad[: 3 * width].astype(F32).reshape(3, width, dim), (2, 0, 1))
    return (
        block_out,
        input_grad,
        vec[5],
        vec[6],
        qkv_grad,
        qv_all[0],
        qv_all[2],
        qo_grad[3 * width :].astype(F32),
        vec[2],
        vec[4],
        vec[0],
        vec[1],
        ff_grad[:dim].astype(F32),
        own_vec[3 * width :],
        ff_grad[dim:].astype(F32),
        vec[3],
    )


def solution(mesh):
    return jax.shard_map(
        functools.partial(body, mesh.shape["dp"]),
        mesh=mesh,
        in_specs=(
            P(("dp", "tp"), None), P(("dp", "tp"), None), P("dp", None), P("dp"), P(), P(), P(None, None, "tp"),
            P("tp"), P("tp"), P("tp", None), P(), P(), P(), P(), P(None, "tp"), P("tp"), P("tp", None), P(),
        ),
        out_specs=(
            P(("dp", "tp"), None), P(("dp", "tp"), None), P(), P(), P(None, None, "tp"), P("tp"), P("tp"),
            P("tp", None), P(), P(), P(), P(), P(None, "tp"), P("tp"), P("tp", None), P(),
        ),
        check_vma=False,
    )
```

```python
import functools

import jax
import jax.numpy as jnp
from jax import lax
from jax.experimental import pallas as pl
from jax.experimental.pallas import tpu as pltpu
from jax.sharding import PartitionSpec as P

HEAD = 64
PATCHES = 577
SEQ = 592
EPS = 1e-06
F32 = jnp.float32
BF16 = jnp.bfloat16
VMEM_BYTES = 60 * 1024 * 1024
CORE_SWAP = [(0, 1), (1, 0), (2, 3), (3, 2)]
Y_SWAP = [(0, 2), (1, 3), (2, 0), (3, 1)]

NN = (((1,), (0,)), ((), ()))
NT = (((1,), (1,)), ((), ()))
TN = (((0,), (0,)), ((), ()))


def mm(left, right, dims):
    return lax.dot_general(left, right, dims, preferred_element_type=F32)


def params():
    return pltpu.CompilerParams(vmem_limit_bytes=VMEM_BYTES)


def cost(micros):
    return pl.CostEstimate(flops=int(micros * 0.165e9), bytes_accessed=int(micros * 0.15e6), transcendentals=0)


def whole(shape):
    rank = len(shape)
    return pl.BlockSpec(shape, lambda *ids: (0,) * rank)


def norm_parts(values):
    centre = values - jnp.mean(values, axis=-1, keepdims=True)
    inv = lax.rsqrt(jnp.mean(centre * centre, axis=-1, keepdims=True) + EPS)
    return centre * inv, inv


def split_three(column):
    high = column.astype(BF16).astype(F32)
    rest = column - high
    middle = rest.astype(BF16).astype(F32)
    return high, middle, (rest - middle).astype(BF16).astype(F32)


def pick(lane, base, columns, other):
    out = other
    for place, column in enumerate(columns):
        out = jnp.where(lane == base + place, column, out)
    return out


def attend_kernel(first, *refs):
    if first:
        x_ref, vec_ref, w_ref, qb_ref, vb_ref, live_ref, normed_ref, qkv_ref, mix_ref, lse_ref = refs
        scaled, _ = norm_parts(x_ref[...].astype(F32))
        normed = (scaled * vec_ref[0:1, :] + vec_ref[1:2, :]).astype(BF16)
        normed_ref[...] = normed
    else:
        x_ref, w_ref, qb_ref, vb_ref, live_ref, qkv_ref, mix_ref, lse_ref = refs
        normed = x_ref[...]
    width = w_ref.shape[0] // 3
    rows = normed.shape[0]
    lone = width - 128
    for at, base, size in ((0, 0, 128), (3 * 128, 128, lone)):
        cols = slice(base, base + size)
        project = lambda i: mm(normed, w_ref[at + i * size : at + (i + 1) * size, :], NT)
        queries = (project(0) + qb_ref[:, cols]).astype(BF16)
        qkv_ref[:, cols] = (queries.astype(F32) * HEAD**-0.5).astype(BF16)
        qkv_ref[:, 256 + base : 256 + base + size] = project(1).astype(BF16)
        qkv_ref[:, 512 + base : 512 + base + size] = (project(2) + vb_ref[:, cols]).astype(BF16)
    for i in range(3):
        qkv_ref[:, i * 256 + width : i * 256 + 256] = jnp.zeros((rows, 256 - width), BF16)
    lane = lax.broadcasted_iota(jnp.int32, (rows, 128), 1)
    key_bias = jnp.where(live_ref[...] > 0, 0.0, -1e30)
    lse_all = jnp.zeros((rows, 128), F32)
    for pair in range(2):
        base = pair * 128
        q_pair = qkv_ref[:, base : base + 128].astype(F32)
        k_pair = qkv_ref[:, 256 + base : 384 + base].astype(F32)
        v_pair = qkv_ref[:, 512 + base : 640 + base].astype(F32)
        mixed = jnp.zeros((rows, 128), F32)
        for side in range(2 if pair == 0 else 1):
            inside = (lane >= side * 64) & (lane < side * 64 + 64)
            extra = 64 - side * 64
            q_ext = jnp.where(inside, q_pair, jnp.where(lane == extra, 1.0, 0.0)).astype(BF16)
            k_ext = jnp.where(inside, k_pair, jnp.where(lane == extra, key_bias, 0.0)).astype(BF16)
            v_own = jnp.where(inside, v_pair, 0.0).astype(BF16)
            scores = mm(q_ext, k_ext, NT)
            top = jnp.max(scores, axis=-1, keepdims=True)
            weights = jnp.exp(scores - top)
            total = jnp.sum(weights, axis=-1, keepdims=True)
            mixed = mixed + mm(weights.astype(BF16), v_own, NN) * (1.0 / total)
            lse_all = jnp.where(lane == pair * 2 + side, top + jnp.log(total), lse_all)
        mix_ref[:, base : base + 128] = mixed.astype(BF16)
    lse_ref[...] = lse_all


def attend_call(first, x, extras, weight, q_bias, v_bias, live_col):
    rows = x.shape[0]
    dim = x.shape[1]
    width = weight.shape[0] // 3
    block = lambda lanes: pl.BlockSpec((SEQ, lanes), lambda i: (i, 0))
    shapes = [((rows, 768), BF16), ((rows, 256), BF16), ((rows, 128), F32)]
    if first:
        shapes = [((rows, dim), BF16)] + shapes
    return pl.pallas_call(
        functools.partial(attend_kernel, first),
        grid=(rows // SEQ,),
        in_specs=[block(dim)]
        + [whole(e.shape) for e in extras]
        + [whole(weight.shape), whole((1, width)), whole((1, width)), block(1)],
        out_specs=[block(s[1]) for s, _ in shapes],
        out_shape=[jax.ShapeDtypeStruct(s, d) for s, d in shapes],
        compiler_params=params(),
        cost_estimate=cost(13),
        name="attend",
    )(x, *extras, weight, q_bias, v_bias, live_col)


BLOCK = 224


def row_block(lanes):
    return pl.BlockSpec((BLOCK, lanes), lambda i: (i, 0))


def real_rows(rows):
    place = pl.program_id(0) * BLOCK + lax.broadcasted_iota(jnp.int32, (BLOCK, 1), 0)
    return place < rows


def hidden_kernel(rows, mix_ref, x_ref, cot_ref, live_ref, w_ref, vec_ref,
                  attn_ref, hidden_ref, normed_ref, gm_ref, sig_ref):
    x = x_ref[...].astype(F32)
    attention = mm(mix_ref[...], w_ref[...], NN) + vec_ref[2:3, :]
    sig = jax.nn.sigmoid(jnp.sum(x * vec_ref[3:4, :], axis=-1, keepdims=True))
    gate = live_ref[...] * sig
    hidden = x + gate * attention
    scaled, _ = norm_parts(hidden)
    real = real_rows(rows)
    attn_ref[...] = attention
    hidden_ref[...] = hidden
    normed_ref[...] = jnp.where(real, scaled * vec_ref[4:5, :] + vec_ref[5:6, :], 0.0).astype(BF16)
    gm_ref[...] = jnp.where(real, gate * cot_ref[...].astype(F32), 0.0).astype(BF16)
    sig_ref[...] = sig


def hidden_call(mix, x, cot, live_col, weight, vecs):
    rows, dim = x.shape
    steps = -(-rows // BLOCK)
    args = (mix, x, cot, live_col, weight, vecs)
    shapes = [((rows, dim), F32), ((rows, dim), F32), ((steps * BLOCK, dim), BF16), ((steps * BLOCK, dim), BF16),
              ((rows, 1), F32)]
    return pl.pallas_call(
        functools.partial(hidden_kernel, rows),
        in_specs=[row_block(a.shape[1]) for a in args[:4]] + [whole(a.shape) for a in args[4:]],
        out_specs=[row_block(s[1]) for s, _ in shapes],
        grid=(steps,),
        out_shape=[jax.ShapeDtypeStruct(s, d) for s, d in shapes],
        compiler_params=params(),
        cost_estimate=cost(7),
        name="hidden",
    )(*args)


def ff_kernel(n2_ref, gm_ref, a_ref, b_ref, bias_ref, mlp_ref, gn2_ref, da_ref, db_ref, dbias_ref,
              w1, w2, act_all, pre_all):
    half = w1.shape[0] // 2
    for i, piece in enumerate((a_ref, b_ref)):
        at = i * half
        w1[:, at : at + half] = piece[:, :half]
        w2[at : at + half, :half] = piece[:half, half:]
        w2[at : at + half, half:] = piece[half:, half:]
    steps = 2
    size = n2_ref.shape[0] // steps
    sums = 0.0
    for step in range(steps):
        at = slice(step * size, (step + 1) * size)
        pre = mm(n2_ref[at, :], w1[...], NN) + bias_ref[...]
        grad_act = mm(gm_ref[at, :], w2[...], NT)
        cdf = 0.5 * (1.0 + lax.erf(pre * (0.5**0.5)))
        slope = cdf + pre * (jnp.exp(-0.5 * pre * pre) * (0.5 / jnp.pi) ** 0.5)
        grad_pre = (grad_act * slope).astype(BF16)
        act_all[at, :] = (pre * cdf).astype(BF16)
        pre_all[at, :] = grad_pre
        sums = sums + jnp.sum(grad_pre.astype(F32), axis=0, keepdims=True)
        mlp_ref[at, :] = mm(act_all[at, :], w2[...], NN).astype(BF16)
        gn2_ref[at, :] = mm(pre_all[at, :], w1[...], NT).astype(BF16)
    dbias_ref[...] = sums
    d2 = mm(act_all[...], gm_ref[...], TN).astype(BF16)
    d1 = mm(n2_ref[...], pre_all[...], TN).astype(BF16)
    for i, grad in enumerate((da_ref, db_ref)):
        at = i * half
        grad[:, :half] = d1[:, at : at + half]
        grad[:half, half:] = d2[at : at + half, :half]
        grad[half:, half:] = d2[at : at + half, half:]


def ff_call(n2, gm, pieces, bias):
    rows, dim = n2.shape
    tall, square, line = whole((rows, dim)), whole((dim, dim)), whole((1, dim))
    out = pl.pallas_call(
        ff_kernel,
        grid=(1,),
        in_specs=[tall, tall, square, square, line],
        out_specs=[tall, tall, square, square, line],
        out_shape=[jax.ShapeDtypeStruct((rows, dim), BF16)] * 2
        + [jax.ShapeDtypeStruct((dim, dim), BF16)] * 2
        + [jax.ShapeDtypeStruct((1, dim), F32)],
        scratch_shapes=[pltpu.VMEM((dim, dim), BF16)] * 2 + [pltpu.VMEM((rows, dim), BF16)] * 2,
        compiler_params=params(),
        cost_estimate=cost(12),
        name="feed",
    )(n2, gm, *pieces, bias.reshape(1, dim))
    return out[:2], out[2:4], out[4].reshape(2, dim // 2)


def middle_kernel(rows, parts, *refs):
    mlp_refs, gn2_refs = refs[:parts], refs[parts : 2 * parts]
    (hidden_ref, attn_ref, x_ref, cot_ref, live_ref, sig_ref, gm_ref, mix_ref, w_ref, vec_ref,
     block_ref, carry_ref, gmix_ref, dw_ref, sum_ref, acc_ref) = refs[2 * parts :]
    step = pl.program_id(0)
    real = real_rows(rows)
    x = x_ref[...].astype(F32)
    cot = cot_ref[...].astype(F32)
    sig = sig_ref[...]
    gate = live_ref[...] * sig
    hidden = hidden_ref[...]
    mlp = vec_ref[6:7, :]
    gn2 = 0.0
    for ref in mlp_refs:
        mlp = mlp + ref[...].astype(F32)
    for ref in gn2_refs:
        gn2 = gn2 + ref[...].astype(F32)
    block_ref[...] = (hidden + gate * mlp).astype(BF16)
    scaled, inv = norm_parts(hidden)
    e = gn2 * vec_ref[4:5, :]
    grad_hidden = cot + inv * (
        e - jnp.mean(e, axis=-1, keepdims=True) - scaled * jnp.mean(e * scaled, axis=-1, keepdims=True)
    )
    gate_grad = jnp.sum(grad_hidden * attn_ref[...] + cot * mlp, axis=-1, keepdims=True)
    logit = live_ref[...] * gate_grad * sig * (1.0 - sig)
    carry_ref[...] = grad_hidden + logit * vec_ref[3:4, :]
    grad_attn = jnp.where(real, gate * grad_hidden, 0.0).astype(BF16)
    gmix_ref[...] = mm(grad_attn, w_ref[...], NT).astype(BF16)
    mix = jnp.where(real, mix_ref[...].astype(F32), 0.0).astype(BF16)
    update = mm(mix, grad_attn, TN)
    add = lambda v: jnp.sum(jnp.where(real, v, 0.0), axis=0, keepdims=True)
    sums = jnp.concatenate(
        [add(gn2 * scaled), add(gn2), add(grad_attn.astype(F32)), add(gm_ref[...].astype(F32)), add(x * logit),
         jnp.zeros((3, x.shape[1]), F32)], axis=0)

    @pl.when(step == 0)
    def _():
        acc_ref[...] = update
        sum_ref[...] = sums

    @pl.when(step > 0)
    def _():
        acc_ref[...] += update
        sum_ref[...] += sums

    @pl.when(step == pl.num_programs(0) - 1)
    def _():
        dw_ref[...] = acc_ref[...].astype(BF16)


def middle_call(mlp, gn2, *args):
    x, weight, vecs = args[2], args[8], args[9]
    rows, dim = x.shape
    shapes = [((rows, dim), BF16), ((rows, dim), F32), ((rows, dim), BF16)]
    ins = (*mlp, *gn2, *args)
    return pl.pallas_call(
        functools.partial(middle_kernel, rows, len(mlp)),
        in_specs=[row_block(a.shape[1]) for a in ins[:-2]] + [whole(weight.shape), whole(vecs.shape)],
        out_specs=[row_block(dim)] * 3 + [whole((dim, dim)), whole((8, dim))],
        grid=(-(-rows // BLOCK),),
        out_shape=[jax.ShapeDtypeStruct(s, d) for s, d in shapes]
        + [jax.ShapeDtypeStruct((dim, dim), BF16), jax.ShapeDtypeStruct((8, dim), F32)],
        scratch_shapes=[pltpu.VMEM((dim, dim), F32)],
        compiler_params=params(),
        cost_estimate=cost(11),
        name="middle",
    )(*ins)


def attend_back_kernel(pair, *refs):
    qkv_ref, mix_ref, lse_ref, gmix_ref, live_ref, normed_ref, dw_ref, gp_ref, bias_ref, gp_all = refs
    rows = qkv_ref.shape[0]
    width = gp_ref.shape[1] // 3
    base = pair * 128
    step = pl.program_id(0)
    lane = lax.broadcasted_iota(jnp.int32, (rows, 128), 1)
    key_bias = jnp.where(live_ref[...] > 0, 0.0, -1e30)
    lse_all = lse_ref[...]
    q_pair = qkv_ref[:, base : base + 128].astype(F32)
    k_pair = qkv_ref[:, 256 + base : 384 + base].astype(F32)
    v_pair = qkv_ref[:, 512 + base : 640 + base].astype(F32)
    m_pair = mix_ref[:, base : base + 128].astype(F32)
    g_pair = gmix_ref[:, base : base + width].astype(F32)
    if width < 128:
        g_pair = jnp.concatenate([g_pair, jnp.zeros((rows, 128 - width), F32)], axis=1)
    gq = jnp.zeros((rows, 128), F32)
    gk = jnp.zeros((rows, 128), F32)
    gv = jnp.zeros((rows, 128), F32)
    one = jnp.ones((rows, 1), F32)
    for side in range(width // 64):
        inside = (lane >= side * 64) & (lane < side * 64 + 64)
        extra = 64 - side * 64
        lse = jnp.sum(jnp.where(lane == pair * 2 + side, lse_all, 0.0), axis=-1, keepdims=True)
        delta = jnp.sum(jnp.where(inside, g_pair * m_pair, 0.0), axis=-1, keepdims=True)
        l0, l1, l2 = split_three(lse)
        d0, d1, d2 = split_three(delta)
        q_ext = jnp.where(inside, q_pair, pick(lane, extra, (-l0, -l1, -l2, one), 0.0)).astype(BF16)
        k_ext = jnp.where(inside, k_pair, pick(lane, extra, (one, one, one, key_bias), 0.0)).astype(BF16)
        g_ext = jnp.where(inside, g_pair, pick(lane, extra, (-d0, -d1, -d2), 0.0)).astype(BF16)
        v_ext = jnp.where(inside, v_pair, pick(lane, extra, (one, one, one), 0.0)).astype(BF16)
        q_own = jnp.where(inside, q_pair, 0.0).astype(BF16)
        k_own = jnp.where(inside, k_pair, 0.0).astype(BF16)
        g_own = jnp.where(inside, g_pair, 0.0).astype(BF16)
        probs = jnp.exp(mm(k_ext, q_ext, NT))
        grad_scores = (probs * mm(v_ext, g_ext, NT)).astype(BF16)
        gv = gv + mm(probs.astype(BF16), g_own, NN)
        gk = gk + mm(grad_scores, q_own, NN)
        gq = gq + mm(grad_scores, k_own, TN)
    sums = []
    for part, grad in enumerate((gq * HEAD**-0.5, gk, gv)):
        piece = grad.astype(BF16)[:, :width]
        gp_ref[:, part * width : (part + 1) * width] = piece
        sums.append(jnp.sum(piece.astype(F32), axis=0, keepdims=True))
    gp_all[pl.ds(pl.multiple_of(step * rows, 16), rows), :] = gp_ref[...]
    sums = jnp.concatenate(sums, axis=0)

    @pl.when(step == 0)
    def _():
        bias_ref[...] = sums

    @pl.when(step > 0)
    def _():
        bias_ref[...] += sums

    @pl.when(step == pl.num_programs(0) - 1)
    def _():
        dw_ref[...] = mm(gp_all[...], normed_ref[...], TN).astype(BF16)


def attend_back_call(pair, qkv, mix, lse, gmix, live_col, normed):
    rows, dim = normed.shape
    width = 128 if pair == 0 else gmix.shape[1] - 128
    block = lambda lanes: pl.BlockSpec((SEQ, lanes), lambda i: (i, 0))
    ins = [qkv, mix, lse, gmix, live_col, normed]
    return pl.pallas_call(
        functools.partial(attend_back_kernel, pair),
        grid=(rows // SEQ,),
        in_specs=[block(a.shape[1]) for a in ins[:5]] + [whole(normed.shape)],
        out_specs=[whole((3 * width, dim)), block(3 * width), whole((3, width))],
        out_shape=[
            jax.ShapeDtypeStruct((3 * width, dim), BF16),
            jax.ShapeDtypeStruct((rows, 3 * width), BF16),
            jax.ShapeDtypeStruct((3, width), F32),
        ],
        scratch_shapes=[pltpu.VMEM((rows, 3 * width), BF16)],
        compiler_params=params(),
        cost_estimate=cost(14 if pair == 0 else 8),
        name="attend_back",
    )(*ins)


def last_kernel(rows, splits, *refs):
    count = sum(len(s) for s in splits)
    gp_refs, w_refs = refs[:count], refs[count : count + len(splits)]
    x_ref, carry_ref, vec_ref, grad_ref, sum_ref = refs[count + len(splits) :]
    gn = 0.0
    at = 0
    for w_ref, widths in zip(w_refs, splits):
        start = 0
        for width in widths:
            gn = gn + mm(gp_refs[at][...], w_ref[start : start + width, :], NN)
            start += width
            at += 1
    scaled, inv = norm_parts(x_ref[...].astype(F32))
    f = gn * vec_ref[0:1, :]
    grad_ref[...] = carry_ref[...] + inv * (
        f - jnp.mean(f, axis=-1, keepdims=True) - scaled * jnp.mean(f * scaled, axis=-1, keepdims=True)
    )
    real = real_rows(rows)
    add = lambda v: jnp.sum(jnp.where(real, v, 0.0), axis=0, keepdims=True)
    sums = jnp.concatenate([add(gn * scaled), add(gn), jnp.zeros((6, gn.shape[1]), F32)], axis=0)

    @pl.when(pl.program_id(0) == 0)
    def _():
        sum_ref[...] = sums

    @pl.when(pl.program_id(0) > 0)
    def _():
        sum_ref[...] += sums


def last_call(groups, x, carry, vecs):
    rows, dim = x.shape
    gps = [g for _, parts in groups for g in parts]
    weights = [w for w, _ in groups]
    splits = tuple(tuple(g.shape[1] for g in parts) for _, parts in groups)
    return pl.pallas_call(
        functools.partial(last_kernel, rows, splits),
        in_specs=[row_block(g.shape[1]) for g in gps]
        + [whole(w.shape) for w in weights]
        + [row_block(dim), row_block(dim), whole(vecs.shape)],
        out_specs=[row_block(dim), whole((8, dim))],
        grid=(-(-rows // BLOCK),),
        out_shape=[jax.ShapeDtypeStruct((rows, dim), F32), jax.ShapeDtypeStruct((8, dim), F32)],
        compiler_params=params(),
        cost_estimate=cost(9),
        name="last",
    )(*gps, *weights, x, carry, vecs)


def total(*terms):
    out = terms[0].astype(F32)
    for term in terms[1:]:
        out = out + term.astype(F32)
    return out.astype(BF16)


def after(first, *rest):
    return lax.optimization_barrier((first, *rest))


def unxor(value, index):
    count = value.shape[0]
    bit = 1
    while bit < count:
        split = value.reshape(count // (2 * bit), 2, bit, *value.shape[1:])
        value = jnp.where((index // bit) % 2 == 1, jnp.flip(split, 1), split).reshape(value.shape)
        bit *= 2
    return value


def stages(size):
    out = []
    stride = 2
    while stride < size:
        radix = 4 if size % (stride * 4) == 0 else 2
        out.append((stride, radix))
        stride *= radix
    return out


def dp_swap(value, size, offset):
    return lax.ppermute(value, "dp", [(i, i ^ offset) for i in range(size)])


def scatter_rest(value, size, index):
    for stride, radix in stages(size):
        digit = (index // stride) % radix
        share = value.shape[0] // radix
        cut = lambda o: lax.dynamic_slice_in_dim(value, (digit ^ o) * share, share)
        value = total(cut(0), *[dp_swap(cut(o), size, o * stride) for o in range(1, radix)])
    return value


def gather_rest(value, size):
    for stride, radix in reversed(stages(size)):
        value = jnp.concatenate([value] + [dp_swap(value, size, o * stride) for o in range(1, radix)])
    return value


def natural_rest(value, size, index):
    order = 0
    for stride, radix in stages(size):
        order = order * radix + (index // stride) % radix
    blocks = value.reshape(size // 2, -1, value.shape[-1])
    return unxor(blocks, order).reshape(value.shape)


def scatter_side(value, side, size):
    half = value.shape[0] // 2
    send = lax.dynamic_slice_in_dim(value, (1 - side) * half, half)
    keep = lax.dynamic_slice_in_dim(value, side * half, half)
    return total(keep, dp_swap(send, size, 1))


def gather_side(mine, side, size, index):
    both = unxor(jnp.stack([mine, dp_swap(mine, size, 1)]), side)
    return jnp.concatenate([natural_rest(both[0], size, index), natural_rest(both[1], size, index)])


def sum_tp(value):
    return value + sum(lax.ppermute(value, "tp", [(i, i ^ o) for i in range(4)]) for o in range(1, 4))


def sum_rest(value, size):
    for stride, radix in stages(size):
        value = value + sum(dp_swap(value, size, o * stride) for o in range(1, radix))
    return value


def body(
    size,
    tokens, cotangent, patch_rank, kept_counts, norm1_gain, norm1_shift, qkv_weight, query_bias, value_bias,
    out_weight, out_bias, router_weight, norm2_gain, norm2_shift, fc1_weight, fc1_bias, fc2_weight, fc2_bias,
):
    rows, dim = tokens.shape
    half = dim // 2
    images = patch_rank.shape[0]
    tp_index = lax.axis_index("tp")
    index = lax.axis_index("dp")
    core = tp_index % 2
    chip = tp_index // 2
    side = index % 2
    core_swap = lambda v: lax.ppermute(v, "tp", CORE_SWAP)
    y_swap = lambda v: lax.ppermute(v, "tp", Y_SWAP)
    x_swap = lambda v: dp_swap(v, size, 1)
    row_vec = lambda v: v.astype(F32).reshape(1, -1)

    width = out_weight.shape[0]
    by_part = jnp.transpose(qkv_weight, (1, 2, 0))
    regroup = lambda w: jnp.concatenate([w[:, :128].reshape(-1, dim), w[:, 128:].reshape(-1, dim)])
    qkv_own = regroup(by_part)
    tokens_other = core_swap(tokens)
    qkv_y = y_swap(qkv_own)
    small_own = jnp.concatenate([query_bias, value_bias, fc1_bias]).astype(F32)
    small_y = y_swap(small_own)
    vecs = jnp.stack(
        [norm1_gain, norm1_shift, out_bias, router_weight, norm2_gain, norm2_shift, fc2_bias, fc2_bias]
    ).astype(F32)

    padded = jnp.concatenate([patch_rank, jnp.full((images, SEQ - PATCHES), PATCHES, jnp.int32)], axis=1)
    live_image = (padded < kept_counts[:, None]).astype(F32)
    live_chip = lax.dynamic_slice_in_dim(live_image, chip * (images // 2), images // 2).reshape(-1, 1)
    live_own = lax.dynamic_slice_in_dim(live_chip, core * rows, rows)

    def pack(s):
        w1 = lax.dynamic_slice_in_dim(fc1_weight, s * half, half, axis=1)
        w2 = lax.dynamic_slice_in_dim(fc2_weight, s * half, half)
        return jnp.concatenate([w1, jnp.concatenate([w2[:, :half], w2[:, half:]])], axis=1)

    own_k, own_s = pack(side), pack(1 - side)
    tokens_chip = jnp.where(
        core == 0, jnp.concatenate([tokens, tokens_other]), jnp.concatenate([tokens_other, tokens])
    )
    normed, qkv_a, mix_a, lse_a = attend_call(
        True, tokens_chip, (vecs,), qkv_own,
        row_vec(query_bias), row_vec(value_bias), live_chip,
    )
    normed, qkv_y, small_y, own_k, own_s, out_weight = after(normed, qkv_y, small_y, own_k, own_s, out_weight)
    out_y = y_swap(out_weight)
    y_k = y_swap(own_k)
    core_k, core_s, out_core, qkv_core = [core_swap(v) for v in (own_k, own_s, out_weight, qkv_own)]
    small_far = core_swap(jnp.stack([small_own, small_y]))

    qkv_b, mix_b, lse_b = attend_call(
        False, normed, (), qkv_y, row_vec(small_y[:width]), row_vec(small_y[width : 2 * width]), live_chip
    )
    mix_b, out_y = after(mix_b, out_y)
    out_yd = core_swap(out_y)
    part = lambda v, s: lax.dynamic_slice(v, (s * rows, 0), (rows, width))
    send_mix = jnp.concatenate([part(mix_a, 1 - core), part(mix_b, 1 - core)], axis=1)
    mix_rows = jnp.concatenate([part(mix_a, core), part(mix_b, core), core_swap(send_mix)], axis=1)
    out_all = jnp.concatenate([out_weight, out_y, out_core, out_yd], axis=0)

    attn, hidden, n2, gm, sig = hidden_call(mix_rows, tokens, cotangent, live_own, out_all, vecs)
    n2, y_k = after(n2, y_k)
    y_s = x_swap(y_k)
    yd_k = core_swap(y_k)
    halves = lambda v: unxor(v[2 * width :].reshape(2, half), side)
    b_own, b_y, b_core, b_yd = halves(small_own), halves(small_y), halves(small_far[0]), halves(small_far[1])

    sums1, (dy_k, dyd_k), fb1 = ff_call(n2, gm, (y_k, yd_k), jnp.stack([b_y[0], b_yd[0]]))
    n2, dyd_k, dy_k = after(n2, dyd_k, dy_k)
    ryd_k = core_swap(dyd_k)
    sums2, (do_s, dc_s), fb2 = ff_call(n2, gm, (own_s, core_s), jnp.stack([b_own[1], b_core[1]]))
    n2, do_s, dc_s, ryd_k, y_s = after(n2, do_s, dc_s, ryd_k, y_s)
    rc_s = core_swap(dc_s)
    yd_s = core_swap(y_s)
    y_k_sum = total(dy_k, ryd_k)
    own_s_sum = total(do_s, rc_s)
    n2, y_k_sum, own_s_sum, yd_s = after(n2, y_k_sum, own_s_sum, yd_s)
    from_y_k = y_swap(y_k_sum)
    from_x = x_swap(own_s_sum)
    sums3, (dy_s, dyd_s), fb3 = ff_call(n2, gm, (y_s, yd_s), jnp.stack([b_y[1], b_yd[1]]))
    n2, dy_s, dyd_s = after(n2, dy_s, dyd_s)
    ryd_s = core_swap(dyd_s)
    sums4, (do_k, dc_k), fb4 = ff_call(n2, gm, (own_k, core_k), jnp.stack([b_own[0], b_core[0]]))
    sums4, do_k, dc_k, ryd_s = after(sums4, do_k, dc_k, ryd_s)
    y_s_sum = total(dy_s, ryd_s)
    sums4, y_s_sum = after(sums4, y_s_sum)
    over_x = x_swap(y_s_sum[:half])
    over_y = y_swap(y_s_sum[half:])
    rc_k = core_swap(dc_k)

    four = (sums1, sums2, sums3, sums4)
    block_out, carry, gmix, d_out, vec2 = middle_call(
        [f[0] for f in four], [f[1] for f in four], hidden, attn, tokens, cotangent, live_own, sig, gm, mix_rows,
        out_all, vecs,
    )
    gmix, rc_k, from_x, from_y_k, over_x, over_y, vec2 = after(gmix, rc_k, from_x, from_y_k, over_x, over_y, vec2)
    gmix_other = core_swap(gmix[:, 2 * width :])
    over_xy = y_swap(over_x)
    over_yx = x_swap(over_y)
    rd_out = core_swap(d_out[2 * width :])
    ff_sum = total(do_k, rc_k, from_y_k, from_x)
    fb_k, fb_s = jnp.stack([fb4[0], fb4[1], fb1[0], fb1[1]]), jnp.stack([fb2[0], fb2[1], fb3[0], fb3[1]])
    fb = unxor(jnp.stack([fb_k, fb_s]), side).transpose(1, 0, 2).reshape(4, dim)
    early = sum_tp(jnp.concatenate([vec2[:5], unxor(fb, tp_index)]))

    join = lambda lo: jnp.where(
        core == 0,
        jnp.concatenate([gmix[:, lo : lo + width], gmix_other[:, lo : lo + width]]),
        jnp.concatenate([gmix_other[:, lo : lo + width], gmix[:, lo : lo + width]]),
    )
    gmix_a, gmix_b = join(0), join(width)
    rows_of = lambda v, s: lax.dynamic_slice_in_dim(v, s * rows, rows)

    dy0, gy0, sy0 = attend_back_call(0, qkv_b, mix_b, lse_b, gmix_b, live_chip, normed)
    gmix_b, gy0, over_xy, over_yx, early = after(gmix_b, gy0, over_xy, over_yx, early)
    ff_k = total(ff_sum, jnp.concatenate([over_xy, over_yx]))
    ff_share = scatter_rest(ff_k, size, index)
    rgy0 = core_swap(rows_of(gy0, 1 - core))
    early = early + x_swap(early)

    dy1, gy1, sy1 = attend_back_call(1, qkv_b, mix_b, lse_b, gmix_b, live_chip, normed)
    gmix_a, gy1, dy1, rd_out, rgy0, early = after(gmix_a, gy1, dy1, rd_out, rgy0, early)
    rgy1 = core_swap(rows_of(gy1, 1 - core))
    d_out_half = total(d_out[: 2 * width], rd_out)
    from_y = y_swap(jnp.concatenate([dy0, d_out_half[width:], dy1], axis=0))
    early = sum_rest(early, size)

    do0, go0, so0 = attend_back_call(0, qkv_a, mix_a, lse_a, gmix_a, live_chip, normed)
    gmix_a, do0, go0, from_y, rgy1, ff_share = after(gmix_a, do0, go0, from_y, rgy1, ff_share)
    ff_mine = gather_rest(ff_share, size)
    first = 3 * 128
    rgo0 = core_swap(rows_of(go0, 1 - core))
    qkv_yd = core_swap(qkv_y)
    pair_own = total(jnp.concatenate([do0, d_out_half[:width]]), from_y[: first + width])
    pair_keep = scatter_side(pair_own, side, size)

    do1, go1, so1 = attend_back_call(1, qkv_a, mix_a, lse_a, gmix_a, live_chip, normed)
    go1, do1, pair_keep, rgo0, qkv_yd, early = after(go1, do1, pair_keep, rgo0, qkv_yd, early)
    fb_grad = lax.dynamic_index_in_dim(early, 5 + tp_index, keepdims=False)
    rgo1 = core_swap(rows_of(go1, 1 - core))
    last_keep = scatter_side(total(do1, from_y[first + width :]), side, size)
    rgo1, last_keep = after(rgo1, last_keep)
    qo_share = scatter_rest(jnp.concatenate([pair_keep, last_keep]), size, index)
    keep = lambda v: rows_of(v, core)
    input_grad, vec1 = last_call(
        ((qkv_y, (keep(gy0), keep(gy1))), (qkv_yd, (rgy0, rgy1)), (qkv_own, (keep(go0), keep(go1))),
         (qkv_core, (rgo0, rgo1))),
        tokens, carry, vecs,
    )
    vec1, ff_mine = after(vec1, ff_mine)
    ff_other = x_swap(ff_mine)
    qo_mine = gather_rest(qo_share, size)
    qo_both = unxor(jnp.stack([qo_mine, x_swap(qo_mine)]), side)
    qo_both = jax.vmap(lambda v: natural_rest(v, size, index))(qo_both)
    cut = (first + width) // 2
    pair_grad = qo_both[:, :cut].reshape(-1, dim)
    last_grad = qo_both[:, cut:].reshape(-1, dim)

    qv = lambda a, b: jnp.concatenate([a[0], b[0], a[2], b[2]])
    zero = jnp.zeros((2 * width,), F32)
    late = unxor(jnp.stack([qv(so0, so1), zero, qv(sy0, sy1), zero]), tp_index)
    late = sum_tp(jnp.concatenate([vec1[:2], late.reshape(2, dim)]))
    late = sum_rest(late + x_swap(late), size)
    qv_grad = lax.dynamic_index_in_dim(late[2:].reshape(4, 2, width), tp_index, keepdims=False)

    ff_both = unxor(jnp.stack([natural_rest(ff_mine, size, index), natural_rest(ff_other, size, index)]), side)
    ff_both = ff_both.astype(F32)
    fc1_grad = jnp.concatenate([ff_both[0, :, :half], ff_both[1, :, :half]], axis=1)
    second = lambda v: jnp.concatenate([v[:half, half:], v[half:, half:]], axis=1)
    fc2_grad = jnp.concatenate([second(ff_both[0]), second(ff_both[1])], axis=0)
    pair_part = pair_grad[:first].reshape(3, 128, dim)
    last_part = last_grad.reshape(3, width - 128, dim)
    qkv_grad = jnp.concatenate([pair_part, last_part], axis=1).astype(F32)
    return (
        block_out,
        input_grad,
        late[0],
        late[1],
        jnp.transpose(qkv_grad, (2, 0, 1)),
        qv_grad[0],
        qv_grad[1],
        pair_grad[first:].astype(F32),
        early[2],
        early[4],
        early[0],
        early[1],
        fc1_grad,
        fb_grad,
        fc2_grad,
        early[3],
    )


def solution(mesh):
    return jax.shard_map(
        functools.partial(body, mesh.shape["dp"]),
        mesh=mesh,
        in_specs=(
            P(("dp", "tp"), None), P(("dp", "tp"), None), P("dp", None), P("dp"), P(), P(), P(None, None, "tp"),
            P("tp"), P("tp"), P("tp", None), P(), P(), P(), P(), P(None, "tp"), P("tp"), P("tp", None), P(),
        ),
        out_specs=(
            P(("dp", "tp"), None), P(("dp", "tp"), None), P(), P(), P(None, None, "tp"), P("tp"), P("tp"),
            P("tp", None), P(), P(), P(), P(), P(None, "tp"), P("tp"), P("tp", None), P(),
        ),
        check_vma=False,
    )
```

```python
import functools

import jax
import jax.numpy as jnp
from jax import lax
from jax.experimental import pallas as pl
from jax.experimental.pallas import tpu as pltpu
from jax.sharding import PartitionSpec as P

HEAD = 64
PATCHES = 577
SEQ = 592
EPS = 1e-06
F32 = jnp.float32
BF16 = jnp.bfloat16
VMEM_BYTES = 60 * 1024 * 1024
CORE_SWAP = [(0, 1), (1, 0), (2, 3), (3, 2)]
Y_SWAP = [(0, 2), (1, 3), (2, 0), (3, 1)]

NN = (((1,), (0,)), ((), ()))
NT = (((1,), (1,)), ((), ()))
TN = (((0,), (0,)), ((), ()))


def mm(left, right, dims):
    return lax.dot_general(left, right, dims, preferred_element_type=F32)


def params():
    return pltpu.CompilerParams(vmem_limit_bytes=VMEM_BYTES)


def cost(micros):
    return pl.CostEstimate(flops=int(micros * 0.11e9), bytes_accessed=int(micros * 1e5), transcendentals=0)


def whole(shape):
    rank = len(shape)
    return pl.BlockSpec(shape, lambda *ids: (0,) * rank)


def norm_parts(values):
    centre = values - jnp.mean(values, axis=-1, keepdims=True)
    inv = lax.rsqrt(jnp.mean(centre * centre, axis=-1, keepdims=True) + EPS)
    return centre * inv, inv


def split_three(column):
    high = column.astype(BF16).astype(F32)
    rest = column - high
    middle = rest.astype(BF16).astype(F32)
    return high, middle, (rest - middle).astype(BF16).astype(F32)


def pick(lane, base, columns, other):
    out = other
    for place, column in enumerate(columns):
        out = jnp.where(lane == base + place, column, out)
    return out


def attend_kernel(first, *refs):
    if first:
        x_ref, vec_ref, w_ref, qb_ref, vb_ref, live_ref, normed_ref, qkv_ref, mix_ref, lse_ref = refs
        scaled, _ = norm_parts(x_ref[...].astype(F32))
        normed = (scaled * vec_ref[0:1, :] + vec_ref[1:2, :]).astype(BF16)
        normed_ref[...] = normed
    else:
        x_ref, w_ref, qb_ref, vb_ref, live_ref, qkv_ref, mix_ref, lse_ref = refs
        normed = x_ref[...]
    width = w_ref.shape[0] // 3
    rows = normed.shape[0]
    queries = (mm(normed, w_ref[:width, :], NT) + qb_ref[...]).astype(BF16)
    qkv_ref[:, :width] = (queries.astype(F32) * HEAD**-0.5).astype(BF16)
    qkv_ref[:, 256 : 256 + width] = mm(normed, w_ref[width : 2 * width, :], NT).astype(BF16)
    qkv_ref[:, 512 : 512 + width] = (mm(normed, w_ref[2 * width :, :], NT) + vb_ref[...]).astype(BF16)
    for i in range(3):
        qkv_ref[:, i * 256 + width : i * 256 + 256] = jnp.zeros((rows, 256 - width), BF16)
    lane = lax.broadcasted_iota(jnp.int32, (rows, 128), 1)
    key_bias = jnp.where(live_ref[...] > 0, 0.0, -1e30)
    lse_all = jnp.zeros((rows, 128), F32)
    for pair in range(2):
        base = pair * 128
        q_pair = qkv_ref[:, base : base + 128].astype(F32)
        k_pair = qkv_ref[:, 256 + base : 384 + base].astype(F32)
        v_pair = qkv_ref[:, 512 + base : 640 + base].astype(F32)
        mixed = jnp.zeros((rows, 128), F32)
        for side in range(2 if pair == 0 else 1):
            inside = (lane >= side * 64) & (lane < side * 64 + 64)
            extra = 64 - side * 64
            q_ext = jnp.where(inside, q_pair, jnp.where(lane == extra, 1.0, 0.0)).astype(BF16)
            k_ext = jnp.where(inside, k_pair, jnp.where(lane == extra, key_bias, 0.0)).astype(BF16)
            v_own = jnp.where(inside, v_pair, 0.0).astype(BF16)
            scores = mm(q_ext, k_ext, NT)
            top = jnp.max(scores, axis=-1, keepdims=True)
            weights = jnp.exp(scores - top)
            total = jnp.sum(weights, axis=-1, keepdims=True)
            mixed = mixed + mm(weights.astype(BF16), v_own, NN) * (1.0 / total)
            lse_all = jnp.where(lane == pair * 2 + side, top + jnp.log(total), lse_all)
        mix_ref[:, base : base + 128] = mixed.astype(BF16)
    lse_ref[...] = lse_all


def attend_call(first, x, extras, weight, q_bias, v_bias, live_col):
    rows = x.shape[0]
    dim = x.shape[1]
    width = weight.shape[0] // 3
    block = lambda lanes: pl.BlockSpec((SEQ, lanes), lambda i: (i, 0))
    shapes = [((rows, 768), BF16), ((rows, 256), BF16), ((rows, 128), F32)]
    if first:
        shapes = [((rows, dim), BF16)] + shapes
    return pl.pallas_call(
        functools.partial(attend_kernel, first),
        grid=(rows // SEQ,),
        in_specs=[block(dim)]
        + [whole(e.shape) for e in extras]
        + [whole(weight.shape), whole((1, width)), whole((1, width)), block(1)],
        out_specs=[block(s[1]) for s, _ in shapes],
        out_shape=[jax.ShapeDtypeStruct(s, d) for s, d in shapes],
        compiler_params=params(),
        cost_estimate=cost(13),
        name="attend",
    )(x, *extras, weight, q_bias, v_bias, live_col)


BLOCK = 224


def row_block(lanes):
    return pl.BlockSpec((BLOCK, lanes), lambda i: (i, 0))


def real_rows(rows):
    place = pl.program_id(0) * BLOCK + lax.broadcasted_iota(jnp.int32, (BLOCK, 1), 0)
    return place < rows


def hidden_kernel(rows, mix_ref, x_ref, cot_ref, live_ref, w_ref, vec_ref,
                  attn_ref, hidden_ref, normed_ref, gm_ref, sig_ref):
    x = x_ref[...].astype(F32)
    attention = mm(mix_ref[...], w_ref[...], NN) + vec_ref[2:3, :]
    sig = jax.nn.sigmoid(jnp.sum(x * vec_ref[3:4, :], axis=-1, keepdims=True))
    gate = live_ref[...] * sig
    hidden = x + gate * attention
    scaled, _ = norm_parts(hidden)
    real = real_rows(rows)
    attn_ref[...] = attention
    hidden_ref[...] = hidden
    normed_ref[...] = jnp.where(real, scaled * vec_ref[4:5, :] + vec_ref[5:6, :], 0.0).astype(BF16)
    gm_ref[...] = jnp.where(real, gate * cot_ref[...].astype(F32), 0.0).astype(BF16)
    sig_ref[...] = sig


def hidden_call(mix, x, cot, live_col, weight, vecs):
    rows, dim = x.shape
    steps = -(-rows // BLOCK)
    args = (mix, x, cot, live_col, weight, vecs)
    shapes = [((rows, dim), F32), ((rows, dim), F32), ((steps * BLOCK, dim), BF16), ((steps * BLOCK, dim), BF16),
              ((rows, 1), F32)]
    return pl.pallas_call(
        functools.partial(hidden_kernel, rows),
        in_specs=[row_block(a.shape[1]) for a in args[:4]] + [whole(a.shape) for a in args[4:]],
        out_specs=[row_block(s[1]) for s, _ in shapes],
        grid=(steps,),
        out_shape=[jax.ShapeDtypeStruct(s, d) for s, d in shapes],
        compiler_params=params(),
        cost_estimate=cost(7),
        name="hidden",
    )(*args)


def ff_kernel(n2_ref, gm_ref, a_ref, b_ref, bias_ref, mlp_ref, gn2_ref, da_ref, db_ref, dbias_ref,
              w1, w2, act_all, pre_all):
    half = w1.shape[0] // 2
    for i, piece in enumerate((a_ref, b_ref)):
        at = i * half
        w1[:, at : at + half] = piece[:, :half]
        w2[at : at + half, :half] = piece[:half, half:]
        w2[at : at + half, half:] = piece[half:, half:]
    steps = 2
    size = n2_ref.shape[0] // steps
    sums = 0.0
    for step in range(steps):
        at = slice(step * size, (step + 1) * size)
        pre = mm(n2_ref[at, :], w1[...], NN) + bias_ref[...]
        grad_act = mm(gm_ref[at, :], w2[...], NT)
        cdf = 0.5 * (1.0 + lax.erf(pre * (0.5**0.5)))
        slope = cdf + pre * (jnp.exp(-0.5 * pre * pre) * (0.5 / jnp.pi) ** 0.5)
        grad_pre = (grad_act * slope).astype(BF16)
        act_all[at, :] = (pre * cdf).astype(BF16)
        pre_all[at, :] = grad_pre
        sums = sums + jnp.sum(grad_pre.astype(F32), axis=0, keepdims=True)
        mlp_ref[at, :] = mm(act_all[at, :], w2[...], NN).astype(BF16)
        gn2_ref[at, :] = mm(pre_all[at, :], w1[...], NT).astype(BF16)
    dbias_ref[...] = sums
    d2 = mm(act_all[...], gm_ref[...], TN).astype(BF16)
    d1 = mm(n2_ref[...], pre_all[...], TN).astype(BF16)
    for i, grad in enumerate((da_ref, db_ref)):
        at = i * half
        grad[:, :half] = d1[:, at : at + half]
        grad[:half, half:] = d2[at : at + half, :half]
        grad[half:, half:] = d2[at : at + half, half:]


def ff_call(n2, gm, pieces, bias):
    rows, dim = n2.shape
    tall, square, line = whole((rows, dim)), whole((dim, dim)), whole((1, dim))
    out = pl.pallas_call(
        ff_kernel,
        grid=(1,),
        in_specs=[tall, tall, square, square, line],
        out_specs=[tall, tall, square, square, line],
        out_shape=[jax.ShapeDtypeStruct((rows, dim), BF16)] * 2
        + [jax.ShapeDtypeStruct((dim, dim), BF16)] * 2
        + [jax.ShapeDtypeStruct((1, dim), F32)],
        scratch_shapes=[pltpu.VMEM((dim, dim), BF16)] * 2 + [pltpu.VMEM((rows, dim), BF16)] * 2,
        compiler_params=params(),
        cost_estimate=cost(12),
        name="feed",
    )(n2, gm, *pieces, bias.reshape(1, dim))
    return out[:2], out[2:4], out[4].reshape(2, dim // 2)


def middle_kernel(rows, parts, *refs):
    mlp_refs, gn2_refs = refs[:parts], refs[parts : 2 * parts]
    (hidden_ref, attn_ref, x_ref, cot_ref, live_ref, sig_ref, gm_ref, mix_ref, w_ref, vec_ref,
     block_ref, carry_ref, near_ref, far_ref, dw_near_ref, dw_far_ref, sum_ref, acc_ref) = refs[2 * parts :]
    step = pl.program_id(0)
    real = real_rows(rows)
    x = x_ref[...].astype(F32)
    cot = cot_ref[...].astype(F32)
    sig = sig_ref[...]
    gate = live_ref[...] * sig
    hidden = hidden_ref[...]
    mlp = vec_ref[6:7, :]
    gn2 = 0.0
    for ref in mlp_refs:
        mlp = mlp + ref[...].astype(F32)
    for ref in gn2_refs:
        gn2 = gn2 + ref[...].astype(F32)
    block_ref[...] = (hidden + gate * mlp).astype(BF16)
    scaled, inv = norm_parts(hidden)
    e = gn2 * vec_ref[4:5, :]
    grad_hidden = cot + inv * (
        e - jnp.mean(e, axis=-1, keepdims=True) - scaled * jnp.mean(e * scaled, axis=-1, keepdims=True)
    )
    gate_grad = jnp.sum(grad_hidden * attn_ref[...] + cot * mlp, axis=-1, keepdims=True)
    logit = live_ref[...] * gate_grad * sig * (1.0 - sig)
    carry_ref[...] = grad_hidden + logit * vec_ref[3:4, :]
    grad_attn = jnp.where(real, gate * grad_hidden, 0.0).astype(BF16)
    half = near_ref.shape[1]
    near_ref[...] = mm(grad_attn, w_ref[:half, :], NT).astype(BF16)
    far_ref[...] = mm(grad_attn, w_ref[half:, :], NT).astype(BF16)
    mix = jnp.where(real, mix_ref[...].astype(F32), 0.0).astype(BF16)
    update = mm(mix, grad_attn, TN)
    add = lambda v: jnp.sum(jnp.where(real, v, 0.0), axis=0, keepdims=True)
    sums = jnp.concatenate(
        [add(gn2 * scaled), add(gn2), add(grad_attn.astype(F32)), add(gm_ref[...].astype(F32)), add(x * logit),
         jnp.zeros((3, x.shape[1]), F32)], axis=0)

    @pl.when(step == 0)
    def _():
        acc_ref[...] = update
        sum_ref[...] = sums

    @pl.when(step > 0)
    def _():
        acc_ref[...] += update
        sum_ref[...] += sums

    @pl.when(step == pl.num_programs(0) - 1)
    def _():
        dw_near_ref[...] = acc_ref[:half, :].astype(BF16)
        dw_far_ref[...] = acc_ref[half:, :].astype(BF16)


def middle_call(mlp, gn2, *args):
    x, weight, vecs = args[2], args[8], args[9]
    rows, dim = x.shape
    half = dim // 2
    shapes = [((rows, dim), BF16), ((rows, dim), F32), ((rows, half), BF16), ((rows, half), BF16)]
    ins = (*mlp, *gn2, *args)
    return pl.pallas_call(
        functools.partial(middle_kernel, rows, len(mlp)),
        in_specs=[row_block(a.shape[1]) for a in ins[:-2]] + [whole(weight.shape), whole(vecs.shape)],
        out_specs=[row_block(s[1]) for s, _ in shapes] + [whole((half, dim))] * 2 + [whole((8, dim))],
        grid=(-(-rows // BLOCK),),
        out_shape=[jax.ShapeDtypeStruct(s, d) for s, d in shapes]
        + [jax.ShapeDtypeStruct((half, dim), BF16)] * 2
        + [jax.ShapeDtypeStruct((8, dim), F32)],
        scratch_shapes=[pltpu.VMEM((dim, dim), F32)],
        compiler_params=params(),
        cost_estimate=cost(11),
        name="middle",
    )(*ins)


def attend_back_kernel(pair, *refs):
    qkv_ref, mix_ref, lse_ref, gmix_ref, live_ref, normed_ref, w_ref, dw_ref, gp_ref, bias_ref, vec_ref, gp_all = refs
    rows = qkv_ref.shape[0]
    width = gp_ref.shape[1] // 3
    base = pair * 128
    step = pl.program_id(0)
    lane = lax.broadcasted_iota(jnp.int32, (rows, 128), 1)
    key_bias = jnp.where(live_ref[...] > 0, 0.0, -1e30)
    lse_all = lse_ref[...]
    q_pair = qkv_ref[:, base : base + 128].astype(F32)
    k_pair = qkv_ref[:, 256 + base : 384 + base].astype(F32)
    v_pair = qkv_ref[:, 512 + base : 640 + base].astype(F32)
    m_pair = mix_ref[:, base : base + 128].astype(F32)
    g_pair = gmix_ref[:, base : base + width].astype(F32)
    if width < 128:
        g_pair = jnp.concatenate([g_pair, jnp.zeros((rows, 128 - width), F32)], axis=1)
    gq = jnp.zeros((rows, 128), F32)
    gk = jnp.zeros((rows, 128), F32)
    gv = jnp.zeros((rows, 128), F32)
    one = jnp.ones((rows, 1), F32)
    for side in range(width // 64):
        inside = (lane >= side * 64) & (lane < side * 64 + 64)
        extra = 64 - side * 64
        lse = jnp.sum(jnp.where(lane == pair * 2 + side, lse_all, 0.0), axis=-1, keepdims=True)
        delta = jnp.sum(jnp.where(inside, g_pair * m_pair, 0.0), axis=-1, keepdims=True)
        l0, l1, l2 = split_three(lse)
        d0, d1, d2 = split_three(delta)
        q_ext = jnp.where(inside, q_pair, pick(lane, extra, (-l0, -l1, -l2, one), 0.0)).astype(BF16)
        k_ext = jnp.where(inside, k_pair, pick(lane, extra, (one, one, one, key_bias), 0.0)).astype(BF16)
        g_ext = jnp.where(inside, g_pair, pick(lane, extra, (-d0, -d1, -d2), 0.0)).astype(BF16)
        v_ext = jnp.where(inside, v_pair, pick(lane, extra, (one, one, one), 0.0)).astype(BF16)
        q_own = jnp.where(inside, q_pair, 0.0).astype(BF16)
        k_own = jnp.where(inside, k_pair, 0.0).astype(BF16)
        g_own = jnp.where(inside, g_pair, 0.0).astype(BF16)
        probs = jnp.exp(mm(k_ext, q_ext, NT))
        grad_scores = (probs * mm(v_ext, g_ext, NT)).astype(BF16)
        gv = gv + mm(probs.astype(BF16), g_own, NN)
        gk = gk + mm(grad_scores, q_own, NN)
        gq = gq + mm(grad_scores, k_own, TN)
    sums = []
    for part, grad in enumerate((gq * HEAD**-0.5, gk, gv)):
        piece = grad.astype(BF16)[:, :width]
        gp_ref[:, part * width : (part + 1) * width] = piece
        sums.append(jnp.sum(piece.astype(F32), axis=0, keepdims=True))
    gp_all[pl.ds(pl.multiple_of(step * rows, 16), rows), :] = gp_ref[...]
    sums = jnp.concatenate(sums, axis=0)

    @pl.when(step == 0)
    def _():
        bias_ref[...] = sums

    @pl.when(step > 0)
    def _():
        bias_ref[...] += sums

    @pl.when(step == pl.num_programs(0) - 1)
    def _():
        update = mm(gp_all[...], normed_ref[...], TN)
        dw_ref[...] = update.astype(BF16)
        third = w_ref.shape[0] // 3
        column = jnp.zeros((1, w_ref.shape[1]), F32)
        product = jnp.zeros((1, w_ref.shape[1]), F32)
        for part in range(3):
            terms = jnp.concatenate(split_three(bias_ref[part : part + 1, :]), axis=0).astype(BF16)
            rows_w = w_ref[part * third + base : part * third + base + width, :]
            column = column + jnp.sum(mm(terms, rows_w, NN), axis=0, keepdims=True)
            own = update[part * width : (part + 1) * width, :] * rows_w.astype(F32)
            product = product + jnp.sum(own, axis=0, keepdims=True)
        vec_ref[0:1, :] = product
        vec_ref[1:2, :] = column


def attend_back_call(pair, qkv, mix, lse, gmix, live_col, normed, weight):
    rows, dim = normed.shape
    width = 128 if pair == 0 else gmix.shape[1] - 128
    block = lambda lanes: pl.BlockSpec((SEQ, lanes), lambda i: (i, 0))
    ins = [qkv, mix, lse, gmix, live_col, normed, weight]
    return pl.pallas_call(
        functools.partial(attend_back_kernel, pair),
        grid=(rows // SEQ,),
        in_specs=[block(a.shape[1]) for a in ins[:5]] + [whole(normed.shape), whole(weight.shape)],
        out_specs=[whole((3 * width, dim)), block(3 * width), whole((3, width)), whole((2, dim))],
        out_shape=[
            jax.ShapeDtypeStruct((3 * width, dim), BF16),
            jax.ShapeDtypeStruct((rows, 3 * width), BF16),
            jax.ShapeDtypeStruct((3, width), F32),
            jax.ShapeDtypeStruct((2, dim), F32),
        ],
        scratch_shapes=[pltpu.VMEM((rows, 3 * width), BF16)],
        compiler_params=params(),
        cost_estimate=cost(14 if pair == 0 else 8),
        name="attend_back",
    )(*ins)


def last_kernel(splits, *refs):
    count = sum(len(s) for s in splits)
    groups = len(splits)
    gp_refs, w_refs = refs[:count], refs[count : count + groups]
    x_ref, carry_ref, vec_ref, grad_ref = refs[count + groups : count + groups + 4]
    scratch = refs[count + groups + 4 :]

    @pl.when(pl.program_id(0) == 0)
    def _():
        for w_ref, to_ref, widths in zip(w_refs, scratch, splits):
            third = w_ref.shape[0] // 3
            start = 0
            base = 0
            for width in widths:
                size = width // 3
                for part in range(3):
                    to_ref[start : start + size, :] = w_ref[part * third + base : part * third + base + size, :]
                    start += size
                base += size

    gn = 0.0
    at = 0
    for to_ref, widths in zip(scratch, splits):
        start = 0
        for width in widths:
            gn = gn + mm(gp_refs[at][...], to_ref[start : start + width, :], NN)
            start += width
            at += 1
    scaled, inv = norm_parts(x_ref[...].astype(F32))
    f = gn * vec_ref[0:1, :]
    grad_ref[...] = carry_ref[...] + inv * (
        f - jnp.mean(f, axis=-1, keepdims=True) - scaled * jnp.mean(f * scaled, axis=-1, keepdims=True)
    )


def last_call(groups, x, carry, vecs):
    rows, dim = x.shape
    gps = [g for _, parts in groups for g in parts]
    weights = [w for w, _ in groups]
    splits = tuple(tuple(g.shape[1] for g in parts) for _, parts in groups)
    return pl.pallas_call(
        functools.partial(last_kernel, splits),
        in_specs=[row_block(g.shape[1]) for g in gps]
        + [whole(w.shape) for w in weights]
        + [row_block(dim), row_block(dim), whole(vecs.shape)],
        out_specs=row_block(dim),
        grid=(-(-rows // BLOCK),),
        out_shape=jax.ShapeDtypeStruct((rows, dim), F32),
        scratch_shapes=[pltpu.VMEM(w.shape, BF16) for w in weights],
        compiler_params=params(),
        cost_estimate=cost(9),
        name="last",
    )(*gps, *weights, x, carry, vecs)


def total(*terms):
    out = terms[0].astype(F32)
    for term in terms[1:]:
        out = out + term.astype(F32)
    return out.astype(BF16)


def after(first, *rest):
    return lax.optimization_barrier((first, *rest))


def unxor(value, index):
    count = value.shape[0]
    bit = 1
    while bit < count:
        split = value.reshape(count // (2 * bit), 2, bit, *value.shape[1:])
        value = jnp.where((index // bit) % 2 == 1, jnp.flip(split, 1), split).reshape(value.shape)
        bit *= 2
    return value


def stages(size):
    out = []
    stride = 2
    while stride < size:
        radix = 4 if size % (stride * 4) == 0 else 2
        out.append((stride, radix))
        stride *= radix
    return out


def dp_swap(value, size, offset):
    return lax.ppermute(value, "dp", [(i, i ^ offset) for i in range(size)])


def split_two(value):
    high = value.astype(BF16)
    return jnp.concatenate([high, (value - high.astype(F32)).astype(BF16)])


def join_two(value):
    high, low = jnp.split(value.astype(F32), 2)
    return high + low


def scatter_rest(value, vec, size, index):
    for stride, radix in stages(size):
        digit = (index // stride) % radix
        share = value.shape[0] // radix
        cut = lambda o: lax.dynamic_slice_in_dim(value, (digit ^ o) * share, share)
        send = cut if vec is None else lambda o: jnp.concatenate([cut(o), split_two(vec)])
        got = [dp_swap(send(o), size, o * stride) for o in range(1, radix)]
        value = total(cut(0), *[g[:share] for g in got])
        if vec is not None:
            vec = vec + sum(join_two(g[share:]) for g in got)
    return value, vec


def gather_rest(value, size):
    parts = [value]
    for stride, radix in reversed(stages(size)):
        value = jnp.concatenate(parts)
        parts = [value] + [dp_swap(value, size, o * stride) for o in range(1, radix)]
    return parts


def natural_rest(value, size, index):
    order = 0
    for stride, radix in stages(size):
        order = order * radix + (index // stride) % radix
    blocks = value.reshape(size // 2, -1, value.shape[-1])
    return unxor(blocks, order).reshape(value.shape)


def scatter_side(value, side, size):
    half = value.shape[0] // 2
    send = lax.dynamic_slice_in_dim(value, (1 - side) * half, half)
    keep = lax.dynamic_slice_in_dim(value, side * half, half)
    return total(keep, dp_swap(send, size, 1))


def sum_tp(value):
    return value + sum(lax.ppermute(value, "tp", [(i, i ^ o) for i in range(4)]) for o in range(1, 4))


def body(
    size,
    tokens, cotangent, patch_rank, kept_counts, norm1_gain, norm1_shift, qkv_weight, query_bias, value_bias,
    out_weight, out_bias, router_weight, norm2_gain, norm2_shift, fc1_weight, fc1_bias, fc2_weight, fc2_bias,
):
    rows, dim = tokens.shape
    half = dim // 2
    images = patch_rank.shape[0]
    tp_index = lax.axis_index("tp")
    index = lax.axis_index("dp")
    core = tp_index % 2
    chip = tp_index // 2
    side = index % 2
    core_swap = lambda v: lax.ppermute(v, "tp", CORE_SWAP)
    y_swap = lambda v: lax.ppermute(v, "tp", Y_SWAP)
    x_swap = lambda v: dp_swap(v, size, 1)
    row_vec = lambda v: v.astype(F32).reshape(1, -1)

    width = out_weight.shape[0]
    qkv_own = jnp.transpose(qkv_weight, (1, 2, 0)).reshape(-1, dim)
    tokens_other = core_swap(tokens)
    qkv_y = y_swap(qkv_own)
    small_own = jnp.concatenate([query_bias, value_bias, fc1_bias]).astype(F32)
    small_y = y_swap(small_own)
    vecs = jnp.stack(
        [norm1_gain, norm1_shift, out_bias, router_weight, norm2_gain, norm2_shift, fc2_bias, fc2_bias]
    ).astype(F32)

    padded = jnp.concatenate([patch_rank, jnp.full((images, SEQ - PATCHES), PATCHES, jnp.int32)], axis=1)
    live_image = (padded < kept_counts[:, None]).astype(F32)
    live_chip = lax.dynamic_slice_in_dim(live_image, chip * (images // 2), images // 2).reshape(-1, 1)
    live_own = lax.dynamic_slice_in_dim(live_chip, core * rows, rows)

    def pack(s):
        w1 = lax.dynamic_slice_in_dim(fc1_weight, s * half, half, axis=1)
        w2 = lax.dynamic_slice_in_dim(fc2_weight, s * half, half)
        return jnp.concatenate([w1, jnp.concatenate([w2[:, :half], w2[:, half:]])], axis=1)

    own_k, own_s = pack(side), pack(1 - side)
    tokens_chip = jnp.where(
        core == 0, jnp.concatenate([tokens, tokens_other]), jnp.concatenate([tokens_other, tokens])
    )
    normed, qkv_a, mix_a, lse_a = attend_call(
        True, tokens_chip, (vecs,), qkv_own,
        row_vec(query_bias), row_vec(value_bias), live_chip,
    )
    normed, qkv_y, small_y, own_k, own_s, out_weight = after(normed, qkv_y, small_y, own_k, own_s, out_weight)
    out_y = y_swap(out_weight)
    y_k = y_swap(own_k)
    core_k, core_s, out_core, qkv_core = [core_swap(v) for v in (own_k, own_s, out_weight, qkv_own)]
    small_far = core_swap(jnp.stack([small_own, small_y]))

    qkv_b, mix_b, lse_b = attend_call(
        False, normed, (), qkv_y, row_vec(small_y[:width]), row_vec(small_y[width : 2 * width]), live_chip
    )
    mix_b, out_y = after(mix_b, out_y)
    out_yd = core_swap(out_y)
    part = lambda v, s: lax.dynamic_slice(v, (s * rows, 0), (rows, width))
    send_mix = jnp.concatenate([part(mix_a, 1 - core), part(mix_b, 1 - core)], axis=1)
    mix_rows = jnp.concatenate([part(mix_a, core), part(mix_b, core), core_swap(send_mix)], axis=1)
    out_all = jnp.concatenate([out_weight, out_y, out_core, out_yd], axis=0)

    attn, hidden, n2, gm, sig = hidden_call(mix_rows, tokens, cotangent, live_own, out_all, vecs)
    n2, y_k = after(n2, y_k)
    y_s = x_swap(y_k)
    yd_k = core_swap(y_k)
    halves = lambda v: unxor(v[2 * width :].reshape(2, half), side)
    b_own, b_y, b_core, b_yd = halves(small_own), halves(small_y), halves(small_far[0]), halves(small_far[1])

    sums1, (dy_k, dyd_k), fb1 = ff_call(n2, gm, (y_k, yd_k), jnp.stack([b_y[0], b_yd[0]]))
    n2, dyd_k, dy_k = after(n2, dyd_k, dy_k)
    ryd_k = core_swap(dyd_k)
    sums2, (do_s, dc_s), fb2 = ff_call(n2, gm, (own_s, core_s), jnp.stack([b_own[1], b_core[1]]))
    n2, do_s, dc_s, ryd_k, y_s = after(n2, do_s, dc_s, ryd_k, y_s)
    rc_s = core_swap(dc_s)
    yd_s = core_swap(y_s)
    y_k_sum = total(dy_k, ryd_k)
    own_s_sum = total(do_s, rc_s)
    n2, y_k_sum, own_s_sum, yd_s = after(n2, y_k_sum, own_s_sum, yd_s)
    from_y_k = [y_swap(y_k_sum[:half])]
    from_x = [x_swap(own_s_sum[:half])]
    sums3, (dy_s, dyd_s), fb3 = ff_call(n2, gm, (y_s, yd_s), jnp.stack([b_y[1], b_yd[1]]))
    n2, dy_s, dyd_s, from_y_k[0], from_x[0] = after(n2, dy_s, dyd_s, from_y_k[0], from_x[0])
    y_k_sum, own_s_sum, n2 = after(y_k_sum, own_s_sum, n2)
    from_y_k.append(y_swap(y_k_sum[half:]))
    from_x.append(x_swap(own_s_sum[half:]))
    ryd_s = core_swap(dyd_s)
    sums4, (do_k, dc_k), fb4 = ff_call(n2, gm, (own_k, core_k), jnp.stack([b_own[0], b_core[0]]))
    sums4, do_k, dc_k, ryd_s, from_x[1], from_y_k[1] = after(sums4, do_k, dc_k, ryd_s, from_x[1], from_y_k[1])
    from_x, from_y_k = jnp.concatenate(from_x), jnp.concatenate(from_y_k)
    y_s_sum = total(dy_s, ryd_s)
    sums4, y_s_sum = after(sums4, y_s_sum)
    over_x = x_swap(y_s_sum[:half])
    over_y = y_swap(y_s_sum[half:])
    rc_k = core_swap(dc_k)

    four = (sums1, sums2, sums3, sums4)
    block_out, carry, gmix, gmix_far, d_out, d_out_far, vec2 = middle_call(
        [f[0] for f in four], [f[1] for f in four], hidden, attn, tokens, cotangent, live_own, sig, gm, mix_rows,
        out_all, vecs,
    )
    gmix, gmix_far, d_out_far, rc_k, vec2, over_x, over_y = after(
        gmix, gmix_far, d_out_far, rc_k, vec2, over_x, over_y
    )
    gmix_other = core_swap(gmix_far)
    rd_out = core_swap(d_out_far)

    join = lambda lo: jnp.where(
        core == 0,
        jnp.concatenate([gmix[:, lo : lo + width], gmix_other[:, lo : lo + width]]),
        jnp.concatenate([gmix_other[:, lo : lo + width], gmix[:, lo : lo + width]]),
    )
    gmix_a, gmix_b = join(0), join(width)
    rows_of = lambda v, s: lax.dynamic_slice_in_dim(v, s * rows, rows)

    over_xy = y_swap(over_x)
    over_yx = x_swap(over_y)
    dy0, gy0, sy0, vy0 = attend_back_call(0, qkv_b, mix_b, lse_b, gmix_b, live_chip, normed, qkv_y)
    gmix_a, dy0, gy0, over_xy, over_yx, rd_out = after(gmix_a, dy0, gy0, over_xy, over_yx, rd_out)
    ff_k = total(do_k, rc_k, from_y_k, from_x, jnp.concatenate([over_xy, over_yx]))
    gmix_a, ff_k = after(gmix_a, ff_k)
    ff_share = scatter_rest(ff_k, None, size, index)[0]
    d_out_half = total(d_out, rd_out)
    from_y0 = y_swap(jnp.concatenate([dy0, d_out_half[width:]]))
    rgy0 = core_swap(rows_of(gy0, 1 - core))

    do0, go0, so0, vo0 = attend_back_call(0, qkv_a, mix_a, lse_a, gmix_a, live_chip, normed, qkv_own)
    gmix_b, do0, go0, rgy0, ff_share, from_y0 = after(gmix_b, do0, go0, rgy0, ff_share, from_y0)
    ff_parts = gather_rest(ff_share, size)
    first = 3 * 128
    rgo0 = core_swap(rows_of(go0, 1 - core))
    qkv_yd = core_swap(qkv_y)

    dy1, gy1, sy1, vy1 = attend_back_call(1, qkv_b, mix_b, lse_b, gmix_b, live_chip, normed, qkv_y)
    gmix_a, dy1, gy1, rgo0, qkv_yd, *ready = after(gmix_a, dy1, gy1, rgo0, qkv_yd, *ff_parts[:-1])
    ff_parts = [*ready, ff_parts[-1]]
    pair_own = total(jnp.concatenate([do0, d_out_half[:width]]), from_y0)
    pair_keep = scatter_side(pair_own, side, size)
    from_y1 = y_swap(dy1)
    rgy1 = core_swap(rows_of(gy1, 1 - core))

    do1, go1, so1, vo1 = attend_back_call(1, qkv_a, mix_a, lse_a, gmix_a, live_chip, normed, qkv_own)
    go1, do1, so1, vo1, pair_keep, rgy1, from_y1, ff_parts[-1] = after(
        go1, do1, so1, vo1, pair_keep, rgy1, from_y1, ff_parts[-1]
    )
    ff_mine = jnp.concatenate(ff_parts)
    rgo1 = core_swap(rows_of(go1, 1 - core))
    last_keep = scatter_side(total(do1, from_y1), side, size)
    fb_k, fb_s = jnp.stack([fb4[0], fb4[1], fb1[0], fb1[1]]), jnp.stack([fb2[0], fb2[1], fb3[0], fb3[1]])
    fb = unxor(jnp.stack([fb_k, fb_s]), side).transpose(1, 0, 2).reshape(4, dim)
    qv = lambda a, b: jnp.concatenate([a[0], b[0], a[2], b[2]])
    zero = jnp.zeros((2 * width,), F32)
    qv_rows = unxor(jnp.stack([qv(so0, so1), zero, qv(sy0, sy1), zero]), tp_index).reshape(2, dim)
    lines = [vec2[:5], unxor(fb, tp_index), vy0 + vy1 + vo0 + vo1, qv_rows, jnp.zeros((3, dim), F32)]
    vec = sum_tp(jnp.concatenate(lines))
    rgo1, last_keep, vec, ff_mine = after(rgo1, last_keep, vec, ff_mine)
    qo_share, vec = scatter_rest(jnp.concatenate([pair_keep, last_keep]), vec, size, index)
    keep = lambda v: rows_of(v, core)
    ff_other = [x_swap(ff_mine[:half])]
    input_grad = last_call(
        ((qkv_y, (keep(gy0), keep(gy1))), (qkv_yd, (rgy0, rgy1)), (qkv_own, (keep(go0), keep(go1))),
         (qkv_core, (rgo0, rgo1))),
        tokens, carry, vecs,
    )
    input_grad, qo_share, vec, ff_other[0] = after(input_grad, qo_share, vec, ff_other[0])
    swapped = x_swap(jnp.concatenate([ff_mine[half:], split_two(vec)]))
    vec = vec + join_two(swapped[half:])
    ff_other = jnp.concatenate([ff_other[0], swapped[:half]])
    qo_mine = jnp.concatenate(gather_rest(qo_share, size))
    qo_both = unxor(jnp.stack([qo_mine, x_swap(qo_mine)]), side)
    qo_both = jax.vmap(lambda v: natural_rest(v, size, index))(qo_both)
    cut = (first + width) // 2
    pair_grad = qo_both[:, :cut].reshape(-1, dim)
    last_grad = qo_both[:, cut:].reshape(-1, dim)

    gain_one, shift_one = vecs[0], vecs[1]
    qv_grad = lax.dynamic_index_in_dim(vec[11:13].reshape(4, 2, width), tp_index, keepdims=False)
    fb_grad = lax.dynamic_index_in_dim(vec[:9], 5 + tp_index, keepdims=False)
    ff_both = unxor(jnp.stack([natural_rest(ff_mine, size, index), natural_rest(ff_other, size, index)]), side)
    ff_both = ff_both.astype(F32)
    fc1_grad = jnp.concatenate([ff_both[0, :, :half], ff_both[1, :, :half]], axis=1)
    second = lambda v: jnp.concatenate([v[:half, half:], v[half:, half:]], axis=1)
    fc2_grad = jnp.concatenate([second(ff_both[0]), second(ff_both[1])], axis=0)
    pair_part = pair_grad[:first].reshape(3, 128, dim)
    last_part = last_grad.reshape(3, width - 128, dim)
    qkv_grad = jnp.concatenate([pair_part, last_part], axis=1).astype(F32)
    return (
        block_out,
        input_grad,
        (vec[9] - shift_one * vec[10]) / gain_one,
        vec[10],
        jnp.transpose(qkv_grad, (2, 0, 1)),
        qv_grad[0],
        qv_grad[1],
        pair_grad[first:].astype(F32),
        vec[2],
        vec[4],
        vec[0],
        vec[1],
        fc1_grad,
        fb_grad,
        fc2_grad,
        vec[3],
    )


def solution(mesh):
    return jax.shard_map(
        functools.partial(body, mesh.shape["dp"]),
        mesh=mesh,
        in_specs=(
            P(("dp", "tp"), None), P(("dp", "tp"), None), P("dp", None), P("dp"), P(), P(), P(None, None, "tp"),
            P("tp"), P("tp"), P("tp", None), P(), P(), P(), P(), P(None, "tp"), P("tp"), P("tp", None), P(),
        ),
        out_specs=(
            P(("dp", "tp"), None), P(("dp", "tp"), None), P(), P(), P(None, None, "tp"), P("tp"), P("tp"),
            P("tp", None), P(), P(), P(), P(), P(None, "tp"), P("tp"), P("tp", None), P(),
        ),
        check_vma=False,
    )
```

```python
import functools

import jax
import jax.numpy as jnp
from jax import lax
from jax.experimental import pallas as pl
from jax.experimental.pallas import tpu as pltpu
from jax.sharding import PartitionSpec as P

HEAD = 64
PATCHES = 577
SEQ = 592
EPS = 1e-06
F32 = jnp.float32
BF16 = jnp.bfloat16
VMEM_BYTES = 60 * 1024 * 1024
CORE_SWAP = [(0, 1), (1, 0), (2, 3), (3, 2)]
Y_SWAP = [(0, 2), (1, 3), (2, 0), (3, 1)]

NN = (((1,), (0,)), ((), ()))
NT = (((1,), (1,)), ((), ()))
TN = (((0,), (0,)), ((), ()))


def mm(left, right, dims):
    return lax.dot_general(left, right, dims, preferred_element_type=F32)


def params():
    return pltpu.CompilerParams(vmem_limit_bytes=VMEM_BYTES)


def cost(micros):
    return pl.CostEstimate(flops=int(micros * 0.11e9), bytes_accessed=int(micros * 1e5), transcendentals=0)


def whole(shape):
    rank = len(shape)
    return pl.BlockSpec(shape, lambda *ids: (0,) * rank)


def norm_parts(values):
    centre = values - jnp.mean(values, axis=-1, keepdims=True)
    inv = lax.rsqrt(jnp.mean(centre * centre, axis=-1, keepdims=True) + EPS)
    return centre * inv, inv


def split_three(column):
    high = column.astype(BF16).astype(F32)
    rest = column - high
    middle = rest.astype(BF16).astype(F32)
    return high, middle, (rest - middle).astype(BF16).astype(F32)


def pick(lane, base, columns, other):
    out = other
    for place, column in enumerate(columns):
        out = jnp.where(lane == base + place, column, out)
    return out


def lines_kernel(*refs):
    *ins, out_ref = refs
    lines = []
    for ref in ins:
        line = ref[...].astype(F32).reshape(1, -1)
        if line.shape[1] < out_ref.shape[1]:
            line = jnp.concatenate([line, jnp.zeros((1, out_ref.shape[1] - line.shape[1]), F32)], axis=1)
        lines.append(line)
    fill = jnp.zeros((out_ref.shape[0] - len(lines), out_ref.shape[1]), F32)
    out_ref[...] = jnp.concatenate(lines + [fill], axis=0)


def lines_call(vectors, dim):
    rows = -(-len(vectors) // 8) * 8
    return pl.pallas_call(
        lines_kernel,
        out_shape=jax.ShapeDtypeStruct((rows, dim), F32),
        cost_estimate=cost(1),
        name="lines",
    )(*vectors)


def attend_kernel(first, *refs):
    step = pl.program_id(0)
    if first:
        own_ref, other_ref, core_ref, vec_ref, w_ref, qb_ref, vb_ref, live_ref = refs[:8]
        normed_ref, qkv_ref, mix_ref, lse_ref = refs[8:]
        here = pl.ds(pl.multiple_of(step * SEQ, 16), SEQ)

        @pl.when(step == 0)
        def _():
            own, other = own_ref[...].astype(F32), other_ref[...].astype(F32)
            swap = core_ref[...] > 0
            blocks = [jnp.where(swap, other, own), jnp.where(swap, own, other)]
            rows = own.shape[0]
            for image in range(2 * rows // SEQ):
                pieces = []
                start, left = image * SEQ, SEQ
                while left:
                    block, at = start // rows, start % rows
                    take = min(left, rows - at)
                    pieces.append(blocks[block][at : at + take, :])
                    start, left = start + take, left - take
                x = pieces[0] if len(pieces) == 1 else jnp.concatenate(pieces, axis=0)
                scaled, _ = norm_parts(x)
                value = (scaled * vec_ref[0:1, :] + vec_ref[1:2, :]).astype(BF16)
                normed_ref[image * SEQ : (image + 1) * SEQ, :] = value

        normed = normed_ref[here, :]
    else:
        x_ref, w_ref, qb_ref, vb_ref, live_ref, qkv_ref, mix_ref, lse_ref = refs
        normed = x_ref[...]
    width = w_ref.shape[0] // 3
    rows = normed.shape[0]
    queries = (mm(normed, w_ref[:width, :], NT) + qb_ref[...]).astype(BF16)
    qkv_ref[:, :width] = (queries.astype(F32) * HEAD**-0.5).astype(BF16)
    qkv_ref[:, 256 : 256 + width] = mm(normed, w_ref[width : 2 * width, :], NT).astype(BF16)
    qkv_ref[:, 512 : 512 + width] = (mm(normed, w_ref[2 * width :, :], NT) + vb_ref[...]).astype(BF16)
    for i in range(3):
        qkv_ref[:, i * 256 + width : i * 256 + 256] = jnp.zeros((rows, 256 - width), BF16)
    lane = lax.broadcasted_iota(jnp.int32, (rows, 128), 1)
    key_bias = jnp.where(live_ref[...] > 0, 0.0, -1e30)
    lse_all = jnp.zeros((rows, 128), F32)
    for pair in range(2):
        base = pair * 128
        q_pair = qkv_ref[:, base : base + 128].astype(F32)
        k_pair = qkv_ref[:, 256 + base : 384 + base].astype(F32)
        v_pair = qkv_ref[:, 512 + base : 640 + base].astype(F32)
        mixed = jnp.zeros((rows, 128), F32)
        for side in range(2 if pair == 0 else 1):
            inside = (lane >= side * 64) & (lane < side * 64 + 64)
            extra = 64 - side * 64
            q_ext = jnp.where(inside, q_pair, jnp.where(lane == extra, 1.0, 0.0)).astype(BF16)
            k_ext = jnp.where(inside, k_pair, jnp.where(lane == extra, key_bias, 0.0)).astype(BF16)
            v_own = jnp.where(inside, v_pair, 0.0).astype(BF16)
            scores = mm(q_ext, k_ext, NT)
            top = jnp.max(scores, axis=-1, keepdims=True)
            weights = jnp.exp(scores - top)
            total = jnp.sum(weights, axis=-1, keepdims=True)
            mixed = mixed + mm(weights.astype(BF16), v_own, NN) * (1.0 / total)
            lse_all = jnp.where(lane == pair * 2 + side, top + jnp.log(total), lse_all)
        mix_ref[:, base : base + 128] = mixed.astype(BF16)
    lse_ref[...] = lse_all


def attend_call(x, extras, weight, q_bias, v_bias, live_col):
    rows, dim = live_col.shape[0], x.shape[1]
    width = weight.shape[0] // 3
    block = lambda lanes: pl.BlockSpec((SEQ, lanes), lambda i: (i, 0))
    shapes = [((rows, 768), BF16), ((rows, 256), BF16), ((rows, 128), F32)]
    out_specs = [block(s[1]) for s, _ in shapes]
    if extras:
        shapes = [((rows, dim), BF16)] + shapes
        out_specs = [whole((rows, dim))] + out_specs
    return pl.pallas_call(
        functools.partial(attend_kernel, bool(extras)),
        grid=(rows // SEQ,),
        in_specs=[whole(x.shape) if extras else block(dim)]
        + [whole(e.shape) for e in extras]
        + [whole(weight.shape), whole((1, width)), whole((1, width)), block(1)],
        out_specs=out_specs,
        out_shape=[jax.ShapeDtypeStruct(s, d) for s, d in shapes],
        compiler_params=params(),
        cost_estimate=cost(13),
        name="attend",
    )(x, *extras, weight, q_bias, v_bias, live_col)


BLOCK = 224


def row_block(lanes):
    return pl.BlockSpec((BLOCK, lanes), lambda i: (i, 0))


def real_rows(rows):
    place = pl.program_id(0) * BLOCK + lax.broadcasted_iota(jnp.int32, (BLOCK, 1), 0)
    return place < rows


def hidden_kernel(rows, mix_ref, x_ref, cot_ref, live_ref, w_ref, vec_ref,
                  attn_ref, hidden_ref, normed_ref, gm_ref, sig_ref):
    x = x_ref[...].astype(F32)
    attention = mm(mix_ref[...], w_ref[...], NN) + vec_ref[2:3, :]
    sig = jax.nn.sigmoid(jnp.sum(x * vec_ref[3:4, :], axis=-1, keepdims=True))
    gate = live_ref[...] * sig
    hidden = x + gate * attention
    scaled, _ = norm_parts(hidden)
    real = real_rows(rows)
    attn_ref[...] = attention
    hidden_ref[...] = hidden
    normed_ref[...] = jnp.where(real, scaled * vec_ref[4:5, :] + vec_ref[5:6, :], 0.0).astype(BF16)
    gm_ref[...] = jnp.where(real, gate * cot_ref[...].astype(F32), 0.0).astype(BF16)
    sig_ref[...] = sig


def hidden_call(mix, x, cot, live_col, weight, vecs):
    rows, dim = x.shape
    steps = -(-rows // BLOCK)
    args = (mix, x, cot, live_col, weight, vecs)
    shapes = [((rows, dim), F32), ((rows, dim), F32), ((steps * BLOCK, dim), BF16), ((steps * BLOCK, dim), BF16),
              ((rows, 1), F32)]
    return pl.pallas_call(
        functools.partial(hidden_kernel, rows),
        in_specs=[row_block(a.shape[1]) for a in args[:4]] + [whole(a.shape) for a in args[4:]],
        out_specs=[row_block(s[1]) for s, _ in shapes],
        grid=(steps,),
        out_shape=[jax.ShapeDtypeStruct(s, d) for s, d in shapes],
        compiler_params=params(),
        cost_estimate=cost(7),
        name="hidden",
    )(*args)


def ff_kernel(n2_ref, gm_ref, a_ref, b_ref, bias_ref, mlp_ref, gn2_ref, da_ref, db_ref, dbias_ref,
              w1, w2, act_all, pre_all):
    half = w1.shape[0] // 2
    for i, piece in enumerate((a_ref, b_ref)):
        at = i * half
        w1[:, at : at + half] = piece[:, :half]
        w2[at : at + half, :half] = piece[:half, half:]
        w2[at : at + half, half:] = piece[half:, half:]
    steps = 2
    size = n2_ref.shape[0] // steps
    sums = 0.0
    for step in range(steps):
        at = slice(step * size, (step + 1) * size)
        pre = mm(n2_ref[at, :], w1[...], NN) + bias_ref[...]
        grad_act = mm(gm_ref[at, :], w2[...], NT)
        cdf = 0.5 * (1.0 + lax.erf(pre * (0.5**0.5)))
        slope = cdf + pre * (jnp.exp(-0.5 * pre * pre) * (0.5 / jnp.pi) ** 0.5)
        grad_pre = (grad_act * slope).astype(BF16)
        act_all[at, :] = (pre * cdf).astype(BF16)
        pre_all[at, :] = grad_pre
        sums = sums + jnp.sum(grad_pre.astype(F32), axis=0, keepdims=True)
        mlp_ref[at, :] = mm(act_all[at, :], w2[...], NN).astype(BF16)
        gn2_ref[at, :] = mm(pre_all[at, :], w1[...], NT).astype(BF16)
    dbias_ref[...] = sums
    d2 = mm(act_all[...], gm_ref[...], TN).astype(BF16)
    d1 = mm(n2_ref[...], pre_all[...], TN).astype(BF16)
    for i, grad in enumerate((da_ref, db_ref)):
        at = i * half
        grad[:, :half] = d1[:, at : at + half]
        grad[:half, half:] = d2[at : at + half, :half]
        grad[half:, half:] = d2[at : at + half, half:]


def ff_call(n2, gm, pieces, bias):
    rows, dim = n2.shape
    tall, square, line = whole((rows, dim)), whole((dim, dim)), whole((1, dim))
    out = pl.pallas_call(
        ff_kernel,
        grid=(1,),
        in_specs=[tall, tall, square, square, line],
        out_specs=[tall, tall, square, square, line],
        out_shape=[jax.ShapeDtypeStruct((rows, dim), BF16)] * 2
        + [jax.ShapeDtypeStruct((dim, dim), BF16)] * 2
        + [jax.ShapeDtypeStruct((1, dim), F32)],
        scratch_shapes=[pltpu.VMEM((dim, dim), BF16)] * 2 + [pltpu.VMEM((rows, dim), BF16)] * 2,
        compiler_params=params(),
        cost_estimate=cost(12),
        name="feed",
    )(n2, gm, *pieces, bias.reshape(1, dim))
    return out[:2], out[2:4], out[4].reshape(2, dim // 2)


def middle_kernel(rows, parts, *refs):
    mlp_refs, gn2_refs = refs[:parts], refs[parts : 2 * parts]
    (hidden_ref, attn_ref, x_ref, cot_ref, live_ref, sig_ref, gm_ref, mix_ref, w_ref, vec_ref,
     block_ref, carry_ref, near_ref, far_ref, dw_near_ref, dw_far_ref, sum_ref, acc_ref) = refs[2 * parts :]
    step = pl.program_id(0)
    real = real_rows(rows)
    x = x_ref[...].astype(F32)
    cot = cot_ref[...].astype(F32)
    sig = sig_ref[...]
    gate = live_ref[...] * sig
    hidden = hidden_ref[...]
    mlp = vec_ref[6:7, :]
    gn2 = 0.0
    for ref in mlp_refs:
        mlp = mlp + ref[...].astype(F32)
    for ref in gn2_refs:
        gn2 = gn2 + ref[...].astype(F32)
    block_ref[...] = (hidden + gate * mlp).astype(BF16)
    scaled, inv = norm_parts(hidden)
    e = gn2 * vec_ref[4:5, :]
    grad_hidden = cot + inv * (
        e - jnp.mean(e, axis=-1, keepdims=True) - scaled * jnp.mean(e * scaled, axis=-1, keepdims=True)
    )
    gate_grad = jnp.sum(grad_hidden * attn_ref[...] + cot * mlp, axis=-1, keepdims=True)
    logit = live_ref[...] * gate_grad * sig * (1.0 - sig)
    carry_ref[...] = grad_hidden + logit * vec_ref[3:4, :]
    grad_attn = jnp.where(real, gate * grad_hidden, 0.0).astype(BF16)
    half = near_ref.shape[1]
    near_ref[...] = mm(grad_attn, w_ref[:half, :], NT).astype(BF16)
    far_ref[...] = mm(grad_attn, w_ref[half:, :], NT).astype(BF16)
    mix = jnp.where(real, mix_ref[...].astype(F32), 0.0).astype(BF16)
    update = mm(mix, grad_attn, TN)
    add = lambda v: jnp.sum(jnp.where(real, v, 0.0), axis=0, keepdims=True)
    sums = jnp.concatenate(
        [add(gn2 * scaled), add(gn2), add(grad_attn.astype(F32)), add(gm_ref[...].astype(F32)), add(x * logit),
         jnp.zeros((3, x.shape[1]), F32)], axis=0)

    @pl.when(step == 0)
    def _():
        acc_ref[...] = update
        sum_ref[...] = sums

    @pl.when(step > 0)
    def _():
        acc_ref[...] += update
        sum_ref[...] += sums

    @pl.when(step == pl.num_programs(0) - 1)
    def _():
        dw_near_ref[...] = acc_ref[:half, :].astype(BF16)
        dw_far_ref[...] = acc_ref[half:, :].astype(BF16)


def middle_call(mlp, gn2, *args):
    x, weight, vecs = args[2], args[8], args[9]
    rows, dim = x.shape
    half = dim // 2
    shapes = [((rows, dim), BF16), ((rows, dim), F32), ((rows, half), BF16), ((rows, half), BF16)]
    ins = (*mlp, *gn2, *args)
    return pl.pallas_call(
        functools.partial(middle_kernel, rows, len(mlp)),
        in_specs=[row_block(a.shape[1]) for a in ins[:-2]] + [whole(weight.shape), whole(vecs.shape)],
        out_specs=[row_block(s[1]) for s, _ in shapes] + [whole((half, dim))] * 2 + [whole((8, dim))],
        grid=(-(-rows // BLOCK),),
        out_shape=[jax.ShapeDtypeStruct(s, d) for s, d in shapes]
        + [jax.ShapeDtypeStruct((half, dim), BF16)] * 2
        + [jax.ShapeDtypeStruct((8, dim), F32)],
        scratch_shapes=[pltpu.VMEM((dim, dim), F32)],
        compiler_params=params(),
        cost_estimate=cost(11),
        name="middle",
    )(*ins)


def attend_back_kernel(*refs):
    qkv_ref, mix_ref, lse_ref, gmix_ref, live_ref, normed_ref, w_ref, dw_ref, gp_ref, bias_ref, vec_ref, gp_all = refs
    rows = qkv_ref.shape[0]
    third = w_ref.shape[0] // 3
    step = pl.program_id(0)
    lane = lax.broadcasted_iota(jnp.int32, (rows, 128), 1)
    key_bias = jnp.where(live_ref[...] > 0, 0.0, -1e30)
    lse_all = lse_ref[...]
    one = jnp.ones((rows, 1), F32)
    sums = []
    start = 0
    for pair in range(2):
        base = pair * 128
        width = min(128, third - base)
        q_pair = qkv_ref[:, base : base + 128].astype(F32)
        k_pair = qkv_ref[:, 256 + base : 384 + base].astype(F32)
        v_pair = qkv_ref[:, 512 + base : 640 + base].astype(F32)
        m_pair = mix_ref[:, base : base + 128].astype(F32)
        g_pair = gmix_ref[:, base : base + width].astype(F32)
        if width < 128:
            g_pair = jnp.concatenate([g_pair, jnp.zeros((rows, 128 - width), F32)], axis=1)
        gq = jnp.zeros((rows, 128), F32)
        gk = jnp.zeros((rows, 128), F32)
        gv = jnp.zeros((rows, 128), F32)
        for side in range(width // 64):
            inside = (lane >= side * 64) & (lane < side * 64 + 64)
            extra = 64 - side * 64
            lse = jnp.sum(jnp.where(lane == pair * 2 + side, lse_all, 0.0), axis=-1, keepdims=True)
            delta = jnp.sum(jnp.where(inside, g_pair * m_pair, 0.0), axis=-1, keepdims=True)
            l0, l1, l2 = split_three(lse)
            d0, d1, d2 = split_three(delta)
            q_ext = jnp.where(inside, q_pair, pick(lane, extra, (-l0, -l1, -l2, one), 0.0)).astype(BF16)
            k_ext = jnp.where(inside, k_pair, pick(lane, extra, (one, one, one, key_bias), 0.0)).astype(BF16)
            g_ext = jnp.where(inside, g_pair, pick(lane, extra, (-d0, -d1, -d2), 0.0)).astype(BF16)
            v_ext = jnp.where(inside, v_pair, pick(lane, extra, (one, one, one), 0.0)).astype(BF16)
            q_own = jnp.where(inside, q_pair, 0.0).astype(BF16)
            k_own = jnp.where(inside, k_pair, 0.0).astype(BF16)
            g_own = jnp.where(inside, g_pair, 0.0).astype(BF16)
            probs = jnp.exp(mm(k_ext, q_ext, NT))
            grad_scores = (probs * mm(v_ext, g_ext, NT)).astype(BF16)
            gv = gv + mm(probs.astype(BF16), g_own, NN)
            gk = gk + mm(grad_scores, q_own, NN)
            gq = gq + mm(grad_scores, k_own, TN)
        line = []
        for grad in (gq * HEAD**-0.5, gk, gv):
            piece = grad.astype(BF16)[:, :width]
            gp_ref[:, start : start + width] = piece
            line.append(jnp.sum(piece.astype(F32), axis=0, keepdims=True))
            start += width
        sums.append(jnp.concatenate(line, axis=0))
    gp_ref[:, start:] = jnp.zeros((rows, gp_ref.shape[1] - start), BF16)
    gp_all[pl.ds(pl.multiple_of(step * rows, 16), rows), :] = gp_ref[...]
    sums = jnp.concatenate(sums, axis=1)

    @pl.when(step == 0)
    def _():
        bias_ref[...] = sums

    @pl.when(step > 0)
    def _():
        bias_ref[...] += sums

    @pl.when(step == pl.num_programs(0) - 1)
    def _():
        update = mm(gp_all[...], normed_ref[...], TN)[: w_ref.shape[0], :]
        dw_ref[...] = update.astype(BF16)
        column = jnp.zeros((1, w_ref.shape[1]), F32)
        product = jnp.zeros((1, w_ref.shape[1]), F32)
        for part in range(3):
            terms = jnp.concatenate(split_three(bias_ref[part : part + 1, :]), axis=0).astype(BF16)
            rows_w = w_ref[part * third : (part + 1) * third, :]
            column = column + jnp.sum(mm(terms, rows_w, NN), axis=0, keepdims=True)
            lone = third - 128
            pair_rows = update[part * 128 : part * 128 + 128, :]
            lone_rows = update[3 * 128 + part * lone : 3 * 128 + (part + 1) * lone, :]
            own = jnp.concatenate([pair_rows, lone_rows], axis=0) * rows_w.astype(F32)
            product = product + jnp.sum(own, axis=0, keepdims=True)
        vec_ref[0:1, :] = product
        vec_ref[1:2, :] = column


def attend_back_call(qkv, mix, lse, gmix, live_col, normed, weight):
    rows, dim = normed.shape
    height = weight.shape[0]
    columns = -(-height // 128) * 128
    block = lambda lanes: pl.BlockSpec((SEQ, lanes), lambda i: (i, 0))
    ins = [qkv, mix, lse, gmix, live_col, normed, weight]
    return pl.pallas_call(
        attend_back_kernel,
        grid=(rows // SEQ,),
        in_specs=[block(a.shape[1]) for a in ins[:5]] + [whole(normed.shape), whole(weight.shape)],
        out_specs=[whole((height, dim)), block(columns), whole((3, height // 3)), whole((2, dim))],
        out_shape=[
            jax.ShapeDtypeStruct((height, dim), BF16),
            jax.ShapeDtypeStruct((rows, columns), BF16),
            jax.ShapeDtypeStruct((3, height // 3), F32),
            jax.ShapeDtypeStruct((2, dim), F32),
        ],
        scratch_shapes=[pltpu.VMEM((rows, columns), BF16)],
        compiler_params=params(),
        cost_estimate=cost(21),
        name="attend_back",
    )(*ins)


def last_kernel(groups, *refs):
    gp_refs, w_refs = refs[:groups], refs[groups : 2 * groups]
    x_ref, carry_ref, vec_ref, grad_ref = refs[2 * groups : 2 * groups + 4]
    scratch = refs[2 * groups + 4 :]

    @pl.when(pl.program_id(0) == 0)
    def _():
        for w_ref, to_ref in zip(w_refs, scratch):
            third = w_ref.shape[0] // 3
            start = 0
            base = 0
            for size in (128, third - 128):
                for part in range(3):
                    to_ref[start : start + size, :] = w_ref[part * third + base : part * third + base + size, :]
                    start += size
                base += size
            to_ref[start:, :] = jnp.zeros((to_ref.shape[0] - start, to_ref.shape[1]), BF16)

    gn = 0.0
    for gp_ref, to_ref in zip(gp_refs, scratch):
        gn = gn + mm(gp_ref[...], to_ref[...], NN)
    scaled, inv = norm_parts(x_ref[...].astype(F32))
    f = gn * vec_ref[0:1, :]
    grad_ref[...] = carry_ref[...] + inv * (
        f - jnp.mean(f, axis=-1, keepdims=True) - scaled * jnp.mean(f * scaled, axis=-1, keepdims=True)
    )


def last_call(groups, x, carry, vecs):
    rows, dim = x.shape
    gps = [g for _, g in groups]
    weights = [w for w, _ in groups]
    return pl.pallas_call(
        functools.partial(last_kernel, len(groups)),
        in_specs=[row_block(g.shape[1]) for g in gps]
        + [whole(w.shape) for w in weights]
        + [row_block(dim), row_block(dim), whole(vecs.shape)],
        out_specs=row_block(dim),
        grid=(-(-rows // BLOCK),),
        out_shape=jax.ShapeDtypeStruct((rows, dim), F32),
        scratch_shapes=[pltpu.VMEM((g.shape[1], dim), BF16) for g in gps],
        compiler_params=params(),
        cost_estimate=cost(9),
        name="last",
    )(*gps, *weights, x, carry, vecs)


def total(*terms):
    out = terms[0].astype(F32)
    for term in terms[1:]:
        out = out + term.astype(F32)
    return out.astype(BF16)


def after(first, *rest):
    return lax.optimization_barrier((first, *rest))


def unxor(value, index):
    count = value.shape[0]
    bit = 1
    while bit < count:
        split = value.reshape(count // (2 * bit), 2, bit, *value.shape[1:])
        value = jnp.where((index // bit) % 2 == 1, jnp.flip(split, 1), split).reshape(value.shape)
        bit *= 2
    return value


def stages(size):
    out = []
    stride = 2
    while stride < size:
        radix = 4 if size % (stride * 4) == 0 else 2
        out.append((stride, radix))
        stride *= radix
    return out


def dp_swap(value, size, offset):
    return lax.ppermute(value, "dp", [(i, i ^ offset) for i in range(size)])


def split_rows(value):
    high = value.astype(BF16)
    return jnp.concatenate([high, (value[:2] - high[:2].astype(F32)).astype(BF16)])


def join_rows(value):
    value = value.astype(F32)
    return jnp.concatenate([value[:2] + value[-2:], value[2:-2]])


def scatter_rest(value, vec, size, index):
    for stride, radix in stages(size):
        digit = (index // stride) % radix
        share = value.shape[0] // radix
        cut = lambda o: lax.dynamic_slice_in_dim(value, (digit ^ o) * share, share)
        send = cut if vec is None else lambda o: jnp.concatenate([cut(o), split_rows(vec)])
        got = [dp_swap(send(o), size, o * stride) for o in range(1, radix)]
        value = total(cut(0), *[g[:share] for g in got])
        if vec is not None:
            vec = vec + sum(join_rows(g[share:]) for g in got)
    return value, vec


def gather_rest(value, size):
    parts = [value]
    for stride, radix in reversed(stages(size)):
        value = jnp.concatenate(parts)
        parts = [value] + [dp_swap(value, size, o * stride) for o in range(1, radix - 1)]
        parts.append(dp_swap(value, size, (radix - 1) * stride))
    return parts


def natural_rest(value, size, index):
    order = 0
    for stride, radix in stages(size):
        order = order * radix + (index // stride) % radix
    blocks = value.reshape(size // 2, -1, value.shape[-1])
    return unxor(blocks, order).reshape(value.shape)


def scatter_side(value, side, size):
    half = value.shape[0] // 2
    send = lax.dynamic_slice_in_dim(value, (1 - side) * half, half)
    keep = lax.dynamic_slice_in_dim(value, side * half, half)
    return total(keep, dp_swap(send, size, 1))


def sum_tp(value):
    return value + sum(lax.ppermute(value, "tp", [(i, i ^ o) for i in range(4)]) for o in range(1, 4))


def body(
    size,
    tokens, cotangent, patch_rank, kept_counts, norm1_gain, norm1_shift, qkv_weight, query_bias, value_bias,
    out_weight, out_bias, router_weight, norm2_gain, norm2_shift, fc1_weight, fc1_bias, fc2_weight, fc2_bias,
):
    rows, dim = tokens.shape
    half = dim // 2
    images = patch_rank.shape[0]
    tp_index = lax.axis_index("tp")
    index = lax.axis_index("dp")
    core = tp_index % 2
    chip = tp_index // 2
    side = index % 2
    core_swap = lambda v: lax.ppermute(v, "tp", CORE_SWAP)
    y_swap = lambda v: lax.ppermute(v, "tp", Y_SWAP)
    x_swap = lambda v: dp_swap(v, size, 1)
    row_vec = lambda v: v.astype(F32).reshape(1, -1)

    width = out_weight.shape[0]
    qkv_own = jnp.transpose(qkv_weight, (1, 2, 0)).reshape(-1, dim)
    tokens_other = core_swap(tokens)
    qkv_y = y_swap(qkv_own)
    out_y = y_swap(out_weight)
    vecs = lines_call([norm1_gain, norm1_shift, out_bias, router_weight, norm2_gain, norm2_shift, fc2_bias], dim)
    small_own = lines_call([query_bias, value_bias, fc1_bias], dim)
    small_y = y_swap(small_own)

    padded = jnp.concatenate([patch_rank, jnp.full((images, SEQ - PATCHES), PATCHES, jnp.int32)], axis=1)
    live_image = (padded < kept_counts[:, None]).astype(F32)
    live_chip = lax.dynamic_slice_in_dim(live_image, chip * (images // 2), images // 2).reshape(-1, 1)
    live_own = lax.dynamic_slice_in_dim(live_chip, core * rows, rows)

    def pack(s):
        w1 = lax.dynamic_slice_in_dim(fc1_weight, s * half, half, axis=1)
        w2 = lax.dynamic_slice_in_dim(fc2_weight, s * half, half)
        return jnp.concatenate([w1, jnp.concatenate([w2[:, :half], w2[:, half:]])], axis=1)

    own_k, own_s = pack(side), pack(1 - side)
    core_line = jnp.full((1, dim), core, jnp.int32)
    normed, qkv_a, mix_a, lse_a = attend_call(
        tokens, (tokens_other, core_line, vecs), qkv_own, small_own[0:1, :width], small_own[1:2, :width], live_chip
    )
    normed, qkv_y, small_y, own_k, own_s, out_y = after(normed, qkv_y, small_y, own_k, own_s, out_y)
    out_yd = core_swap(out_y)
    y_k = y_swap(own_k)
    core_k, core_s, out_core, qkv_core = [core_swap(v) for v in (own_k, own_s, out_weight, qkv_own)]
    small_far = core_swap(jnp.stack([small_own, small_y]))

    qkv_b, mix_b, lse_b = attend_call(normed, (), qkv_y, small_y[0:1, :width], small_y[1:2, :width], live_chip)
    part = lambda v, s: lax.dynamic_slice(v, (s * rows, 0), (rows, width))
    send_mix = jnp.concatenate([part(mix_a, 1 - core), part(mix_b, 1 - core)], axis=1)
    mix_rows = jnp.concatenate([part(mix_a, core), part(mix_b, core), core_swap(send_mix)], axis=1)
    out_all = jnp.concatenate([out_weight, out_y, out_core, out_yd], axis=0)

    attn, hidden, n2, gm, sig = hidden_call(mix_rows, tokens, cotangent, live_own, out_all, vecs)
    n2, y_k, qkv_core, small_far = after(n2, y_k, qkv_core, small_far)
    y_s = x_swap(y_k)
    yd_k = core_swap(y_k)
    qkv_yd = core_swap(qkv_y)
    halves = lambda v: unxor(v[2].reshape(2, half), side)
    b_own, b_y, b_core, b_yd = halves(small_own), halves(small_y), halves(small_far[0]), halves(small_far[1])

    sums1, (dy_k, dyd_k), fb1 = ff_call(n2, gm, (y_k, yd_k), jnp.stack([b_y[0], b_yd[0]]))
    n2, dyd_k, dy_k, qkv_yd = after(n2, dyd_k, dy_k, qkv_yd)
    ryd_k = core_swap(dyd_k)
    sums2, (do_s, dc_s), fb2 = ff_call(n2, gm, (own_s, core_s), jnp.stack([b_own[1], b_core[1]]))
    n2, do_s, dc_s, ryd_k, y_s = after(n2, do_s, dc_s, ryd_k, y_s)
    rc_s = core_swap(dc_s)
    yd_s = core_swap(y_s)
    y_k_sum = total(dy_k, ryd_k)
    own_s_sum = total(do_s, rc_s)
    n2, y_k_sum, own_s_sum, yd_s = after(n2, y_k_sum, own_s_sum, yd_s)
    from_y_k = [y_swap(y_k_sum[:half])]
    from_x = [x_swap(own_s_sum[:half])]
    sums3, (dy_s, dyd_s), fb3 = ff_call(n2, gm, (y_s, yd_s), jnp.stack([b_y[1], b_yd[1]]))
    n2, dy_s, dyd_s, from_y_k[0], from_x[0] = after(n2, dy_s, dyd_s, from_y_k[0], from_x[0])
    y_k_sum, own_s_sum, n2 = after(y_k_sum, own_s_sum, n2)
    from_y_k.append(y_swap(y_k_sum[half:]))
    from_x.append(x_swap(own_s_sum[half:]))
    ryd_s = core_swap(dyd_s)
    sums4, (do_k, dc_k), fb4 = ff_call(n2, gm, (own_k, core_k), jnp.stack([b_own[0], b_core[0]]))
    sums4, do_k, dc_k, ryd_s, from_x[1], from_y_k[1] = after(sums4, do_k, dc_k, ryd_s, from_x[1], from_y_k[1])
    from_x, from_y_k = jnp.concatenate(from_x), jnp.concatenate(from_y_k)
    y_s_sum = total(dy_s, ryd_s)
    sums4, y_s_sum = after(sums4, y_s_sum)
    over_x = x_swap(y_s_sum[:half])
    over_y = y_swap(y_s_sum[half:])
    rc_k = core_swap(dc_k)

    four = (sums1, sums2, sums3, sums4)
    block_out, carry, gmix, gmix_far, d_out, d_out_far, vec2 = middle_call(
        [f[0] for f in four], [f[1] for f in four], hidden, attn, tokens, cotangent, live_own, sig, gm, mix_rows,
        out_all, vecs,
    )
    gmix, gmix_far, d_out_far, rc_k, vec2, over_x, over_y = after(
        gmix, gmix_far, d_out_far, rc_k, vec2, over_x, over_y
    )
    gmix_other = core_swap(gmix_far)
    rd_out = core_swap(d_out_far)

    join = lambda lo: jnp.where(
        core == 0,
        jnp.concatenate([gmix[:, lo : lo + width], gmix_other[:, lo : lo + width]]),
        jnp.concatenate([gmix_other[:, lo : lo + width], gmix[:, lo : lo + width]]),
    )
    gmix_a, gmix_b = join(0), join(width)
    rows_of = lambda v, s: lax.dynamic_slice_in_dim(v, s * rows, rows)

    over_xy = y_swap(over_x)
    over_yx = x_swap(over_y)
    gmix_b, rd_out = after(gmix_b, rd_out)
    d_out_half = total(d_out, rd_out)
    gmix_b, d_out_half = after(gmix_b, d_out_half)
    out_from_y = y_swap(d_out_half[width:])
    dy, gy, sy, vy = attend_back_call(qkv_b, mix_b, lse_b, gmix_b, live_chip, normed, qkv_y)
    gmix_a, dy, gy, over_xy, over_yx, out_from_y = after(gmix_a, dy, gy, over_xy, over_yx, out_from_y)
    ff_k = total(do_k, rc_k, from_y_k, from_x, jnp.concatenate([over_xy, over_yx]))
    gmix_a, ff_k = after(gmix_a, ff_k)
    ff_share = scatter_rest(ff_k, None, size, index)[0]
    from_y = y_swap(dy)
    rgy = core_swap(rows_of(gy, 1 - core))

    do, go, so, vo = attend_back_call(qkv_a, mix_a, lse_a, gmix_a, live_chip, normed, qkv_own)
    do, go, so, vo, from_y, rgy, ff_share = after(do, go, so, vo, from_y, rgy, ff_share)
    ff_parts = gather_rest(ff_share, size)
    rgo = core_swap(rows_of(go, 1 - core))
    qo_own = jnp.concatenate([total(do, from_y), total(d_out_half[:width], out_from_y)])
    fb_k, fb_s = jnp.stack([fb4[0], fb4[1], fb1[0], fb1[1]]), jnp.stack([fb2[0], fb2[1], fb3[0], fb3[1]])
    fb = unxor(jnp.stack([fb_k, fb_s]), side).transpose(1, 0, 2).reshape(4, dim)
    qv = lambda v: jnp.concatenate([v[0], v[2]])
    zero = jnp.zeros((2 * width,), F32)
    qv_rows = unxor(jnp.stack([qv(so), zero, qv(sy), zero]), tp_index).reshape(2, dim)
    lines = [vy + vo, vec2[:5], unxor(fb, tp_index), qv_rows, jnp.zeros((1, dim), F32)]
    lines = jnp.concatenate(lines)
    ready = len(ff_parts) - 1
    rgo, qo_own, carry, lines, *early = after(rgo, qo_own, carry, lines, *ff_parts[:ready])
    ff_parts = [*early, *ff_parts[ready:]]
    vec = sum_tp(lines)
    qo_keep = scatter_side(qo_own, side, size)
    keep = lambda v: rows_of(v, core)
    input_grad = last_call(
        ((qkv_y, keep(gy)), (qkv_yd, rgy), (qkv_own, keep(go)), (qkv_core, rgo)), tokens, carry, vecs
    )
    input_grad, qo_keep, vec, *ff_parts = after(input_grad, qo_keep, vec, *ff_parts)
    ff_mine = jnp.concatenate(ff_parts)
    ff_other = [x_swap(ff_mine[:half])]
    qo_share, vec = scatter_rest(qo_keep, vec, size, index)
    qo_share, vec, ff_other[0] = after(qo_share, vec, ff_other[0])
    qo_mine = jnp.concatenate(gather_rest(qo_share, size))
    swapped = x_swap(jnp.concatenate([ff_mine[half:], split_rows(vec)]))
    vec = vec + join_rows(swapped[half:])
    ff_other = jnp.concatenate([*ff_other, swapped[:half]])
    qo_both = unxor(jnp.stack([qo_mine, x_swap(qo_mine)]), side)
    qo_both = jax.vmap(lambda v: natural_rest(v, size, index))(qo_both).reshape(-1, dim)
    first = 3 * 128

    gain_one, shift_one = vecs[0], vecs[1]
    qv_grad = lax.dynamic_index_in_dim(vec[11:13].reshape(4, 2, width), tp_index, keepdims=False)
    fb_grad = lax.dynamic_index_in_dim(vec[:11], 7 + tp_index, keepdims=False)
    ff_both = unxor(jnp.stack([natural_rest(ff_mine, size, index), natural_rest(ff_other, size, index)]), side)
    ff_both = ff_both.astype(F32)
    fc1_grad = jnp.concatenate([ff_both[0, :, :half], ff_both[1, :, :half]], axis=1)
    second = lambda v: jnp.concatenate([v[:half, half:], v[half:, half:]], axis=1)
    fc2_grad = jnp.concatenate([second(ff_both[0]), second(ff_both[1])], axis=0)
    pair_part = qo_both[:first].reshape(3, 128, dim)
    last_part = qo_both[first : 3 * width].reshape(3, width - 128, dim)
    qkv_grad = jnp.concatenate([pair_part, last_part], axis=1).astype(F32)
    return (
        block_out,
        input_grad,
        (vec[0] - shift_one * vec[1]) / gain_one,
        vec[1],
        jnp.transpose(qkv_grad, (2, 0, 1)),
        qv_grad[0],
        qv_grad[1],
        qo_both[3 * width :].astype(F32),
        vec[4],
        vec[6],
        vec[2],
        vec[3],
        fc1_grad,
        fb_grad,
        fc2_grad,
        vec[5],
    )


def solution(mesh):
    return jax.shard_map(
        functools.partial(body, mesh.shape["dp"]),
        mesh=mesh,
        in_specs=(
            P(("dp", "tp"), None), P(("dp", "tp"), None), P("dp", None), P("dp"), P(), P(), P(None, None, "tp"),
            P("tp"), P("tp"), P("tp", None), P(), P(), P(), P(), P(None, "tp"), P("tp"), P("tp", None), P(),
        ),
        out_specs=(
            P(("dp", "tp"), None), P(("dp", "tp"), None), P(), P(), P(None, None, "tp"), P("tp"), P("tp"),
            P("tp", None), P(), P(), P(), P(), P(None, "tp"), P("tp"), P("tp", None), P(),
        ),
        check_vma=False,
    )
```

```python
import functools

import jax
import jax.numpy as jnp
from jax import lax
from jax.experimental import pallas as pl
from jax.experimental.pallas import tpu as pltpu
from jax.sharding import PartitionSpec as P

HEAD = 64
PATCHES = 577
SEQ = 592
EPS = 1e-06
F32 = jnp.float32
BF16 = jnp.bfloat16
MIB = 1024 * 1024
VMEM_BYTES = 44 * MIB
CORE_SWAP = [(0, 1), (1, 0), (2, 3), (3, 2)]
Y_SWAP = [(0, 2), (1, 3), (2, 0), (3, 1)]

NN = (((1,), (0,)), ((), ()))
NT = (((1,), (1,)), ((), ()))
TN = (((0,), (0,)), ((), ()))


def mm(left, right, dims):
    return lax.dot_general(left, right, dims, preferred_element_type=F32)


def params(size=VMEM_BYTES):
    return pltpu.CompilerParams(vmem_limit_bytes=size)


def cost(micros):
    return pl.CostEstimate(flops=int(micros * 0.11e9), bytes_accessed=int(micros * 1e5), transcendentals=0)


def whole(shape):
    rank = len(shape)
    return pl.BlockSpec(shape, lambda *ids: (0,) * rank)


def norm_parts(values):
    centre = values - jnp.mean(values, axis=-1, keepdims=True)
    inv = lax.rsqrt(jnp.mean(centre * centre, axis=-1, keepdims=True) + EPS)
    return centre * inv, inv


def split_three(column):
    high = column.astype(BF16).astype(F32)
    rest = column - high
    middle = rest.astype(BF16).astype(F32)
    return high, middle, (rest - middle).astype(BF16).astype(F32)


def pick(lane, base, columns, other):
    out = other
    for place, column in enumerate(columns):
        out = jnp.where(lane == base + place, column, out)
    return out


def lines_kernel(*refs):
    *ins, out_ref = refs
    lines = []
    for ref in ins:
        line = ref[...].astype(F32).reshape(1, -1)
        if line.shape[1] < out_ref.shape[1]:
            line = jnp.concatenate([line, jnp.zeros((1, out_ref.shape[1] - line.shape[1]), F32)], axis=1)
        lines.append(line)
    fill = jnp.zeros((out_ref.shape[0] - len(lines), out_ref.shape[1]), F32)
    out_ref[...] = jnp.concatenate(lines + [fill], axis=0)


def lines_call(vectors, dim):
    rows = -(-len(vectors) // 8) * 8
    return pl.pallas_call(
        lines_kernel,
        out_shape=jax.ShapeDtypeStruct((rows, dim), F32),
        cost_estimate=cost(1),
        name="lines",
    )(*vectors)


def attend_kernel(first, *refs):
    step = pl.program_id(0)
    if first:
        own_ref, other_ref, core_ref, vec_ref, w_ref, qb_ref, vb_ref, live_ref = refs[:8]
        normed_ref, qkv_ref, mix_ref, lse_ref = refs[8:]
        here = pl.ds(pl.multiple_of(step * SEQ, 16), SEQ)

        @pl.when(step == 0)
        def _():
            own, other = own_ref[...].astype(F32), other_ref[...].astype(F32)
            swap = core_ref[...] > 0
            blocks = [jnp.where(swap, other, own), jnp.where(swap, own, other)]
            rows = own.shape[0]
            for image in range(2 * rows // SEQ):
                pieces = []
                start, left = image * SEQ, SEQ
                while left:
                    block, at = start // rows, start % rows
                    take = min(left, rows - at)
                    pieces.append(blocks[block][at : at + take, :])
                    start, left = start + take, left - take
                x = pieces[0] if len(pieces) == 1 else jnp.concatenate(pieces, axis=0)
                scaled, _ = norm_parts(x)
                value = (scaled * vec_ref[0:1, :] + vec_ref[1:2, :]).astype(BF16)
                normed_ref[image * SEQ : (image + 1) * SEQ, :] = value

        normed = normed_ref[here, :]
    else:
        x_ref, w_ref, qb_ref, vb_ref, live_ref, qkv_ref, mix_ref, lse_ref = refs
        normed = x_ref[...]
    width = w_ref.shape[0] // 3
    rows = normed.shape[0]
    queries = (mm(normed, w_ref[:width, :], NT) + qb_ref[...]).astype(BF16)
    qkv_ref[:, :width] = (queries.astype(F32) * HEAD**-0.5).astype(BF16)
    qkv_ref[:, 256 : 256 + width] = mm(normed, w_ref[width : 2 * width, :], NT).astype(BF16)
    qkv_ref[:, 512 : 512 + width] = (mm(normed, w_ref[2 * width :, :], NT) + vb_ref[...]).astype(BF16)
    for i in range(3):
        qkv_ref[:, i * 256 + width : i * 256 + 256] = jnp.zeros((rows, 256 - width), BF16)
    lane = lax.broadcasted_iota(jnp.int32, (rows, 128), 1)
    key_bias = jnp.where(live_ref[...] > 0, 0.0, -1e30)
    lse_all = jnp.zeros((rows, 128), F32)
    for pair in range(2):
        base = pair * 128
        q_pair = qkv_ref[:, base : base + 128].astype(F32)
        k_pair = qkv_ref[:, 256 + base : 384 + base].astype(F32)
        v_pair = qkv_ref[:, 512 + base : 640 + base].astype(F32)
        mixed = jnp.zeros((rows, 128), F32)
        for side in range(2 if pair == 0 else 1):
            inside = (lane >= side * 64) & (lane < side * 64 + 64)
            extra = 64 - side * 64
            q_ext = jnp.where(inside, q_pair, jnp.where(lane == extra, 1.0, 0.0)).astype(BF16)
            k_ext = jnp.where(inside, k_pair, jnp.where(lane == extra, key_bias, 0.0)).astype(BF16)
            v_own = jnp.where(inside, v_pair, 0.0).astype(BF16)
            scores = mm(q_ext, k_ext, NT)
            top = jnp.max(scores, axis=-1, keepdims=True)
            weights = jnp.exp(scores - top)
            total = jnp.sum(weights, axis=-1, keepdims=True)
            mixed = mixed + mm(weights.astype(BF16), v_own, NN) * (1.0 / total)
            lse_all = jnp.where(lane == pair * 2 + side, top + jnp.log(total), lse_all)
        mix_ref[:, base : base + 128] = mixed.astype(BF16)
    lse_ref[...] = lse_all


def attend_call(x, extras, weight, q_bias, v_bias, live_col):
    rows, dim = live_col.shape[0], x.shape[1]
    width = weight.shape[0] // 3
    block = lambda lanes: pl.BlockSpec((SEQ, lanes), lambda i: (i, 0))
    shapes = [((rows, 768), BF16), ((rows, 256), BF16), ((rows, 128), F32)]
    out_specs = [block(s[1]) for s, _ in shapes]
    kinds = [pltpu.HBM] * 3
    if extras:
        shapes = [((rows, dim), BF16)] + shapes
        kinds = [jax.ShapeDtypeStruct] + kinds
        out_specs = [whole((rows, dim))] + out_specs
    return pl.pallas_call(
        functools.partial(attend_kernel, bool(extras)),
        grid=(rows // SEQ,),
        in_specs=[whole(x.shape) if extras else block(dim)]
        + [whole(e.shape) for e in extras]
        + [whole(weight.shape), whole((1, width)), whole((1, width)), block(1)],
        out_specs=out_specs,
        out_shape=[kind(s, d) for kind, (s, d) in zip(kinds, shapes)],
        compiler_params=params(),
        cost_estimate=cost(13),
        name="attend",
    )(x, *extras, weight, q_bias, v_bias, live_col)


BLOCK = 224


def row_block(lanes):
    return pl.BlockSpec((BLOCK, lanes), lambda i: (i, 0))


def real_rows(rows):
    place = pl.program_id(0) * BLOCK + lax.broadcasted_iota(jnp.int32, (BLOCK, 1), 0)
    return place < rows


def hidden_kernel(rows, mix_ref, x_ref, cot_ref, live_ref, w_ref, vec_ref,
                  attn_ref, hidden_ref, normed_ref, gm_ref, sig_ref):
    x = x_ref[...].astype(F32)
    attention = mm(mix_ref[...], w_ref[...], NN) + vec_ref[2:3, :]
    sig = jax.nn.sigmoid(jnp.sum(x * vec_ref[3:4, :], axis=-1, keepdims=True))
    gate = live_ref[...] * sig
    hidden = x + gate * attention
    scaled, _ = norm_parts(hidden)
    real = real_rows(rows)
    attn_ref[...] = attention
    hidden_ref[...] = hidden
    normed_ref[...] = jnp.where(real, scaled * vec_ref[4:5, :] + vec_ref[5:6, :], 0.0).astype(BF16)
    gm_ref[...] = jnp.where(real, gate * cot_ref[...].astype(F32), 0.0).astype(BF16)
    sig_ref[...] = sig


def hidden_call(mix, x, cot, live_col, weight, vecs):
    rows, dim = x.shape
    steps = -(-rows // BLOCK)
    args = (mix, x, cot, live_col, weight, vecs)
    shapes = [((rows, dim), F32), ((rows, dim), F32), ((steps * BLOCK, dim), BF16), ((steps * BLOCK, dim), BF16),
              ((rows, 1), F32)]
    return pl.pallas_call(
        functools.partial(hidden_kernel, rows),
        in_specs=[row_block(a.shape[1]) for a in args[:4]] + [whole(a.shape) for a in args[4:]],
        out_specs=[row_block(s[1]) for s, _ in shapes],
        grid=(steps,),
        out_shape=[(pltpu.HBM if d == F32 and s[1] == dim else jax.ShapeDtypeStruct)(s, d) for s, d in shapes],
        compiler_params=params(),
        cost_estimate=cost(7),
        name="hidden",
    )(*args)


def ff_kernel(n2_ref, gm_ref, a_ref, b_ref, bias_ref, mlp_ref, gn2_ref, da_ref, db_ref, dbias_ref,
              w1, w2, act_all, pre_all):
    half = w1.shape[0] // 2
    for i, piece in enumerate((a_ref, b_ref)):
        at = i * half
        w1[:, at : at + half] = piece[:, :half]
        w2[at : at + half, :half] = piece[:half, half:]
        w2[at : at + half, half:] = piece[half:, half:]
    steps = 2
    size = n2_ref.shape[0] // steps
    sums = 0.0
    for step in range(steps):
        at = slice(step * size, (step + 1) * size)
        pre = mm(n2_ref[at, :], w1[...], NN) + bias_ref[...]
        grad_act = mm(gm_ref[at, :], w2[...], NT)
        cdf = 0.5 * (1.0 + lax.erf(pre * (0.5**0.5)))
        slope = cdf + pre * (jnp.exp(-0.5 * pre * pre) * (0.5 / jnp.pi) ** 0.5)
        grad_pre = (grad_act * slope).astype(BF16)
        act_all[at, :] = (pre * cdf).astype(BF16)
        pre_all[at, :] = grad_pre
        sums = sums + jnp.sum(grad_pre.astype(F32), axis=0, keepdims=True)
        mlp_ref[at, :] = mm(act_all[at, :], w2[...], NN).astype(BF16)
        gn2_ref[at, :] = mm(pre_all[at, :], w1[...], NT).astype(BF16)
    dbias_ref[...] = sums
    d2 = mm(act_all[...], gm_ref[...], TN).astype(BF16)
    d1 = mm(n2_ref[...], pre_all[...], TN).astype(BF16)
    for i, grad in enumerate((da_ref, db_ref)):
        at = i * half
        grad[:, :half] = d1[:, at : at + half]
        grad[:half, half:] = d2[at : at + half, :half]
        grad[half:, half:] = d2[at : at + half, half:]


def ff_call(n2, gm, pieces, bias):
    rows, dim = n2.shape
    tall, square, line = whole((rows, dim)), whole((dim, dim)), whole((1, dim))
    out = pl.pallas_call(
        ff_kernel,
        grid=(1,),
        in_specs=[tall, tall, square, square, line],
        out_specs=[tall, tall, square, square, line],
        out_shape=[pltpu.HBM((rows, dim), BF16)] * 2
        + [pltpu.HBM((dim, dim), BF16)] * 2
        + [jax.ShapeDtypeStruct((1, dim), F32)],
        scratch_shapes=[pltpu.VMEM((dim, dim), BF16)] * 2 + [pltpu.VMEM((rows, dim), BF16)] * 2,
        compiler_params=params(),
        cost_estimate=cost(12),
        name="feed",
    )(n2, gm, *pieces, bias.reshape(1, dim))
    return out[:2], out[2:4], out[4].reshape(2, dim // 2)


def middle_kernel(rows, parts, *refs):
    mlp_refs, gn2_refs = refs[:parts], refs[parts : 2 * parts]
    (hidden_ref, attn_ref, x_ref, cot_ref, live_ref, sig_ref, gm_ref, mix_ref, w_ref, vec_ref,
     block_ref, carry_ref, near_ref, far_ref, dw_near_ref, dw_far_ref, sum_ref, acc_ref) = refs[2 * parts :]
    step = pl.program_id(0)
    real = real_rows(rows)
    x = x_ref[...].astype(F32)
    cot = cot_ref[...].astype(F32)
    sig = sig_ref[...]
    gate = live_ref[...] * sig
    hidden = hidden_ref[...]
    mlp = vec_ref[6:7, :]
    gn2 = 0.0
    for ref in mlp_refs:
        mlp = mlp + ref[...].astype(F32)
    for ref in gn2_refs:
        gn2 = gn2 + ref[...].astype(F32)
    block_ref[...] = (hidden + gate * mlp).astype(BF16)
    scaled, inv = norm_parts(hidden)
    e = gn2 * vec_ref[4:5, :]
    grad_hidden = cot + inv * (
        e - jnp.mean(e, axis=-1, keepdims=True) - scaled * jnp.mean(e * scaled, axis=-1, keepdims=True)
    )
    gate_grad = jnp.sum(grad_hidden * attn_ref[...] + cot * mlp, axis=-1, keepdims=True)
    logit = live_ref[...] * gate_grad * sig * (1.0 - sig)
    carry_ref[...] = grad_hidden + logit * vec_ref[3:4, :]
    grad_attn = jnp.where(real, gate * grad_hidden, 0.0).astype(BF16)
    half = near_ref.shape[1]
    near_ref[...] = mm(grad_attn, w_ref[:half, :], NT).astype(BF16)
    far_ref[...] = mm(grad_attn, w_ref[half:, :], NT).astype(BF16)
    mix = jnp.where(real, mix_ref[...].astype(F32), 0.0).astype(BF16)
    update = mm(mix, grad_attn, TN)
    add = lambda v: jnp.sum(jnp.where(real, v, 0.0), axis=0, keepdims=True)
    sums = jnp.concatenate(
        [add(gn2 * scaled), add(gn2), add(grad_attn.astype(F32)), add(gm_ref[...].astype(F32)), add(x * logit),
         jnp.zeros((3, x.shape[1]), F32)], axis=0)

    @pl.when(step == 0)
    def _():
        acc_ref[...] = update
        sum_ref[...] = sums

    @pl.when(step > 0)
    def _():
        acc_ref[...] += update
        sum_ref[...] += sums

    @pl.when(step == pl.num_programs(0) - 1)
    def _():
        dw_near_ref[...] = acc_ref[:half, :].astype(BF16)
        dw_far_ref[...] = acc_ref[half:, :].astype(BF16)


def middle_call(mlp, gn2, *args):
    x, weight, vecs = args[2], args[8], args[9]
    rows, dim = x.shape
    half = dim // 2
    shapes = [((rows, dim), BF16), ((rows, dim), F32), ((rows, half), BF16), ((rows, half), BF16)]
    ins = (*mlp, *gn2, *args)
    return pl.pallas_call(
        functools.partial(middle_kernel, rows, len(mlp)),
        in_specs=[row_block(a.shape[1]) for a in ins[:-2]] + [whole(weight.shape), whole(vecs.shape)],
        out_specs=[row_block(s[1]) for s, _ in shapes] + [whole((half, dim))] * 2 + [whole((8, dim))],
        grid=(-(-rows // BLOCK),),
        out_shape=[pltpu.HBM(s, d) for s, d in shapes]
        + [pltpu.HBM((half, dim), BF16)] * 2
        + [jax.ShapeDtypeStruct((8, dim), F32)],
        scratch_shapes=[pltpu.VMEM((dim, dim), F32)],
        compiler_params=params(60 * MIB),
        cost_estimate=cost(11),
        name="middle",
    )(*ins)


def attend_back_kernel(*refs):
    qkv_ref, mix_ref, lse_ref, gmix_ref, live_ref, normed_ref, w_ref, dw_ref, gp_ref, bias_ref, vec_ref, gp_all = refs
    rows = qkv_ref.shape[0]
    third = w_ref.shape[0] // 3
    step = pl.program_id(0)
    lane = lax.broadcasted_iota(jnp.int32, (rows, 128), 1)
    key_bias = jnp.where(live_ref[...] > 0, 0.0, -1e30)
    lse_all = lse_ref[...]
    one = jnp.ones((rows, 1), F32)
    sums = []
    start = 0
    for pair in range(2):
        base = pair * 128
        width = min(128, third - base)
        q_pair = qkv_ref[:, base : base + 128].astype(F32)
        k_pair = qkv_ref[:, 256 + base : 384 + base].astype(F32)
        v_pair = qkv_ref[:, 512 + base : 640 + base].astype(F32)
        m_pair = mix_ref[:, base : base + 128].astype(F32)
        g_pair = gmix_ref[:, base : base + width].astype(F32)
        if width < 128:
            g_pair = jnp.concatenate([g_pair, jnp.zeros((rows, 128 - width), F32)], axis=1)
        gq = jnp.zeros((rows, 128), F32)
        gk = jnp.zeros((rows, 128), F32)
        gv = jnp.zeros((rows, 128), F32)
        for side in range(width // 64):
            inside = (lane >= side * 64) & (lane < side * 64 + 64)
            extra = 64 - side * 64
            lse = jnp.sum(jnp.where(lane == pair * 2 + side, lse_all, 0.0), axis=-1, keepdims=True)
            delta = jnp.sum(jnp.where(inside, g_pair * m_pair, 0.0), axis=-1, keepdims=True)
            l0, l1, l2 = split_three(lse)
            d0, d1, d2 = split_three(delta)
            q_ext = jnp.where(inside, q_pair, pick(lane, extra, (-l0, -l1, -l2, one), 0.0)).astype(BF16)
            k_ext = jnp.where(inside, k_pair, pick(lane, extra, (one, one, one, key_bias), 0.0)).astype(BF16)
            g_ext = jnp.where(inside, g_pair, pick(lane, extra, (-d0, -d1, -d2), 0.0)).astype(BF16)
            v_ext = jnp.where(inside, v_pair, pick(lane, extra, (one, one, one), 0.0)).astype(BF16)
            q_own = jnp.where(inside, q_pair, 0.0).astype(BF16)
            k_own = jnp.where(inside, k_pair, 0.0).astype(BF16)
            g_own = jnp.where(inside, g_pair, 0.0).astype(BF16)
            probs = jnp.exp(mm(k_ext, q_ext, NT))
            grad_scores = (probs * mm(v_ext, g_ext, NT)).astype(BF16)
            gv = gv + mm(probs.astype(BF16), g_own, NN)
            gk = gk + mm(grad_scores, q_own, NN)
            gq = gq + mm(grad_scores, k_own, TN)
        line = []
        for grad in (gq * HEAD**-0.5, gk, gv):
            piece = grad.astype(BF16)[:, :width]
            gp_ref[:, start : start + width] = piece
            line.append(jnp.sum(piece.astype(F32), axis=0, keepdims=True))
            start += width
        sums.append(jnp.concatenate(line, axis=0))
    gp_ref[:, start:] = jnp.zeros((rows, gp_ref.shape[1] - start), BF16)
    gp_all[pl.ds(pl.multiple_of(step * rows, 16), rows), :] = gp_ref[...]
    sums = jnp.concatenate(sums, axis=1)

    @pl.when(step == 0)
    def _():
        bias_ref[...] = sums

    @pl.when(step > 0)
    def _():
        bias_ref[...] += sums

    @pl.when(step == pl.num_programs(0) - 1)
    def _():
        update = mm(gp_all[...], normed_ref[...], TN)[: w_ref.shape[0], :]
        dw_ref[...] = update.astype(BF16)
        column = jnp.zeros((1, w_ref.shape[1]), F32)
        product = jnp.zeros((1, w_ref.shape[1]), F32)
        for part in range(3):
            terms = jnp.concatenate(split_three(bias_ref[part : part + 1, :]), axis=0).astype(BF16)
            rows_w = w_ref[part * third : (part + 1) * third, :]
            column = column + jnp.sum(mm(terms, rows_w, NN), axis=0, keepdims=True)
            lone = third - 128
            pair_rows = update[part * 128 : part * 128 + 128, :]
            lone_rows = update[3 * 128 + part * lone : 3 * 128 + (part + 1) * lone, :]
            own = jnp.concatenate([pair_rows, lone_rows], axis=0) * rows_w.astype(F32)
            product = product + jnp.sum(own, axis=0, keepdims=True)
        vec_ref[0:1, :] = product
        vec_ref[1:2, :] = column


def attend_back_call(qkv, mix, lse, gmix, live_col, normed, weight):
    rows, dim = normed.shape
    height = weight.shape[0]
    columns = -(-height // 128) * 128
    block = lambda lanes: pl.BlockSpec((SEQ, lanes), lambda i: (i, 0))
    ins = [qkv, mix, lse, gmix, live_col, normed, weight]
    return pl.pallas_call(
        attend_back_kernel,
        grid=(rows // SEQ,),
        in_specs=[block(a.shape[1]) for a in ins[:5]] + [whole(normed.shape), whole(weight.shape)],
        out_specs=[whole((height, dim)), block(columns), whole((3, height // 3)), whole((2, dim))],
        out_shape=[
            pltpu.HBM((height, dim), BF16),
            pltpu.HBM((rows, columns), BF16),
            jax.ShapeDtypeStruct((3, height // 3), F32),
            jax.ShapeDtypeStruct((2, dim), F32),
        ],
        scratch_shapes=[pltpu.VMEM((rows, columns), BF16)],
        compiler_params=params(),
        cost_estimate=cost(21),
        name="attend_back",
    )(*ins)


def last_kernel(groups, *refs):
    gp_refs, w_refs = refs[:groups], refs[groups : 2 * groups]
    x_ref, carry_ref, vec_ref, grad_ref = refs[2 * groups : 2 * groups + 4]
    scratch = refs[2 * groups + 4 :]

    @pl.when(pl.program_id(0) == 0)
    def _():
        for w_ref, to_ref in zip(w_refs, scratch):
            third = w_ref.shape[0] // 3
            start = 0
            base = 0
            for size in (128, third - 128):
                for part in range(3):
                    to_ref[start : start + size, :] = w_ref[part * third + base : part * third + base + size, :]
                    start += size
                base += size
            to_ref[start:, :] = jnp.zeros((to_ref.shape[0] - start, to_ref.shape[1]), BF16)

    gn = 0.0
    for gp_ref, to_ref in zip(gp_refs, scratch):
        gn = gn + mm(gp_ref[...], to_ref[...], NN)
    scaled, inv = norm_parts(x_ref[...].astype(F32))
    f = gn * vec_ref[0:1, :]
    grad_ref[...] = carry_ref[...] + inv * (
        f - jnp.mean(f, axis=-1, keepdims=True) - scaled * jnp.mean(f * scaled, axis=-1, keepdims=True)
    )


def last_call(groups, x, carry, vecs):
    rows, dim = x.shape
    gps = [g for _, g in groups]
    weights = [w for w, _ in groups]
    return pl.pallas_call(
        functools.partial(last_kernel, len(groups)),
        in_specs=[row_block(g.shape[1]) for g in gps]
        + [whole(w.shape) for w in weights]
        + [row_block(dim), row_block(dim), whole(vecs.shape)],
        out_specs=row_block(dim),
        grid=(-(-rows // BLOCK),),
        out_shape=jax.ShapeDtypeStruct((rows, dim), F32),
        scratch_shapes=[pltpu.VMEM((g.shape[1], dim), BF16) for g in gps],
        compiler_params=params(60 * MIB),
        cost_estimate=cost(9),
        name="last",
    )(*gps, *weights, x, carry, vecs)


def total(*terms):
    out = terms[0].astype(F32)
    for term in terms[1:]:
        out = out + term.astype(F32)
    return out.astype(BF16)


def after(first, *rest):
    return lax.optimization_barrier((first, *rest))


def unxor(value, index):
    count = value.shape[0]
    bit = 1
    while bit < count:
        split = value.reshape(count // (2 * bit), 2, bit, *value.shape[1:])
        value = jnp.where((index // bit) % 2 == 1, jnp.flip(split, 1), split).reshape(value.shape)
        bit *= 2
    return value


def stages(size):
    out = []
    stride = 2
    while stride < size:
        radix = 4 if size % (stride * 4) == 0 else 2
        out.append((stride, radix))
        stride *= radix
    return out


def dp_swap(value, size, offset):
    return lax.ppermute(value, "dp", [(i, i ^ offset) for i in range(size)])


def split_rows(value):
    high = value.astype(BF16)
    return jnp.concatenate([high, (value[:2] - high[:2].astype(F32)).astype(BF16)])


def join_rows(value):
    value = value.astype(F32)
    return jnp.concatenate([value[:2] + value[-2:], value[2:-2]])


def scatter_rest(value, vec, size, index):
    for stride, radix in stages(size):
        digit = (index // stride) % radix
        share = value.shape[0] // radix
        cut = lambda o: lax.dynamic_slice_in_dim(value, (digit ^ o) * share, share)
        send = cut if vec is None else lambda o: jnp.concatenate([cut(o), split_rows(vec)])
        got = [dp_swap(send(o), size, o * stride) for o in range(1, radix)]
        value = total(cut(0), *[g[:share] for g in got])
        if vec is not None:
            vec = vec + sum(join_rows(g[share:]) for g in got)
    return value, vec


def gather_rest(value, size):
    parts = [value]
    for stride, radix in reversed(stages(size)):
        value = jnp.concatenate(parts)
        parts = [value] + [dp_swap(value, size, o * stride) for o in range(1, radix - 1)]
        parts.append(dp_swap(value, size, (radix - 1) * stride))
    return parts


def natural_rest(value, size, index):
    order = 0
    for stride, radix in stages(size):
        order = order * radix + (index // stride) % radix
    blocks = value.reshape(size // 2, -1, value.shape[-1])
    return unxor(blocks, order).reshape(value.shape)


def scatter_side(value, side, size):
    half = value.shape[0] // 2
    send = lax.dynamic_slice_in_dim(value, (1 - side) * half, half)
    keep = lax.dynamic_slice_in_dim(value, side * half, half)
    return total(keep, dp_swap(send, size, 1))


def sum_tp(value):
    return value + sum(lax.ppermute(value, "tp", [(i, i ^ o) for i in range(4)]) for o in range(1, 4))


def body(
    size,
    tokens, cotangent, patch_rank, kept_counts, norm1_gain, norm1_shift, qkv_weight, query_bias, value_bias,
    out_weight, out_bias, router_weight, norm2_gain, norm2_shift, fc1_weight, fc1_bias, fc2_weight, fc2_bias,
):
    rows, dim = tokens.shape
    half = dim // 2
    images = patch_rank.shape[0]
    tp_index = lax.axis_index("tp")
    index = lax.axis_index("dp")
    core = tp_index % 2
    chip = tp_index // 2
    side = index % 2
    core_swap = lambda v: lax.ppermute(v, "tp", CORE_SWAP)
    y_swap = lambda v: lax.ppermute(v, "tp", Y_SWAP)
    x_swap = lambda v: dp_swap(v, size, 1)
    row_vec = lambda v: v.astype(F32).reshape(1, -1)

    width = out_weight.shape[0]
    qkv_own = jnp.transpose(qkv_weight, (1, 2, 0)).reshape(-1, dim)
    tokens_other = core_swap(tokens)
    qkv_y = y_swap(qkv_own)
    out_y = y_swap(out_weight)
    vecs = lines_call([norm1_gain, norm1_shift, out_bias, router_weight, norm2_gain, norm2_shift, fc2_bias], dim)
    small_own = lines_call([query_bias, value_bias, fc1_bias], dim)
    small_y = y_swap(small_own)

    padded = jnp.concatenate([patch_rank, jnp.full((images, SEQ - PATCHES), PATCHES, jnp.int32)], axis=1)
    live_image = (padded < kept_counts[:, None]).astype(F32)
    live_chip = lax.dynamic_slice_in_dim(live_image, chip * (images // 2), images // 2).reshape(-1, 1)
    live_own = lax.dynamic_slice_in_dim(live_chip, core * rows, rows)

    def pack(s):
        w1 = lax.dynamic_slice_in_dim(fc1_weight, s * half, half, axis=1)
        w2 = lax.dynamic_slice_in_dim(fc2_weight, s * half, half)
        return jnp.concatenate([w1, jnp.concatenate([w2[:, :half], w2[:, half:]])], axis=1)

    own_k, own_s = pack(side), pack(1 - side)
    core_line = jnp.full((1, dim), core, jnp.int32)
    normed, qkv_a, mix_a, lse_a = attend_call(
        tokens, (tokens_other, core_line, vecs), qkv_own, small_own[0:1, :width], small_own[1:2, :width], live_chip
    )
    normed, qkv_y, small_y, own_k, own_s, out_y = after(normed, qkv_y, small_y, own_k, own_s, out_y)
    out_yd = core_swap(out_y)
    y_k = y_swap(own_k)
    core_k, core_s, out_core, qkv_core = [core_swap(v) for v in (own_k, own_s, out_weight, qkv_own)]
    small_far = core_swap(jnp.stack([small_own, small_y]))

    qkv_b, mix_b, lse_b = attend_call(normed, (), qkv_y, small_y[0:1, :width], small_y[1:2, :width], live_chip)
    part = lambda v, s: lax.dynamic_slice(v, (s * rows, 0), (rows, width))
    send_mix = jnp.concatenate([part(mix_a, 1 - core), part(mix_b, 1 - core)], axis=1)
    mix_rows = jnp.concatenate([part(mix_a, core), part(mix_b, core), core_swap(send_mix)], axis=1)
    out_all = jnp.concatenate([out_weight, out_y, out_core, out_yd], axis=0)

    attn, hidden, n2, gm, sig = hidden_call(mix_rows, tokens, cotangent, live_own, out_all, vecs)
    n2, y_k, qkv_core, small_far = after(n2, y_k, qkv_core, small_far)
    y_s = x_swap(y_k)
    yd_k = core_swap(y_k)
    qkv_yd = core_swap(qkv_y)
    halves = lambda v: unxor(v[2].reshape(2, half), side)
    b_own, b_y, b_core, b_yd = halves(small_own), halves(small_y), halves(small_far[0]), halves(small_far[1])

    sums1, (dy_k, dyd_k), fb1 = ff_call(n2, gm, (y_k, yd_k), jnp.stack([b_y[0], b_yd[0]]))
    n2, dyd_k, dy_k, qkv_yd = after(n2, dyd_k, dy_k, qkv_yd)
    ryd_k = core_swap(dyd_k)
    sums2, (do_s, dc_s), fb2 = ff_call(n2, gm, (own_s, core_s), jnp.stack([b_own[1], b_core[1]]))
    n2, do_s, dc_s, ryd_k, y_s = after(n2, do_s, dc_s, ryd_k, y_s)
    rc_s = core_swap(dc_s)
    yd_s = core_swap(y_s)
    y_k_sum = total(dy_k, ryd_k)
    own_s_sum = total(do_s, rc_s)
    n2, y_k_sum, own_s_sum, yd_s = after(n2, y_k_sum, own_s_sum, yd_s)
    from_y_k = [y_swap(y_k_sum[:half])]
    from_x = [x_swap(own_s_sum[:half])]
    sums3, (dy_s, dyd_s), fb3 = ff_call(n2, gm, (y_s, yd_s), jnp.stack([b_y[1], b_yd[1]]))
    n2, dy_s, dyd_s, from_y_k[0], from_x[0] = after(n2, dy_s, dyd_s, from_y_k[0], from_x[0])
    y_k_sum, own_s_sum, n2 = after(y_k_sum, own_s_sum, n2)
    from_y_k.append(y_swap(y_k_sum[half:]))
    from_x.append(x_swap(own_s_sum[half:]))
    ryd_s = core_swap(dyd_s)
    sums4, (do_k, dc_k), fb4 = ff_call(n2, gm, (own_k, core_k), jnp.stack([b_own[0], b_core[0]]))
    sums4, do_k, dc_k, ryd_s, from_x[1], from_y_k[1] = after(sums4, do_k, dc_k, ryd_s, from_x[1], from_y_k[1])
    from_x, from_y_k = jnp.concatenate(from_x), jnp.concatenate(from_y_k)
    y_s_sum = total(dy_s, ryd_s)
    sums4, y_s_sum = after(sums4, y_s_sum)
    over_x = x_swap(y_s_sum[:half])
    over_y = y_swap(y_s_sum[half:])
    rc_k = core_swap(dc_k)

    four = (sums1, sums2, sums3, sums4)
    block_out, carry, gmix, gmix_far, d_out, d_out_far, vec2 = middle_call(
        [f[0] for f in four], [f[1] for f in four], hidden, attn, tokens, cotangent, live_own, sig, gm, mix_rows,
        out_all, vecs,
    )
    gmix, gmix_far, d_out_far, rc_k, vec2, over_x, over_y = after(
        gmix, gmix_far, d_out_far, rc_k, vec2, over_x, over_y
    )
    gmix_other = core_swap(gmix_far)
    rd_out = core_swap(d_out_far)

    join = lambda lo: jnp.where(
        core == 0,
        jnp.concatenate([gmix[:, lo : lo + width], gmix_other[:, lo : lo + width]]),
        jnp.concatenate([gmix_other[:, lo : lo + width], gmix[:, lo : lo + width]]),
    )
    gmix_a, gmix_b = join(0), join(width)
    rows_of = lambda v, s: lax.dynamic_slice_in_dim(v, s * rows, rows)

    over_xy = y_swap(over_x)
    over_yx = x_swap(over_y)
    gmix_b, rd_out = after(gmix_b, rd_out)
    d_out_half = total(d_out, rd_out)
    gmix_b, d_out_half = after(gmix_b, d_out_half)
    out_from_y = y_swap(d_out_half[width:])
    dy, gy, sy, vy = attend_back_call(qkv_b, mix_b, lse_b, gmix_b, live_chip, normed, qkv_y)
    gmix_a, dy, gy, over_xy, over_yx, out_from_y = after(gmix_a, dy, gy, over_xy, over_yx, out_from_y)
    ff_k = total(do_k, rc_k, from_y_k, from_x, jnp.concatenate([over_xy, over_yx]))
    gmix_a, ff_k = after(gmix_a, ff_k)
    ff_share = scatter_rest(ff_k, None, size, index)[0]
    from_y = y_swap(dy)
    rgy = core_swap(rows_of(gy, 1 - core))

    do, go, so, vo = attend_back_call(qkv_a, mix_a, lse_a, gmix_a, live_chip, normed, qkv_own)
    do, go, so, vo, from_y, rgy, ff_share = after(do, go, so, vo, from_y, rgy, ff_share)
    ff_parts = gather_rest(ff_share, size)
    rgo = core_swap(rows_of(go, 1 - core))
    qo_own = jnp.concatenate([total(do, from_y), total(d_out_half[:width], out_from_y)])
    fb_k, fb_s = jnp.stack([fb4[0], fb4[1], fb1[0], fb1[1]]), jnp.stack([fb2[0], fb2[1], fb3[0], fb3[1]])
    fb = unxor(jnp.stack([fb_k, fb_s]), side).transpose(1, 0, 2).reshape(4, dim)
    qv = lambda v: jnp.concatenate([v[0], v[2]])
    zero = jnp.zeros((2 * width,), F32)
    qv_rows = unxor(jnp.stack([qv(so), zero, qv(sy), zero]), tp_index).reshape(2, dim)
    lines = [vy + vo, vec2[:5], unxor(fb, tp_index), qv_rows, jnp.zeros((1, dim), F32)]
    lines = jnp.concatenate(lines)
    ready = len(ff_parts) - 1
    rgo, qo_own, carry, lines, *early = after(rgo, qo_own, carry, lines, *ff_parts[:ready])
    ff_parts = [*early, *ff_parts[ready:]]
    vec = sum_tp(lines)
    qo_keep = scatter_side(qo_own, side, size)
    keep = lambda v: rows_of(v, core)
    input_grad = last_call(
        ((qkv_y, keep(gy)), (qkv_yd, rgy), (qkv_own, keep(go)), (qkv_core, rgo)), tokens, carry, vecs
    )
    input_grad, qo_keep, vec, *ff_parts = after(input_grad, qo_keep, vec, *ff_parts)
    ff_mine = jnp.concatenate(ff_parts)
    ff_other = [x_swap(ff_mine[:half])]
    qo_share, vec = scatter_rest(qo_keep, vec, size, index)
    qo_share, vec, ff_other[0] = after(qo_share, vec, ff_other[0])
    qo_mine = jnp.concatenate(gather_rest(qo_share, size))
    swapped = x_swap(jnp.concatenate([ff_mine[half:], split_rows(vec)]))
    vec = vec + join_rows(swapped[half:])
    ff_other = jnp.concatenate([*ff_other, swapped[:half]])
    qo_both = unxor(jnp.stack([qo_mine, x_swap(qo_mine)]), side)
    qo_both = jax.vmap(lambda v: natural_rest(v, size, index))(qo_both).reshape(-1, dim)
    first = 3 * 128

    gain_one, shift_one = vecs[0], vecs[1]
    qv_grad = lax.dynamic_index_in_dim(vec[11:13].reshape(4, 2, width), tp_index, keepdims=False)
    fb_grad = lax.dynamic_index_in_dim(vec[:11], 7 + tp_index, keepdims=False)
    ff_both = unxor(jnp.stack([natural_rest(ff_mine, size, index), natural_rest(ff_other, size, index)]), side)
    ff_both = ff_both.astype(F32)
    fc1_grad = jnp.concatenate([ff_both[0, :, :half], ff_both[1, :, :half]], axis=1)
    second = lambda v: jnp.concatenate([v[:half, half:], v[half:, half:]], axis=1)
    fc2_grad = jnp.concatenate([second(ff_both[0]), second(ff_both[1])], axis=0)
    pair_part = qo_both[:first].reshape(3, 128, dim)
    last_part = qo_both[first : 3 * width].reshape(3, width - 128, dim)
    qkv_grad = jnp.concatenate([pair_part, last_part], axis=1).astype(F32)
    return (
        block_out,
        input_grad,
        (vec[0] - shift_one * vec[1]) / gain_one,
        vec[1],
        jnp.transpose(qkv_grad, (2, 0, 1)),
        qv_grad[0],
        qv_grad[1],
        qo_both[3 * width :].astype(F32),
        vec[4],
        vec[6],
        vec[2],
        vec[3],
        fc1_grad,
        fb_grad,
        fc2_grad,
        vec[5],
    )


def solution(mesh):
    return jax.shard_map(
        functools.partial(body, mesh.shape["dp"]),
        mesh=mesh,
        in_specs=(
            P(("dp", "tp"), None), P(("dp", "tp"), None), P("dp", None), P("dp"), P(), P(), P(None, None, "tp"),
            P("tp"), P("tp"), P("tp", None), P(), P(), P(), P(), P(None, "tp"), P("tp"), P("tp", None), P(),
        ),
        out_specs=(
            P(("dp", "tp"), None), P(("dp", "tp"), None), P(), P(), P(None, None, "tp"), P("tp"), P("tp"),
            P("tp", None), P(), P(), P(), P(), P(None, "tp"), P("tp"), P("tp", None), P(),
        ),
        check_vma=False,
    )
```

```python
import functools

import jax
import jax.numpy as jnp
from jax import lax
from jax.experimental import pallas as pl
from jax.experimental.pallas import tpu as pltpu
from jax.sharding import PartitionSpec as P

HEAD = 64
PATCHES = 577
SEQ = 592
EPS = 1e-06
F32 = jnp.float32
BF16 = jnp.bfloat16
MIB = 1024 * 1024
VMEM_BYTES = 44 * MIB
CORE_SWAP = [(0, 1), (1, 0), (2, 3), (3, 2)]
Y_SWAP = [(0, 2), (1, 3), (2, 0), (3, 1)]

NN = (((1,), (0,)), ((), ()))
NT = (((1,), (1,)), ((), ()))
TN = (((0,), (0,)), ((), ()))


def mm(left, right, dims):
    return lax.dot_general(left, right, dims, preferred_element_type=F32)


def params(size=VMEM_BYTES):
    return pltpu.CompilerParams(vmem_limit_bytes=size)


def cost(micros):
    return pl.CostEstimate(flops=int(micros * 0.11e9), bytes_accessed=int(micros * 1e5), transcendentals=0)


def whole(shape):
    rank = len(shape)
    return pl.BlockSpec(shape, lambda *ids: (0,) * rank)


def norm_parts(values):
    centre = values - jnp.mean(values, axis=-1, keepdims=True)
    inv = lax.rsqrt(jnp.mean(centre * centre, axis=-1, keepdims=True) + EPS)
    return centre * inv, inv


def split_three(column):
    high = column.astype(BF16).astype(F32)
    rest = column - high
    middle = rest.astype(BF16).astype(F32)
    return high, middle, (rest - middle).astype(BF16).astype(F32)


def pick(lane, base, columns, other):
    out = other
    for place, column in enumerate(columns):
        out = jnp.where(lane == base + place, column, out)
    return out


def lines_kernel(*refs):
    *ins, out_ref = refs
    lines = []
    for ref in ins:
        line = ref[...].astype(F32).reshape(1, -1)
        if line.shape[1] < out_ref.shape[1]:
            line = jnp.concatenate([line, jnp.zeros((1, out_ref.shape[1] - line.shape[1]), F32)], axis=1)
        lines.append(line)
    fill = jnp.zeros((out_ref.shape[0] - len(lines), out_ref.shape[1]), F32)
    out_ref[...] = jnp.concatenate(lines + [fill], axis=0)


def lines_call(vectors, dim):
    rows = -(-len(vectors) // 8) * 8
    return pl.pallas_call(
        lines_kernel,
        out_shape=jax.ShapeDtypeStruct((rows, dim), F32),
        cost_estimate=cost(1),
        name="lines",
    )(*vectors)


def attend_kernel(first, *refs):
    step = pl.program_id(0)
    if first:
        own_ref, other_ref, core_ref, vec_ref, w_ref, qb_ref, vb_ref, live_ref = refs[:8]
        normed_ref, qkv_ref, mix_ref, lse_ref = refs[8:]
        here = pl.ds(pl.multiple_of(step * SEQ, 16), SEQ)

        @pl.when(step == 0)
        def _():
            own, other = own_ref[...].astype(F32), other_ref[...].astype(F32)
            swap = core_ref[...] > 0
            blocks = [jnp.where(swap, other, own), jnp.where(swap, own, other)]
            rows = own.shape[0]
            for image in range(2 * rows // SEQ):
                pieces = []
                start, left = image * SEQ, SEQ
                while left:
                    block, at = start // rows, start % rows
                    take = min(left, rows - at)
                    pieces.append(blocks[block][at : at + take, :])
                    start, left = start + take, left - take
                x = pieces[0] if len(pieces) == 1 else jnp.concatenate(pieces, axis=0)
                scaled, _ = norm_parts(x)
                value = (scaled * vec_ref[0:1, :] + vec_ref[1:2, :]).astype(BF16)
                normed_ref[image * SEQ : (image + 1) * SEQ, :] = value

        normed = normed_ref[here, :]
    else:
        x_ref, w_ref, qb_ref, vb_ref, live_ref, qkv_ref, mix_ref, lse_ref = refs
        normed = x_ref[...]
    width = w_ref.shape[0] // 3
    rows = normed.shape[0]
    queries = (mm(normed, w_ref[:width, :], NT) + qb_ref[...]).astype(BF16)
    qkv_ref[:, :width] = (queries.astype(F32) * HEAD**-0.5).astype(BF16)
    qkv_ref[:, 256 : 256 + width] = mm(normed, w_ref[width : 2 * width, :], NT).astype(BF16)
    qkv_ref[:, 512 : 512 + width] = (mm(normed, w_ref[2 * width :, :], NT) + vb_ref[...]).astype(BF16)
    for i in range(3):
        qkv_ref[:, i * 256 + width : i * 256 + 256] = jnp.zeros((rows, 256 - width), BF16)
    lane = lax.broadcasted_iota(jnp.int32, (rows, 128), 1)
    key_bias = jnp.where(live_ref[...] > 0, 0.0, -1e30)
    lse_all = jnp.zeros((rows, 128), F32)
    heads = []
    for pair in range(2):
        base = pair * 128
        q_pair = qkv_ref[:, base : base + 128].astype(F32)
        k_pair = qkv_ref[:, 256 + base : 384 + base].astype(F32)
        v_pair = qkv_ref[:, 512 + base : 640 + base].astype(F32)
        for side in range(2 if pair == 0 else 1):
            inside = (lane >= side * 64) & (lane < side * 64 + 64)
            extra = 64 - side * 64
            q_ext = jnp.where(inside, q_pair, jnp.where(lane == extra, 1.0, 0.0)).astype(BF16)
            k_ext = jnp.where(inside, k_pair, jnp.where(lane == extra, key_bias, 0.0)).astype(BF16)
            v_own = jnp.where(inside, v_pair, 0.0).astype(BF16)
            heads.append((pair, side, mm(q_ext, k_ext, NT), v_own))
    mixed = [0.0, 0.0]
    for pair, side, scores, v_own in heads:
        top = jnp.max(scores, axis=-1, keepdims=True)
        weights = jnp.exp(scores - top)
        total = jnp.sum(weights, axis=-1, keepdims=True)
        mixed[pair] = mixed[pair] + mm(weights.astype(BF16), v_own, NN) * (1.0 / total)
        lse_all = jnp.where(lane == pair * 2 + side, top + jnp.log(total), lse_all)
    for pair in range(2):
        mix_ref[:, pair * 128 : pair * 128 + 128] = mixed[pair].astype(BF16)
    lse_ref[...] = lse_all


def attend_call(x, extras, weight, q_bias, v_bias, live_col):
    rows, dim = live_col.shape[0], x.shape[1]
    width = weight.shape[0] // 3
    block = lambda lanes: pl.BlockSpec((SEQ, lanes), lambda i: (i, 0))
    shapes = [((rows, 768), BF16), ((rows, 256), BF16), ((rows, 128), F32)]
    out_specs = [block(s[1]) for s, _ in shapes]
    kinds = [pltpu.HBM] * 3
    if extras:
        shapes = [((rows, dim), BF16)] + shapes
        kinds = [jax.ShapeDtypeStruct] + kinds
        out_specs = [whole((rows, dim))] + out_specs
    return pl.pallas_call(
        functools.partial(attend_kernel, bool(extras)),
        grid=(rows // SEQ,),
        in_specs=[whole(x.shape) if extras else block(dim)]
        + [whole(e.shape) for e in extras]
        + [whole(weight.shape), whole((1, width)), whole((1, width)), block(1)],
        out_specs=out_specs,
        out_shape=[kind(s, d) for kind, (s, d) in zip(kinds, shapes)],
        compiler_params=params(),
        cost_estimate=cost(13),
        name="attend",
    )(x, *extras, weight, q_bias, v_bias, live_col)


BLOCK = 224


def row_block(lanes):
    return pl.BlockSpec((BLOCK, lanes), lambda i: (i, 0))


def real_rows(rows):
    place = pl.program_id(0) * BLOCK + lax.broadcasted_iota(jnp.int32, (BLOCK, 1), 0)
    return place < rows


def hidden_kernel(rows, mix_ref, x_ref, cot_ref, live_ref, w_ref, vec_ref,
                  attn_ref, hidden_ref, normed_ref, gm_ref, sig_ref):
    x = x_ref[...].astype(F32)
    attention = mm(mix_ref[...], w_ref[...], NN) + vec_ref[2:3, :]
    sig = jax.nn.sigmoid(jnp.sum(x * vec_ref[3:4, :], axis=-1, keepdims=True))
    gate = live_ref[...] * sig
    hidden = x + gate * attention
    scaled, _ = norm_parts(hidden)
    real = real_rows(rows)
    attn_ref[...] = attention
    hidden_ref[...] = hidden
    normed_ref[...] = jnp.where(real, scaled * vec_ref[4:5, :] + vec_ref[5:6, :], 0.0).astype(BF16)
    gm_ref[...] = jnp.where(real, gate * cot_ref[...].astype(F32), 0.0).astype(BF16)
    sig_ref[...] = sig


def hidden_call(mix, x, cot, live_col, weight, vecs):
    rows, dim = x.shape
    steps = -(-rows // BLOCK)
    args = (mix, x, cot, live_col, weight, vecs)
    shapes = [((rows, dim), F32), ((rows, dim), F32), ((steps * BLOCK, dim), BF16), ((steps * BLOCK, dim), BF16),
              ((rows, 1), F32)]
    return pl.pallas_call(
        functools.partial(hidden_kernel, rows),
        in_specs=[row_block(a.shape[1]) for a in args[:4]] + [whole(a.shape) for a in args[4:]],
        out_specs=[row_block(s[1]) for s, _ in shapes],
        grid=(steps,),
        out_shape=[(pltpu.HBM if d == F32 and s[1] == dim else jax.ShapeDtypeStruct)(s, d) for s, d in shapes],
        compiler_params=params(),
        cost_estimate=cost(7),
        name="hidden",
    )(*args)


def ff_kernel(n2_ref, gm_ref, a_ref, b_ref, bias_ref, mlp_ref, gn2_ref, da_ref, db_ref, dbias_ref,
              w1, w2, act_all, pre_all):
    half = w1.shape[0] // 2
    for i, piece in enumerate((a_ref, b_ref)):
        at = i * half
        w1[:, at : at + half] = piece[:, :half]
        w2[at : at + half, :half] = piece[:half, half:]
        w2[at : at + half, half:] = piece[half:, half:]
    steps = 2
    size = n2_ref.shape[0] // steps
    sums = 0.0
    for step in range(steps):
        at = slice(step * size, (step + 1) * size)
        pre = mm(n2_ref[at, :], w1[...], NN) + bias_ref[...]
        grad_act = mm(gm_ref[at, :], w2[...], NT)
        cdf = 0.5 * (1.0 + lax.erf(pre * (0.5**0.5)))
        slope = cdf + pre * (jnp.exp(-0.5 * pre * pre) * (0.5 / jnp.pi) ** 0.5)
        grad_pre = (grad_act * slope).astype(BF16)
        act_all[at, :] = (pre * cdf).astype(BF16)
        pre_all[at, :] = grad_pre
        sums = sums + jnp.sum(grad_pre.astype(F32), axis=0, keepdims=True)
        mlp_ref[at, :] = mm(act_all[at, :], w2[...], NN).astype(BF16)
        gn2_ref[at, :] = mm(pre_all[at, :], w1[...], NT).astype(BF16)
    dbias_ref[...] = sums
    d2 = mm(act_all[...], gm_ref[...], TN).astype(BF16)
    d1 = mm(n2_ref[...], pre_all[...], TN).astype(BF16)
    for i, grad in enumerate((da_ref, db_ref)):
        at = i * half
        grad[:, :half] = d1[:, at : at + half]
        grad[:half, half:] = d2[at : at + half, :half]
        grad[half:, half:] = d2[at : at + half, half:]


def ff_call(n2, gm, pieces, bias):
    rows, dim = n2.shape
    tall, square, line = whole((rows, dim)), whole((dim, dim)), whole((1, dim))
    out = pl.pallas_call(
        ff_kernel,
        grid=(1,),
        in_specs=[tall, tall, square, square, line],
        out_specs=[tall, tall, square, square, line],
        out_shape=[pltpu.HBM((rows, dim), BF16)] * 2
        + [pltpu.HBM((dim, dim), BF16)] * 2
        + [jax.ShapeDtypeStruct((1, dim), F32)],
        scratch_shapes=[pltpu.VMEM((dim, dim), BF16)] * 2 + [pltpu.VMEM((rows, dim), BF16)] * 2,
        compiler_params=params(),
        cost_estimate=cost(12),
        name="feed",
    )(n2, gm, *pieces, bias.reshape(1, dim))
    return out[:2], out[2:4], out[4].reshape(2, dim // 2)


def middle_kernel(rows, parts, *refs):
    mlp_refs, gn2_refs = refs[:parts], refs[parts : 2 * parts]
    (hidden_ref, attn_ref, x_ref, cot_ref, live_ref, sig_ref, gm_ref, mix_ref, w_ref, vec_ref,
     block_ref, carry_ref, near_ref, far_ref, dw_near_ref, dw_far_ref, sum_ref, acc_ref) = refs[2 * parts :]
    step = pl.program_id(0)
    real = real_rows(rows)
    x = x_ref[...].astype(F32)
    cot = cot_ref[...].astype(F32)
    sig = sig_ref[...]
    gate = live_ref[...] * sig
    hidden = hidden_ref[...]
    mlp = vec_ref[6:7, :]
    gn2 = 0.0
    for ref in mlp_refs:
        mlp = mlp + ref[...].astype(F32)
    for ref in gn2_refs:
        gn2 = gn2 + ref[...].astype(F32)
    block_ref[...] = (hidden + gate * mlp).astype(BF16)
    scaled, inv = norm_parts(hidden)
    e = gn2 * vec_ref[4:5, :]
    grad_hidden = cot + inv * (
        e - jnp.mean(e, axis=-1, keepdims=True) - scaled * jnp.mean(e * scaled, axis=-1, keepdims=True)
    )
    gate_grad = jnp.sum(grad_hidden * attn_ref[...] + cot * mlp, axis=-1, keepdims=True)
    logit = live_ref[...] * gate_grad * sig * (1.0 - sig)
    carry_ref[...] = grad_hidden + logit * vec_ref[3:4, :]
    grad_attn = jnp.where(real, gate * grad_hidden, 0.0).astype(BF16)
    half = near_ref.shape[1]
    near_ref[...] = mm(grad_attn, w_ref[:half, :], NT).astype(BF16)
    far_ref[...] = mm(grad_attn, w_ref[half:, :], NT).astype(BF16)
    mix = jnp.where(real, mix_ref[...].astype(F32), 0.0).astype(BF16)
    update = mm(mix, grad_attn, TN)
    add = lambda v: jnp.sum(jnp.where(real, v, 0.0), axis=0, keepdims=True)
    sums = jnp.concatenate(
        [add(gn2 * scaled), add(gn2), add(grad_attn.astype(F32)), add(gm_ref[...].astype(F32)), add(x * logit),
         jnp.zeros((3, x.shape[1]), F32)], axis=0)

    @pl.when(step == 0)
    def _():
        acc_ref[...] = update
        sum_ref[...] = sums

    @pl.when(step > 0)
    def _():
        acc_ref[...] += update
        sum_ref[...] += sums

    @pl.when(step == pl.num_programs(0) - 1)
    def _():
        dw_near_ref[...] = acc_ref[:half, :].astype(BF16)
        dw_far_ref[...] = acc_ref[half:, :].astype(BF16)


def middle_call(mlp, gn2, *args):
    x, weight, vecs = args[2], args[8], args[9]
    rows, dim = x.shape
    half = dim // 2
    shapes = [((rows, dim), BF16), ((rows, dim), F32), ((rows, half), BF16), ((rows, half), BF16)]
    ins = (*mlp, *gn2, *args)
    return pl.pallas_call(
        functools.partial(middle_kernel, rows, len(mlp)),
        in_specs=[row_block(a.shape[1]) for a in ins[:-2]] + [whole(weight.shape), whole(vecs.shape)],
        out_specs=[row_block(s[1]) for s, _ in shapes] + [whole((half, dim))] * 2 + [whole((8, dim))],
        grid=(-(-rows // BLOCK),),
        out_shape=[pltpu.HBM(s, d) for s, d in shapes]
        + [pltpu.HBM((half, dim), BF16)] * 2
        + [jax.ShapeDtypeStruct((8, dim), F32)],
        scratch_shapes=[pltpu.VMEM((dim, dim), F32)],
        compiler_params=params(60 * MIB),
        cost_estimate=cost(11),
        name="middle",
    )(*ins)


def attend_back_kernel(*refs):
    qkv_ref, mix_ref, lse_ref, gmix_ref, live_ref, normed_ref, w_ref, dw_ref, gp_ref, bias_ref, vec_ref, gp_all = refs
    rows = qkv_ref.shape[0]
    third = w_ref.shape[0] // 3
    step = pl.program_id(0)
    lane = lax.broadcasted_iota(jnp.int32, (rows, 128), 1)
    key_bias = jnp.where(live_ref[...] > 0, 0.0, -1e30)
    lse_all = lse_ref[...]
    one = jnp.ones((rows, 1), F32)
    sums = []
    start = 0
    for pair in range(2):
        base = pair * 128
        width = min(128, third - base)
        q_pair = qkv_ref[:, base : base + 128].astype(F32)
        k_pair = qkv_ref[:, 256 + base : 384 + base].astype(F32)
        v_pair = qkv_ref[:, 512 + base : 640 + base].astype(F32)
        m_pair = mix_ref[:, base : base + 128].astype(F32)
        g_pair = gmix_ref[:, base : base + width].astype(F32)
        if width < 128:
            g_pair = jnp.concatenate([g_pair, jnp.zeros((rows, 128 - width), F32)], axis=1)
        gq = jnp.zeros((rows, 128), F32)
        gk = jnp.zeros((rows, 128), F32)
        gv = jnp.zeros((rows, 128), F32)
        for side in range(width // 64):
            inside = (lane >= side * 64) & (lane < side * 64 + 64)
            extra = 64 - side * 64
            lse = jnp.sum(jnp.where(lane == pair * 2 + side, lse_all, 0.0), axis=-1, keepdims=True)
            delta = jnp.sum(jnp.where(inside, g_pair * m_pair, 0.0), axis=-1, keepdims=True)
            l0, l1, l2 = split_three(lse)
            d0, d1, d2 = split_three(delta)
            q_ext = jnp.where(inside, q_pair, pick(lane, extra, (-l0, -l1, -l2, one), 0.0)).astype(BF16)
            k_ext = jnp.where(inside, k_pair, pick(lane, extra, (one, one, one, key_bias), 0.0)).astype(BF16)
            g_ext = jnp.where(inside, g_pair, pick(lane, extra, (-d0, -d1, -d2), 0.0)).astype(BF16)
            v_ext = jnp.where(inside, v_pair, pick(lane, extra, (one, one, one), 0.0)).astype(BF16)
            q_own = jnp.where(inside, q_pair, 0.0).astype(BF16)
            k_own = jnp.where(inside, k_pair, 0.0).astype(BF16)
            g_own = jnp.where(inside, g_pair, 0.0).astype(BF16)
            probs = jnp.exp(mm(k_ext, q_ext, NT))
            grad_scores = (probs * mm(v_ext, g_ext, NT)).astype(BF16)
            gv = gv + mm(probs.astype(BF16), g_own, NN)
            gk = gk + mm(grad_scores, q_own, NN)
            gq = gq + mm(grad_scores, k_own, TN)
        line = []
        for grad in (gq * HEAD**-0.5, gk, gv):
            piece = grad.astype(BF16)[:, :width]
            gp_ref[:, start : start + width] = piece
            line.append(jnp.sum(piece.astype(F32), axis=0, keepdims=True))
            start += width
        sums.append(jnp.concatenate(line, axis=0))
    gp_ref[:, start:] = jnp.zeros((rows, gp_ref.shape[1] - start), BF16)
    gp_all[pl.ds(pl.multiple_of(step * rows, 16), rows), :] = gp_ref[...]
    sums = jnp.concatenate(sums, axis=1)

    @pl.when(step == 0)
    def _():
        bias_ref[...] = sums

    @pl.when(step > 0)
    def _():
        bias_ref[...] += sums

    @pl.when(step == pl.num_programs(0) - 1)
    def _():
        update = mm(gp_all[...], normed_ref[...], TN)[: w_ref.shape[0], :]
        dw_ref[...] = update.astype(BF16)
        column = jnp.zeros((1, w_ref.shape[1]), F32)
        product = jnp.zeros((1, w_ref.shape[1]), F32)
        for part in range(3):
            terms = jnp.concatenate(split_three(bias_ref[part : part + 1, :]), axis=0).astype(BF16)
            rows_w = w_ref[part * third : (part + 1) * third, :]
            column = column + jnp.sum(mm(terms, rows_w, NN), axis=0, keepdims=True)
            lone = third - 128
            pair_rows = update[part * 128 : part * 128 + 128, :]
            lone_rows = update[3 * 128 + part * lone : 3 * 128 + (part + 1) * lone, :]
            own = jnp.concatenate([pair_rows, lone_rows], axis=0) * rows_w.astype(F32)
            product = product + jnp.sum(own, axis=0, keepdims=True)
        vec_ref[0:1, :] = product
        vec_ref[1:2, :] = column


def attend_back_call(qkv, mix, lse, gmix, live_col, normed, weight):
    rows, dim = normed.shape
    height = weight.shape[0]
    columns = -(-height // 128) * 128
    block = lambda lanes: pl.BlockSpec((SEQ, lanes), lambda i: (i, 0))
    ins = [qkv, mix, lse, gmix, live_col, normed, weight]
    return pl.pallas_call(
        attend_back_kernel,
        grid=(rows // SEQ,),
        in_specs=[block(a.shape[1]) for a in ins[:5]] + [whole(normed.shape), whole(weight.shape)],
        out_specs=[whole((height, dim)), block(columns), whole((3, height // 3)), whole((2, dim))],
        out_shape=[
            pltpu.HBM((height, dim), BF16),
            pltpu.HBM((rows, columns), BF16),
            jax.ShapeDtypeStruct((3, height // 3), F32),
            jax.ShapeDtypeStruct((2, dim), F32),
        ],
        scratch_shapes=[pltpu.VMEM((rows, columns), BF16)],
        compiler_params=params(),
        cost_estimate=cost(21),
        name="attend_back",
    )(*ins)


def last_kernel(groups, *refs):
    gp_refs, w_refs = refs[:groups], refs[groups : 2 * groups]
    x_ref, carry_ref, vec_ref, grad_ref = refs[2 * groups : 2 * groups + 4]
    scratch = refs[2 * groups + 4 :]

    @pl.when(pl.program_id(0) == 0)
    def _():
        for w_ref, to_ref in zip(w_refs, scratch):
            third = w_ref.shape[0] // 3
            start = 0
            base = 0
            for size in (128, third - 128):
                for part in range(3):
                    to_ref[start : start + size, :] = w_ref[part * third + base : part * third + base + size, :]
                    start += size
                base += size
            to_ref[start:, :] = jnp.zeros((to_ref.shape[0] - start, to_ref.shape[1]), BF16)

    gn = 0.0
    for gp_ref, to_ref in zip(gp_refs, scratch):
        gn = gn + mm(gp_ref[...], to_ref[...], NN)
    scaled, inv = norm_parts(x_ref[...].astype(F32))
    f = gn * vec_ref[0:1, :]
    grad_ref[...] = carry_ref[...] + inv * (
        f - jnp.mean(f, axis=-1, keepdims=True) - scaled * jnp.mean(f * scaled, axis=-1, keepdims=True)
    )


def last_call(groups, x, carry, vecs):
    rows, dim = x.shape
    gps = [g for _, g in groups]
    weights = [w for w, _ in groups]
    return pl.pallas_call(
        functools.partial(last_kernel, len(groups)),
        in_specs=[row_block(g.shape[1]) for g in gps]
        + [whole(w.shape) for w in weights]
        + [row_block(dim), row_block(dim), whole(vecs.shape)],
        out_specs=row_block(dim),
        grid=(-(-rows // BLOCK),),
        out_shape=jax.ShapeDtypeStruct((rows, dim), F32),
        scratch_shapes=[pltpu.VMEM((g.shape[1], dim), BF16) for g in gps],
        compiler_params=params(60 * MIB),
        cost_estimate=cost(9),
        name="last",
    )(*gps, *weights, x, carry, vecs)


def total(*terms):
    out = terms[0].astype(F32)
    for term in terms[1:]:
        out = out + term.astype(F32)
    return out.astype(BF16)


def after(first, *rest):
    return lax.optimization_barrier((first, *rest))


def unxor(value, index):
    count = value.shape[0]
    bit = 1
    while bit < count:
        split = value.reshape(count // (2 * bit), 2, bit, *value.shape[1:])
        value = jnp.where((index // bit) % 2 == 1, jnp.flip(split, 1), split).reshape(value.shape)
        bit *= 2
    return value


def stages(size):
    out = []
    stride = 2
    while stride < size:
        radix = 4 if size % (stride * 4) == 0 else 2
        out.append((stride, radix))
        stride *= radix
    return out


def dp_swap(value, size, offset):
    return lax.ppermute(value, "dp", [(i, i ^ offset) for i in range(size)])


def split_rows(value):
    high = value.astype(BF16)
    return jnp.concatenate([high, (value[:2] - high[:2].astype(F32)).astype(BF16)])


def join_rows(value):
    value = value.astype(F32)
    return jnp.concatenate([value[:2] + value[-2:], value[2:-2]])


def scatter_rest(value, size, index):
    for stride, radix in stages(size):
        digit = (index // stride) % radix
        share = value.shape[0] // radix
        cut = lambda o: lax.dynamic_slice_in_dim(value, (digit ^ o) * share, share)
        value = total(cut(0), *[dp_swap(cut(o), size, o * stride) for o in range(1, radix)])
    return value


def rest_bits(size):
    out = []
    bit = 2
    while bit < size:
        out.append(bit)
        bit *= 2
    return out


def scatter_step(value, vec, size, index, bit):
    share = value.shape[0] // 2
    place = (index // bit) % 2
    cut = lambda p: lax.dynamic_slice_in_dim(value, p * share, share)
    got = dp_swap(jnp.concatenate([cut(1 - place), split_rows(vec)]), size, bit)
    return total(cut(place), got[:share]), vec + join_rows(got[share:])


def natural_bits(value, size, index):
    order = 0
    for bit in rest_bits(size):
        order = order * 2 + (index // bit) % 2
    return unxor(value.reshape(size // 2, -1, value.shape[-1]), order).reshape(value.shape)


def gather_rest(value, size):
    parts = [value]
    for stride, radix in reversed(stages(size)):
        value = jnp.concatenate(parts)
        parts = [value] + [dp_swap(value, size, o * stride) for o in range(1, radix - 1)]
        parts.append(dp_swap(value, size, (radix - 1) * stride))
    return parts


def natural_rest(value, size, index):
    order = 0
    for stride, radix in stages(size):
        order = order * radix + (index // stride) % radix
    blocks = value.reshape(size // 2, -1, value.shape[-1])
    return unxor(blocks, order).reshape(value.shape)


def scatter_side(value, side, size):
    half = value.shape[0] // 2
    send = lax.dynamic_slice_in_dim(value, (1 - side) * half, half)
    keep = lax.dynamic_slice_in_dim(value, side * half, half)
    return total(keep, dp_swap(send, size, 1))


def sum_tp(value):
    return value + sum(lax.ppermute(value, "tp", [(i, i ^ o) for i in range(4)]) for o in range(1, 4))


def body(
    size,
    tokens, cotangent, patch_rank, kept_counts, norm1_gain, norm1_shift, qkv_weight, query_bias, value_bias,
    out_weight, out_bias, router_weight, norm2_gain, norm2_shift, fc1_weight, fc1_bias, fc2_weight, fc2_bias,
):
    rows, dim = tokens.shape
    half = dim // 2
    images = patch_rank.shape[0]
    tp_index = lax.axis_index("tp")
    index = lax.axis_index("dp")
    core = tp_index % 2
    chip = tp_index // 2
    side = index % 2
    core_swap = lambda v: lax.ppermute(v, "tp", CORE_SWAP)
    y_swap = lambda v: lax.ppermute(v, "tp", Y_SWAP)
    x_swap = lambda v: dp_swap(v, size, 1)
    row_vec = lambda v: v.astype(F32).reshape(1, -1)

    width = out_weight.shape[0]
    qkv_own = jnp.transpose(qkv_weight, (1, 2, 0)).reshape(-1, dim)
    tokens_other = core_swap(tokens)
    qkv_y = y_swap(qkv_own)
    out_y = y_swap(out_weight)
    vecs = lines_call([norm1_gain, norm1_shift, out_bias, router_weight, norm2_gain, norm2_shift, fc2_bias], dim)
    small_own = lines_call([query_bias, value_bias, fc1_bias], dim)
    small_y = y_swap(small_own)

    padded = jnp.concatenate([patch_rank, jnp.full((images, SEQ - PATCHES), PATCHES, jnp.int32)], axis=1)
    live_image = (padded < kept_counts[:, None]).astype(F32)
    live_chip = lax.dynamic_slice_in_dim(live_image, chip * (images // 2), images // 2).reshape(-1, 1)
    live_own = lax.dynamic_slice_in_dim(live_chip, core * rows, rows)

    def pack(s):
        w1 = lax.dynamic_slice_in_dim(fc1_weight, s * half, half, axis=1)
        w2 = lax.dynamic_slice_in_dim(fc2_weight, s * half, half)
        return jnp.concatenate([w1, jnp.concatenate([w2[:, :half], w2[:, half:]])], axis=1)

    own_k, own_s = pack(side), pack(1 - side)
    core_line = jnp.full((1, dim), core, jnp.int32)
    normed, qkv_a, mix_a, lse_a = attend_call(
        tokens, (tokens_other, core_line, vecs), qkv_own, small_own[0:1, :width], small_own[1:2, :width], live_chip
    )
    normed, qkv_y, small_y, own_k, own_s, out_y = after(normed, qkv_y, small_y, own_k, own_s, out_y)
    out_yd = core_swap(out_y)
    y_k = y_swap(own_k)
    core_k, core_s, out_core, qkv_core = [core_swap(v) for v in (own_k, own_s, out_weight, qkv_own)]
    small_far = core_swap(jnp.stack([small_own, small_y]))

    qkv_b, mix_b, lse_b = attend_call(normed, (), qkv_y, small_y[0:1, :width], small_y[1:2, :width], live_chip)
    part = lambda v, s: lax.dynamic_slice(v, (s * rows, 0), (rows, width))
    send_mix = jnp.concatenate([part(mix_a, 1 - core), part(mix_b, 1 - core)], axis=1)
    mix_rows = jnp.concatenate([part(mix_a, core), part(mix_b, core), core_swap(send_mix)], axis=1)
    out_all = jnp.concatenate([out_weight, out_y, out_core, out_yd], axis=0)

    attn, hidden, n2, gm, sig = hidden_call(mix_rows, tokens, cotangent, live_own, out_all, vecs)
    n2, y_k, qkv_core, small_far = after(n2, y_k, qkv_core, small_far)
    y_s = x_swap(y_k)
    yd_k = core_swap(y_k)
    qkv_yd = core_swap(qkv_y)
    halves = lambda v: unxor(v[2].reshape(2, half), side)
    b_own, b_y, b_core, b_yd = halves(small_own), halves(small_y), halves(small_far[0]), halves(small_far[1])

    sums1, (dy_k, dyd_k), fb1 = ff_call(n2, gm, (y_k, yd_k), jnp.stack([b_y[0], b_yd[0]]))
    n2, dyd_k, dy_k, qkv_yd = after(n2, dyd_k, dy_k, qkv_yd)
    ryd_k = core_swap(dyd_k)
    sums2, (do_s, dc_s), fb2 = ff_call(n2, gm, (own_s, core_s), jnp.stack([b_own[1], b_core[1]]))
    n2, do_s, dc_s, ryd_k, y_s = after(n2, do_s, dc_s, ryd_k, y_s)
    rc_s = core_swap(dc_s)
    yd_s = core_swap(y_s)
    y_k_sum = total(dy_k, ryd_k)
    own_s_sum = total(do_s, rc_s)
    n2, y_k_sum, own_s_sum, yd_s = after(n2, y_k_sum, own_s_sum, yd_s)
    from_y_k = [y_swap(y_k_sum[:half])]
    from_x = [x_swap(own_s_sum[:half])]
    sums3, (dy_s, dyd_s), fb3 = ff_call(n2, gm, (y_s, yd_s), jnp.stack([b_y[1], b_yd[1]]))
    n2, dy_s, dyd_s, from_y_k[0], from_x[0] = after(n2, dy_s, dyd_s, from_y_k[0], from_x[0])
    y_k_sum, own_s_sum, n2 = after(y_k_sum, own_s_sum, n2)
    from_y_k.append(y_swap(y_k_sum[half:]))
    from_x.append(x_swap(own_s_sum[half:]))
    ryd_s = core_swap(dyd_s)
    sums4, (do_k, dc_k), fb4 = ff_call(n2, gm, (own_k, core_k), jnp.stack([b_own[0], b_core[0]]))
    sums4, do_k, dc_k, ryd_s, from_x[1], from_y_k[1] = after(sums4, do_k, dc_k, ryd_s, from_x[1], from_y_k[1])
    from_x, from_y_k = jnp.concatenate(from_x), jnp.concatenate(from_y_k)
    y_s_sum = total(dy_s, ryd_s)
    sums4, y_s_sum = after(sums4, y_s_sum)
    over_x = x_swap(y_s_sum[:half])
    over_y = y_swap(y_s_sum[half:])
    rc_k = core_swap(dc_k)

    four = (sums1, sums2, sums3, sums4)
    block_out, carry, gmix, gmix_far, d_out, d_out_far, vec2 = middle_call(
        [f[0] for f in four], [f[1] for f in four], hidden, attn, tokens, cotangent, live_own, sig, gm, mix_rows,
        out_all, vecs,
    )
    gmix, gmix_far, d_out_far, rc_k, vec2, over_x, over_y = after(
        gmix, gmix_far, d_out_far, rc_k, vec2, over_x, over_y
    )
    gmix_other = core_swap(gmix_far)
    rd_out = core_swap(d_out_far)

    join = lambda lo: jnp.where(
        core == 0,
        jnp.concatenate([gmix[:, lo : lo + width], gmix_other[:, lo : lo + width]]),
        jnp.concatenate([gmix_other[:, lo : lo + width], gmix[:, lo : lo + width]]),
    )
    gmix_a, gmix_b = join(0), join(width)
    rows_of = lambda v, s: lax.dynamic_slice_in_dim(v, s * rows, rows)

    over_xy = y_swap(over_x)
    over_yx = x_swap(over_y)
    gmix_b, rd_out = after(gmix_b, rd_out)
    d_out_half = total(d_out, rd_out)
    gmix_b, d_out_half = after(gmix_b, d_out_half)
    out_from_y = y_swap(d_out_half[width:])
    dy, gy, sy, vy = attend_back_call(qkv_b, mix_b, lse_b, gmix_b, live_chip, normed, qkv_y)
    gmix_a, dy, gy, over_xy, over_yx, out_from_y = after(gmix_a, dy, gy, over_xy, over_yx, out_from_y)
    ff_k = total(do_k, rc_k, from_y_k, from_x, jnp.concatenate([over_xy, over_yx]))
    gmix_a, ff_k = after(gmix_a, ff_k)
    ff_share = scatter_rest(ff_k, size, index)
    from_y = y_swap(dy)
    rgy = core_swap(rows_of(gy, 1 - core))

    do, go, so, vo = attend_back_call(qkv_a, mix_a, lse_a, gmix_a, live_chip, normed, qkv_own)
    do, go, so, vo, from_y, rgy, ff_share = after(do, go, so, vo, from_y, rgy, ff_share)
    ff_parts = gather_rest(ff_share, size)
    rgo = core_swap(rows_of(go, 1 - core))
    qo_own = jnp.concatenate([total(do, from_y), total(d_out_half[:width], out_from_y)])
    qo_keep = scatter_side(qo_own, side, size)
    fb_k, fb_s = jnp.stack([fb4[0], fb4[1], fb1[0], fb1[1]]), jnp.stack([fb2[0], fb2[1], fb3[0], fb3[1]])
    fb = unxor(jnp.stack([fb_k, fb_s]), side).transpose(1, 0, 2).reshape(4, dim)
    qv = lambda v: jnp.concatenate([v[0], v[2]])
    zero = jnp.zeros((2 * width,), F32)
    qv_rows = unxor(jnp.stack([qv(so), zero, qv(sy), zero]), tp_index).reshape(2, dim)
    lines = [vy + vo, vec2[:5], unxor(fb, tp_index), qv_rows, jnp.zeros((1, dim), F32)]
    ready = len(ff_parts) - 1
    lines, *early = after(jnp.concatenate(lines), *ff_parts[:ready])
    vec = sum_tp(lines)
    rgo, qo_keep, carry, vec = after(rgo, qo_keep, carry, vec)
    bits = rest_bits(size)
    ff_near = jnp.concatenate(early)
    ff_other = x_swap(ff_near)
    qo_share, vec = scatter_step(qo_keep, vec, size, index, bits[0])
    keep = lambda v: rows_of(v, core)
    input_grad = last_call(
        ((qkv_y, keep(gy)), (qkv_yd, rgy), (qkv_own, keep(go)), (qkv_core, rgo)), tokens, carry, vecs
    )
    input_grad, qo_share, vec, ff_far = after(input_grad, qo_share, vec, ff_parts[ready])
    for bit in bits[1:]:
        qo_share, vec = scatter_step(qo_share, vec, size, index, bit)
    qo_share, vec, ff_other = after(qo_share, vec, ff_other)
    qo_mine = qo_share
    for bit in reversed(bits):
        qo_mine = jnp.concatenate([qo_mine, dp_swap(qo_mine, size, bit)])
    swapped = x_swap(jnp.concatenate([ff_far, split_rows(vec)]))
    vec = vec + join_rows(swapped[ff_far.shape[0] :])
    ff_mine = jnp.concatenate([ff_near, ff_far])
    ff_other = jnp.concatenate([ff_other, swapped[: ff_far.shape[0]]])
    qo_both = unxor(jnp.stack([qo_mine, x_swap(qo_mine)]), side)
    qo_both = jax.vmap(lambda v: natural_bits(v, size, index))(qo_both).reshape(-1, dim)
    first = 3 * 128

    gain_one, shift_one = vecs[0], vecs[1]
    qv_grad = lax.dynamic_index_in_dim(vec[11:13].reshape(4, 2, width), tp_index, keepdims=False)
    fb_grad = lax.dynamic_index_in_dim(vec[:11], 7 + tp_index, keepdims=False)
    ff_both = unxor(jnp.stack([natural_rest(ff_mine, size, index), natural_rest(ff_other, size, index)]), side)
    ff_both = ff_both.astype(F32)
    fc1_grad = jnp.concatenate([ff_both[0, :, :half], ff_both[1, :, :half]], axis=1)
    second = lambda v: jnp.concatenate([v[:half, half:], v[half:, half:]], axis=1)
    fc2_grad = jnp.concatenate([second(ff_both[0]), second(ff_both[1])], axis=0)
    pair_part = qo_both[:first].reshape(3, 128, dim)
    last_part = qo_both[first : 3 * width].reshape(3, width - 128, dim)
    qkv_grad = jnp.concatenate([pair_part, last_part], axis=1).astype(F32)
    return (
        block_out,
        input_grad,
        (vec[0] - shift_one * vec[1]) / gain_one,
        vec[1],
        jnp.transpose(qkv_grad, (2, 0, 1)),
        qv_grad[0],
        qv_grad[1],
        qo_both[3 * width :].astype(F32),
        vec[4],
        vec[6],
        vec[2],
        vec[3],
        fc1_grad,
        fb_grad,
        fc2_grad,
        vec[5],
    )


def solution(mesh):
    return jax.shard_map(
        functools.partial(body, mesh.shape["dp"]),
        mesh=mesh,
        in_specs=(
            P(("dp", "tp"), None), P(("dp", "tp"), None), P("dp", None), P("dp"), P(), P(), P(None, None, "tp"),
            P("tp"), P("tp"), P("tp", None), P(), P(), P(), P(), P(None, "tp"), P("tp"), P("tp", None), P(),
        ),
        out_specs=(
            P(("dp", "tp"), None), P(("dp", "tp"), None), P(), P(), P(None, None, "tp"), P("tp"), P("tp"),
            P("tp", None), P(), P(), P(), P(), P(None, "tp"), P("tp"), P("tp", None), P(),
        ),
        check_vma=False,
    )
```

```python
import functools

import jax
import jax.numpy as jnp
from jax import lax
from jax.experimental import pallas as pl
from jax.experimental.pallas import tpu as pltpu
from jax.sharding import PartitionSpec as P

HEAD = 64
PATCHES = 577
SEQ = 592
EPS = 1e-06
F32 = jnp.float32
BF16 = jnp.bfloat16
MIB = 1024 * 1024
VMEM_BYTES = 44 * MIB
CORE_SWAP = [(0, 1), (1, 0), (2, 3), (3, 2)]
Y_SWAP = [(0, 2), (1, 3), (2, 0), (3, 1)]

NN = (((1,), (0,)), ((), ()))
NT = (((1,), (1,)), ((), ()))
TN = (((0,), (0,)), ((), ()))


def mm(left, right, dims):
    return lax.dot_general(left, right, dims, preferred_element_type=F32)


def params(size=VMEM_BYTES):
    return pltpu.CompilerParams(vmem_limit_bytes=size)


def cost(micros):
    return pl.CostEstimate(flops=int(micros * 0.11e9), bytes_accessed=int(micros * 1e5), transcendentals=0)


def whole(shape):
    rank = len(shape)
    return pl.BlockSpec(shape, lambda *ids: (0,) * rank)


def norm_parts(values):
    centre = values - jnp.mean(values, axis=-1, keepdims=True)
    inv = lax.rsqrt(jnp.mean(centre * centre, axis=-1, keepdims=True) + EPS)
    return centre * inv, inv


def split_three(column):
    high = column.astype(BF16).astype(F32)
    rest = column - high
    middle = rest.astype(BF16).astype(F32)
    return high, middle, (rest - middle).astype(BF16).astype(F32)


def pick(lane, base, columns, other):
    out = other
    for place, column in enumerate(columns):
        out = jnp.where(lane == base + place, column, out)
    return out


def lines_kernel(*refs):
    *ins, out_ref = refs
    lines = []
    for ref in ins:
        line = ref[...].astype(F32).reshape(1, -1)
        if line.shape[1] < out_ref.shape[1]:
            line = jnp.concatenate([line, jnp.zeros((1, out_ref.shape[1] - line.shape[1]), F32)], axis=1)
        lines.append(line)
    fill = jnp.zeros((out_ref.shape[0] - len(lines), out_ref.shape[1]), F32)
    out_ref[...] = jnp.concatenate(lines + [fill], axis=0)


def lines_call(vectors, dim):
    rows = -(-len(vectors) // 8) * 8
    return pl.pallas_call(
        lines_kernel,
        out_shape=jax.ShapeDtypeStruct((rows, dim), F32),
        cost_estimate=cost(1),
        name="lines",
    )(*vectors)


def attend_kernel(first, *refs):
    step = pl.program_id(0)
    if first:
        own_ref, other_ref, core_ref, vec_ref, w_ref, qb_ref, vb_ref, live_ref = refs[:8]
        normed_ref, qkv_ref, mix_ref, lse_ref = refs[8:]
        here = pl.ds(pl.multiple_of(step * SEQ, 16), SEQ)

        @pl.when(step == 0)
        def _():
            own, other = own_ref[...].astype(F32), other_ref[...].astype(F32)
            swap = core_ref[...] > 0
            blocks = [jnp.where(swap, other, own), jnp.where(swap, own, other)]
            rows = own.shape[0]
            for image in range(2 * rows // SEQ):
                pieces = []
                start, left = image * SEQ, SEQ
                while left:
                    block, at = start // rows, start % rows
                    take = min(left, rows - at)
                    pieces.append(blocks[block][at : at + take, :])
                    start, left = start + take, left - take
                x = pieces[0] if len(pieces) == 1 else jnp.concatenate(pieces, axis=0)
                scaled, _ = norm_parts(x)
                value = (scaled * vec_ref[0:1, :] + vec_ref[1:2, :]).astype(BF16)
                normed_ref[image * SEQ : (image + 1) * SEQ, :] = value

        normed = normed_ref[here, :]
    else:
        x_ref, w_ref, qb_ref, vb_ref, live_ref, qkv_ref, mix_ref, lse_ref = refs
        normed = x_ref[...]
    width = w_ref.shape[0] // 3
    rows = normed.shape[0]
    queries = (mm(normed, w_ref[:width, :], NT) + qb_ref[...]).astype(BF16)
    qkv_ref[:, :width] = (queries.astype(F32) * HEAD**-0.5).astype(BF16)
    qkv_ref[:, 256 : 256 + width] = mm(normed, w_ref[width : 2 * width, :], NT).astype(BF16)
    qkv_ref[:, 512 : 512 + width] = (mm(normed, w_ref[2 * width :, :], NT) + vb_ref[...]).astype(BF16)
    for i in range(3):
        qkv_ref[:, i * 256 + width : i * 256 + 256] = jnp.zeros((rows, 256 - width), BF16)
    lane = lax.broadcasted_iota(jnp.int32, (rows, 128), 1)
    key_bias = jnp.where(live_ref[...] > 0, 0.0, -1e30)
    lse_all = jnp.zeros((rows, 128), F32)
    heads = []
    for pair in range(2):
        base = pair * 128
        q_pair = qkv_ref[:, base : base + 128].astype(F32)
        k_pair = qkv_ref[:, 256 + base : 384 + base].astype(F32)
        v_pair = qkv_ref[:, 512 + base : 640 + base].astype(F32)
        for side in range(2 if pair == 0 else 1):
            inside = (lane >= side * 64) & (lane < side * 64 + 64)
            extra = 64 - side * 64
            q_ext = jnp.where(inside, q_pair, jnp.where(lane == extra, 1.0, 0.0)).astype(BF16)
            k_ext = jnp.where(inside, k_pair, jnp.where(lane == extra, key_bias, 0.0)).astype(BF16)
            v_own = jnp.where(inside, v_pair, 0.0).astype(BF16)
            heads.append((pair, side, mm(q_ext, k_ext, NT), v_own))
    mixed = [0.0, 0.0]
    for pair, side, scores, v_own in heads:
        top = jnp.max(scores, axis=-1, keepdims=True)
        weights = jnp.exp(scores - top)
        total = jnp.sum(weights, axis=-1, keepdims=True)
        mixed[pair] = mixed[pair] + mm(weights.astype(BF16), v_own, NN) * (1.0 / total)
        lse_all = jnp.where(lane == pair * 2 + side, top + jnp.log(total), lse_all)
    for pair in range(2):
        mix_ref[:, pair * 128 : pair * 128 + 128] = mixed[pair].astype(BF16)
    lse_ref[...] = lse_all


def attend_call(x, extras, weight, q_bias, v_bias, live_col):
    rows, dim = live_col.shape[0], x.shape[1]
    width = weight.shape[0] // 3
    block = lambda lanes: pl.BlockSpec((SEQ, lanes), lambda i: (i, 0))
    shapes = [((rows, 768), BF16), ((rows, 256), BF16), ((rows, 128), F32)]
    out_specs = [block(s[1]) for s, _ in shapes]
    kinds = [pltpu.HBM] * 3
    if extras:
        shapes = [((rows, dim), BF16)] + shapes
        kinds = [jax.ShapeDtypeStruct] + kinds
        out_specs = [whole((rows, dim))] + out_specs
    return pl.pallas_call(
        functools.partial(attend_kernel, bool(extras)),
        grid=(rows // SEQ,),
        in_specs=[whole(x.shape) if extras else block(dim)]
        + [whole(e.shape) for e in extras]
        + [whole(weight.shape), whole((1, width)), whole((1, width)), block(1)],
        out_specs=out_specs,
        out_shape=[kind(s, d) for kind, (s, d) in zip(kinds, shapes)],
        compiler_params=params(),
        cost_estimate=cost(13),
        name="attend",
    )(x, *extras, weight, q_bias, v_bias, live_col)


BLOCK = 224


def row_block(lanes):
    return pl.BlockSpec((BLOCK, lanes), lambda i: (i, 0))


def real_rows(rows):
    place = pl.program_id(0) * BLOCK + lax.broadcasted_iota(jnp.int32, (BLOCK, 1), 0)
    return place < rows


def hidden_kernel(rows, mix_ref, x_ref, cot_ref, live_ref, w_ref, vec_ref,
                  attn_ref, hidden_ref, normed_ref, gm_ref, sig_ref):
    x = x_ref[...].astype(F32)
    attention = mm(mix_ref[...], w_ref[...], NN) + vec_ref[2:3, :]
    sig = jax.nn.sigmoid(jnp.sum(x * vec_ref[3:4, :], axis=-1, keepdims=True))
    gate = live_ref[...] * sig
    hidden = x + gate * attention
    scaled, _ = norm_parts(hidden)
    real = real_rows(rows)
    attn_ref[...] = attention
    hidden_ref[...] = hidden
    normed_ref[...] = jnp.where(real, scaled * vec_ref[4:5, :] + vec_ref[5:6, :], 0.0).astype(BF16)
    gm_ref[...] = jnp.where(real, gate * cot_ref[...].astype(F32), 0.0).astype(BF16)
    sig_ref[...] = sig


def hidden_call(mix, x, cot, live_col, weight, vecs):
    rows, dim = x.shape
    steps = -(-rows // BLOCK)
    args = (mix, x, cot, live_col, weight, vecs)
    shapes = [((rows, dim), F32), ((rows, dim), F32), ((steps * BLOCK, dim), BF16), ((steps * BLOCK, dim), BF16),
              ((rows, 1), F32)]
    return pl.pallas_call(
        functools.partial(hidden_kernel, rows),
        in_specs=[row_block(a.shape[1]) for a in args[:4]] + [whole(a.shape) for a in args[4:]],
        out_specs=[row_block(s[1]) for s, _ in shapes],
        grid=(steps,),
        out_shape=[(pltpu.HBM if d == F32 and s[1] == dim else jax.ShapeDtypeStruct)(s, d) for s, d in shapes],
        compiler_params=params(),
        cost_estimate=cost(7),
        name="hidden",
    )(*args)


def ff_kernel(n2_ref, gm_ref, a_ref, b_ref, bias_ref, mlp_ref, gn2_ref, da_ref, db_ref, dbias_ref,
              w1, w2, act_all, pre_all):
    half = w1.shape[0] // 2
    for i, piece in enumerate((a_ref, b_ref)):
        at = i * half
        w1[:, at : at + half] = piece[:, :half]
        w2[at : at + half, :half] = piece[:half, half:]
        w2[at : at + half, half:] = piece[half:, half:]
    steps = 2
    size = n2_ref.shape[0] // steps
    sums = 0.0
    for step in range(steps):
        at = slice(step * size, (step + 1) * size)
        pre = mm(n2_ref[at, :], w1[...], NN) + bias_ref[...]
        grad_act = mm(gm_ref[at, :], w2[...], NT)
        cdf = 0.5 * (1.0 + lax.erf(pre * (0.5**0.5)))
        slope = cdf + pre * (jnp.exp(-0.5 * pre * pre) * (0.5 / jnp.pi) ** 0.5)
        grad_pre = (grad_act * slope).astype(BF16)
        act_all[at, :] = (pre * cdf).astype(BF16)
        pre_all[at, :] = grad_pre
        sums = sums + jnp.sum(grad_pre.astype(F32), axis=0, keepdims=True)
        mlp_ref[at, :] = mm(act_all[at, :], w2[...], NN).astype(BF16)
        gn2_ref[at, :] = mm(pre_all[at, :], w1[...], NT).astype(BF16)
    dbias_ref[...] = sums
    d2 = mm(act_all[...], gm_ref[...], TN).astype(BF16)
    d1 = mm(n2_ref[...], pre_all[...], TN).astype(BF16)
    for i, grad in enumerate((da_ref, db_ref)):
        at = i * half
        grad[:, :half] = d1[:, at : at + half]
        grad[:half, half:] = d2[at : at + half, :half]
        grad[half:, half:] = d2[at : at + half, half:]


def ff_call(n2, gm, pieces, bias):
    rows, dim = n2.shape
    tall, square, line = whole((rows, dim)), whole((dim, dim)), whole((1, dim))
    out = pl.pallas_call(
        ff_kernel,
        grid=(1,),
        in_specs=[tall, tall, square, square, line],
        out_specs=[tall, tall, square, square, line],
        out_shape=[pltpu.HBM((rows, dim), BF16)] * 2
        + [pltpu.HBM((dim, dim), BF16)] * 2
        + [jax.ShapeDtypeStruct((1, dim), F32)],
        scratch_shapes=[pltpu.VMEM((dim, dim), BF16)] * 2 + [pltpu.VMEM((rows, dim), BF16)] * 2,
        compiler_params=params(),
        cost_estimate=cost(12),
        name="feed",
    )(n2, gm, *pieces, bias.reshape(1, dim))
    return out[:2], out[2:4], out[4].reshape(2, dim // 2)


def middle_kernel(rows, parts, *refs):
    mlp_refs, gn2_refs = refs[:parts], refs[parts : 2 * parts]
    (hidden_ref, attn_ref, x_ref, cot_ref, live_ref, sig_ref, gm_ref, mix_ref, w_ref, vec_ref,
     block_ref, carry_ref, near_ref, far_ref, dw_near_ref, dw_far_ref, sum_ref, acc_ref) = refs[2 * parts :]
    step = pl.program_id(0)
    real = real_rows(rows)
    x = x_ref[...].astype(F32)
    cot = cot_ref[...].astype(F32)
    sig = sig_ref[...]
    gate = live_ref[...] * sig
    hidden = hidden_ref[...]
    mlp = vec_ref[6:7, :]
    gn2 = 0.0
    for ref in mlp_refs:
        mlp = mlp + ref[...].astype(F32)
    for ref in gn2_refs:
        gn2 = gn2 + ref[...].astype(F32)
    block_ref[...] = (hidden + gate * mlp).astype(BF16)
    scaled, inv = norm_parts(hidden)
    e = gn2 * vec_ref[4:5, :]
    grad_hidden = cot + inv * (
        e - jnp.mean(e, axis=-1, keepdims=True) - scaled * jnp.mean(e * scaled, axis=-1, keepdims=True)
    )
    gate_grad = jnp.sum(grad_hidden * attn_ref[...] + cot * mlp, axis=-1, keepdims=True)
    logit = live_ref[...] * gate_grad * sig * (1.0 - sig)
    carry_ref[...] = grad_hidden + logit * vec_ref[3:4, :]
    grad_attn = jnp.where(real, gate * grad_hidden, 0.0).astype(BF16)
    half = near_ref.shape[1]
    near_ref[...] = mm(grad_attn, w_ref[:half, :], NT).astype(BF16)
    far_ref[...] = mm(grad_attn, w_ref[half:, :], NT).astype(BF16)
    mix = jnp.where(real, mix_ref[...].astype(F32), 0.0).astype(BF16)
    update = mm(mix, grad_attn, TN)
    add = lambda v: jnp.sum(jnp.where(real, v, 0.0), axis=0, keepdims=True)
    sums = jnp.concatenate(
        [add(gn2 * scaled), add(gn2), add(grad_attn.astype(F32)), add(gm_ref[...].astype(F32)), add(x * logit),
         jnp.zeros((3, x.shape[1]), F32)], axis=0)

    @pl.when(step == 0)
    def _():
        acc_ref[...] = update
        sum_ref[...] = sums

    @pl.when(step > 0)
    def _():
        acc_ref[...] += update
        sum_ref[...] += sums

    @pl.when(step == pl.num_programs(0) - 1)
    def _():
        dw_near_ref[...] = acc_ref[:half, :].astype(BF16)
        dw_far_ref[...] = acc_ref[half:, :].astype(BF16)


def middle_call(mlp, gn2, *args):
    x, weight, vecs = args[2], args[8], args[9]
    rows, dim = x.shape
    half = dim // 2
    shapes = [((rows, dim), BF16), ((rows, dim), F32), ((rows, half), BF16), ((rows, half), BF16)]
    ins = (*mlp, *gn2, *args)
    return pl.pallas_call(
        functools.partial(middle_kernel, rows, len(mlp)),
        in_specs=[row_block(a.shape[1]) for a in ins[:-2]] + [whole(weight.shape), whole(vecs.shape)],
        out_specs=[row_block(s[1]) for s, _ in shapes] + [whole((half, dim))] * 2 + [whole((8, dim))],
        grid=(-(-rows // BLOCK),),
        out_shape=[pltpu.HBM(s, d) for s, d in shapes]
        + [pltpu.HBM((half, dim), BF16)] * 2
        + [jax.ShapeDtypeStruct((8, dim), F32)],
        scratch_shapes=[pltpu.VMEM((dim, dim), F32)],
        compiler_params=params(60 * MIB),
        cost_estimate=cost(11),
        name="middle",
    )(*ins)


def attend_back_kernel(*refs):
    qkv_ref, mix_ref, lse_ref, gmix_ref, live_ref, normed_ref, w_ref, dw_ref, gp_ref, bias_ref, vec_ref, gp_all = refs
    rows = qkv_ref.shape[0]
    third = w_ref.shape[0] // 3
    step = pl.program_id(0)
    lane = lax.broadcasted_iota(jnp.int32, (rows, 128), 1)
    key_bias = jnp.where(live_ref[...] > 0, 0.0, -1e30)
    lse_all = lse_ref[...]
    one = jnp.ones((rows, 1), F32)
    sums = []
    start = 0
    for pair in range(2):
        base = pair * 128
        width = min(128, third - base)
        q_pair = qkv_ref[:, base : base + 128].astype(F32)
        k_pair = qkv_ref[:, 256 + base : 384 + base].astype(F32)
        v_pair = qkv_ref[:, 512 + base : 640 + base].astype(F32)
        m_pair = mix_ref[:, base : base + 128].astype(F32)
        g_pair = gmix_ref[:, base : base + width].astype(F32)
        if width < 128:
            g_pair = jnp.concatenate([g_pair, jnp.zeros((rows, 128 - width), F32)], axis=1)
        gq = jnp.zeros((rows, 128), F32)
        gk = jnp.zeros((rows, 128), F32)
        gv = jnp.zeros((rows, 128), F32)
        for side in range(width // 64):
            inside = (lane >= side * 64) & (lane < side * 64 + 64)
            extra = 64 - side * 64
            lse = jnp.sum(jnp.where(lane == pair * 2 + side, lse_all, 0.0), axis=-1, keepdims=True)
            delta = jnp.sum(jnp.where(inside, g_pair * m_pair, 0.0), axis=-1, keepdims=True)
            l0, l1, l2 = split_three(lse)
            d0, d1, d2 = split_three(delta)
            q_ext = jnp.where(inside, q_pair, pick(lane, extra, (-l0, -l1, -l2, one), 0.0)).astype(BF16)
            k_ext = jnp.where(inside, k_pair, pick(lane, extra, (one, one, one, key_bias), 0.0)).astype(BF16)
            g_ext = jnp.where(inside, g_pair, pick(lane, extra, (-d0, -d1, -d2), 0.0)).astype(BF16)
            v_ext = jnp.where(inside, v_pair, pick(lane, extra, (one, one, one), 0.0)).astype(BF16)
            q_own = jnp.where(inside, q_pair, 0.0).astype(BF16)
            k_own = jnp.where(inside, k_pair, 0.0).astype(BF16)
            g_own = jnp.where(inside, g_pair, 0.0).astype(BF16)
            probs = jnp.exp(mm(k_ext, q_ext, NT))
            grad_scores = (probs * mm(v_ext, g_ext, NT)).astype(BF16)
            gv = gv + mm(probs.astype(BF16), g_own, NN)
            gk = gk + mm(grad_scores, q_own, NN)
            gq = gq + mm(grad_scores, k_own, TN)
        line = []
        for grad in (gq * HEAD**-0.5, gk, gv):
            piece = grad.astype(BF16)[:, :width]
            gp_ref[:, start : start + width] = piece
            line.append(jnp.sum(piece.astype(F32), axis=0, keepdims=True))
            start += width
        sums.append(jnp.concatenate(line, axis=0))
    gp_ref[:, start:] = jnp.zeros((rows, gp_ref.shape[1] - start), BF16)
    gp_all[pl.ds(pl.multiple_of(step * rows, 16), rows), :] = gp_ref[...]
    sums = jnp.concatenate(sums, axis=1)

    @pl.when(step == 0)
    def _():
        bias_ref[...] = sums

    @pl.when(step > 0)
    def _():
        bias_ref[...] += sums

    @pl.when(step == pl.num_programs(0) - 1)
    def _():
        update = mm(gp_all[...], normed_ref[...], TN)[: w_ref.shape[0], :]
        dw_ref[...] = update.astype(BF16)
        column = jnp.zeros((1, w_ref.shape[1]), F32)
        product = jnp.zeros((1, w_ref.shape[1]), F32)
        for part in range(3):
            terms = jnp.concatenate(split_three(bias_ref[part : part + 1, :]), axis=0).astype(BF16)
            rows_w = w_ref[part * third : (part + 1) * third, :]
            column = column + jnp.sum(mm(terms, rows_w, NN), axis=0, keepdims=True)
            lone = third - 128
            pair_rows = update[part * 128 : part * 128 + 128, :]
            lone_rows = update[3 * 128 + part * lone : 3 * 128 + (part + 1) * lone, :]
            own = jnp.concatenate([pair_rows, lone_rows], axis=0) * rows_w.astype(F32)
            product = product + jnp.sum(own, axis=0, keepdims=True)
        vec_ref[0:1, :] = product
        vec_ref[1:2, :] = column


def attend_back_call(qkv, mix, lse, gmix, live_col, normed, weight):
    rows, dim = normed.shape
    height = weight.shape[0]
    columns = -(-height // 128) * 128
    block = lambda lanes: pl.BlockSpec((SEQ, lanes), lambda i: (i, 0))
    ins = [qkv, mix, lse, gmix, live_col, normed, weight]
    return pl.pallas_call(
        attend_back_kernel,
        grid=(rows // SEQ,),
        in_specs=[block(a.shape[1]) for a in ins[:5]] + [whole(normed.shape), whole(weight.shape)],
        out_specs=[whole((height, dim)), block(columns), whole((3, height // 3)), whole((2, dim))],
        out_shape=[
            pltpu.HBM((height, dim), BF16),
            pltpu.HBM((rows, columns), BF16),
            jax.ShapeDtypeStruct((3, height // 3), F32),
            jax.ShapeDtypeStruct((2, dim), F32),
        ],
        scratch_shapes=[pltpu.VMEM((rows, columns), BF16)],
        compiler_params=params(),
        cost_estimate=cost(21),
        name="attend_back",
    )(*ins)


def last_kernel(groups, *refs):
    gp_refs, w_refs = refs[:groups], refs[groups : 2 * groups]
    x_ref, carry_ref, vec_ref, grad_ref = refs[2 * groups : 2 * groups + 4]
    scratch = refs[2 * groups + 4 :]

    @pl.when(pl.program_id(0) == 0)
    def _():
        for w_ref, to_ref in zip(w_refs, scratch):
            third = w_ref.shape[0] // 3
            start = 0
            base = 0
            for size in (128, third - 128):
                for part in range(3):
                    to_ref[start : start + size, :] = w_ref[part * third + base : part * third + base + size, :]
                    start += size
                base += size
            to_ref[start:, :] = jnp.zeros((to_ref.shape[0] - start, to_ref.shape[1]), BF16)

    gn = 0.0
    for gp_ref, to_ref in zip(gp_refs, scratch):
        gn = gn + mm(gp_ref[...], to_ref[...], NN)
    scaled, inv = norm_parts(x_ref[...].astype(F32))
    f = gn * vec_ref[0:1, :]
    grad_ref[...] = carry_ref[...] + inv * (
        f - jnp.mean(f, axis=-1, keepdims=True) - scaled * jnp.mean(f * scaled, axis=-1, keepdims=True)
    )


def last_call(groups, x, carry, vecs):
    rows, dim = x.shape
    gps = [g for _, g in groups]
    weights = [w for w, _ in groups]
    return pl.pallas_call(
        functools.partial(last_kernel, len(groups)),
        in_specs=[row_block(g.shape[1]) for g in gps]
        + [whole(w.shape) for w in weights]
        + [row_block(dim), row_block(dim), whole(vecs.shape)],
        out_specs=row_block(dim),
        grid=(-(-rows // BLOCK),),
        out_shape=jax.ShapeDtypeStruct((rows, dim), F32),
        scratch_shapes=[pltpu.VMEM((g.shape[1], dim), BF16) for g in gps],
        compiler_params=params(60 * MIB),
        cost_estimate=cost(9),
        name="last",
    )(*gps, *weights, x, carry, vecs)


def total(*terms):
    out = terms[0].astype(F32)
    for term in terms[1:]:
        out = out + term.astype(F32)
    return out.astype(BF16)


def after(first, *rest):
    return lax.optimization_barrier((first, *rest))


def unxor(value, index):
    count = value.shape[0]
    bit = 1
    while bit < count:
        split = value.reshape(count // (2 * bit), 2, bit, *value.shape[1:])
        value = jnp.where((index // bit) % 2 == 1, jnp.flip(split, 1), split).reshape(value.shape)
        bit *= 2
    return value


def stages(size):
    out = []
    stride = 2
    while stride < size:
        radix = 4 if size % (stride * 4) == 0 else 2
        out.append((stride, radix))
        stride *= radix
    return out


def dp_swap(value, size, offset):
    return lax.ppermute(value, "dp", [(i, i ^ offset) for i in range(size)])


def split_rows(value):
    high = value.astype(BF16)
    return jnp.concatenate([high, (value[:2] - high[:2].astype(F32)).astype(BF16)])


def join_rows(value):
    value = value.astype(F32)
    return jnp.concatenate([value[:2] + value[-2:], value[2:-2]])


def scatter_rest(value, size, index):
    for stride, radix in stages(size):
        digit = (index // stride) % radix
        share = value.shape[0] // radix
        cut = lambda o: lax.dynamic_slice_in_dim(value, (digit ^ o) * share, share)
        value = total(cut(0), *[dp_swap(cut(o), size, o * stride) for o in range(1, radix)])
    return value


def rest_bits(size):
    out = []
    bit = 2
    while bit < size:
        out.append(bit)
        bit *= 2
    return out


def scatter_step(value, vec, size, index, bit):
    share = value.shape[0] // 2
    place = (index // bit) % 2
    cut = lambda p: lax.dynamic_slice_in_dim(value, p * share, share)
    got = dp_swap(jnp.concatenate([cut(1 - place), split_rows(vec)]), size, bit)
    return total(cut(place), got[:share]), vec + join_rows(got[share:])


def natural_bits(value, size, index):
    order = 0
    for bit in rest_bits(size):
        order = order * 2 + (index // bit) % 2
    return unxor(value.reshape(size // 2, -1, value.shape[-1]), order).reshape(value.shape)


def gather_rest(value, size):
    parts = [value]
    for stride, radix in reversed(stages(size)):
        value = jnp.concatenate(parts)
        parts = [value] + [dp_swap(value, size, o * stride) for o in range(1, radix - 1)]
        parts.append(dp_swap(value, size, (radix - 1) * stride))
    return parts


def natural_rest(value, size, index):
    order = 0
    for stride, radix in stages(size):
        order = order * radix + (index // stride) % radix
    blocks = value.reshape(size // 2, -1, value.shape[-1])
    return unxor(blocks, order).reshape(value.shape)


def scatter_side(value, side, size):
    half = value.shape[0] // 2
    send = lax.dynamic_slice_in_dim(value, (1 - side) * half, half)
    keep = lax.dynamic_slice_in_dim(value, side * half, half)
    return total(keep, dp_swap(send, size, 1))


def sum_tp(value):
    return value + sum(lax.ppermute(value, "tp", [(i, i ^ o) for i in range(4)]) for o in range(1, 4))


def body(
    size,
    tokens, cotangent, patch_rank, kept_counts, norm1_gain, norm1_shift, qkv_weight, query_bias, value_bias,
    out_weight, out_bias, router_weight, norm2_gain, norm2_shift, fc1_weight, fc1_bias, fc2_weight, fc2_bias,
):
    rows, dim = tokens.shape
    half = dim // 2
    images = patch_rank.shape[0]
    tp_index = lax.axis_index("tp")
    index = lax.axis_index("dp")
    core = tp_index % 2
    chip = tp_index // 2
    side = index % 2
    core_swap = lambda v: lax.ppermute(v, "tp", CORE_SWAP)
    y_swap = lambda v: lax.ppermute(v, "tp", Y_SWAP)
    x_swap = lambda v: dp_swap(v, size, 1)
    row_vec = lambda v: v.astype(F32).reshape(1, -1)

    width = out_weight.shape[0]
    qkv_own = jnp.transpose(qkv_weight, (1, 2, 0)).reshape(-1, dim)
    tokens_other = core_swap(tokens)
    qkv_y = y_swap(qkv_own)
    out_y = y_swap(out_weight)
    vecs = lines_call([norm1_gain, norm1_shift, out_bias, router_weight, norm2_gain, norm2_shift, fc2_bias], dim)
    small_own = lines_call([query_bias, value_bias, fc1_bias], dim)
    small_y = y_swap(small_own)

    padded = jnp.concatenate([patch_rank, jnp.full((images, SEQ - PATCHES), PATCHES, jnp.int32)], axis=1)
    live_image = (padded < kept_counts[:, None]).astype(F32)
    live_chip = lax.dynamic_slice_in_dim(live_image, chip * (images // 2), images // 2).reshape(-1, 1)
    live_own = lax.dynamic_slice_in_dim(live_chip, core * rows, rows)

    def pack(s):
        w1 = lax.dynamic_slice_in_dim(fc1_weight, s * half, half, axis=1)
        w2 = lax.dynamic_slice_in_dim(fc2_weight, s * half, half)
        return jnp.concatenate([w1, jnp.concatenate([w2[:, :half], w2[:, half:]])], axis=1)

    own_k, own_s = pack(side), pack(1 - side)
    core_line = jnp.full((1, dim), core, jnp.int32)
    normed, qkv_a, mix_a, lse_a = attend_call(
        tokens, (tokens_other, core_line, vecs), qkv_own, small_own[0:1, :width], small_own[1:2, :width], live_chip
    )
    normed, qkv_y, small_y, own_k, own_s, out_y = after(normed, qkv_y, small_y, own_k, own_s, out_y)
    out_yd = core_swap(out_y)
    y_k = y_swap(own_k)
    core_k, core_s, out_core, qkv_core = [core_swap(v) for v in (own_k, own_s, out_weight, qkv_own)]
    small_far = core_swap(jnp.stack([small_own, small_y]))

    qkv_b, mix_b, lse_b = attend_call(normed, (), qkv_y, small_y[0:1, :width], small_y[1:2, :width], live_chip)
    part = lambda v, s: lax.dynamic_slice(v, (s * rows, 0), (rows, width))
    send_mix = jnp.concatenate([part(mix_a, 1 - core), part(mix_b, 1 - core)], axis=1)
    mix_rows = jnp.concatenate([part(mix_a, core), part(mix_b, core), core_swap(send_mix)], axis=1)
    out_all = jnp.concatenate([out_weight, out_y, out_core, out_yd], axis=0)

    attn, hidden, n2, gm, sig = hidden_call(mix_rows, tokens, cotangent, live_own, out_all, vecs)
    n2, y_k, qkv_core, small_far = after(n2, y_k, qkv_core, small_far)
    y_s = x_swap(y_k)
    yd_k = core_swap(y_k)
    qkv_yd = core_swap(qkv_y)
    halves = lambda v: unxor(v[2].reshape(2, half), side)
    b_own, b_y, b_core, b_yd = halves(small_own), halves(small_y), halves(small_far[0]), halves(small_far[1])

    sums1, (dy_k, dyd_k), fb1 = ff_call(n2, gm, (y_k, yd_k), jnp.stack([b_y[0], b_yd[0]]))
    n2, dyd_k, dy_k, qkv_yd = after(n2, dyd_k, dy_k, qkv_yd)
    ryd_k = core_swap(dyd_k)
    sums2, (do_s, dc_s), fb2 = ff_call(n2, gm, (own_s, core_s), jnp.stack([b_own[1], b_core[1]]))
    n2, do_s, dc_s, ryd_k, y_s = after(n2, do_s, dc_s, ryd_k, y_s)
    rc_s = core_swap(dc_s)
    yd_s = core_swap(y_s)
    y_k_sum = total(dy_k, ryd_k)
    own_s_sum = total(do_s, rc_s)
    n2, y_k_sum, own_s_sum, yd_s = after(n2, y_k_sum, own_s_sum, yd_s)
    from_y_k = [y_swap(y_k_sum[:half])]
    from_x = [x_swap(own_s_sum[:half])]
    sums3, (dy_s, dyd_s), fb3 = ff_call(n2, gm, (y_s, yd_s), jnp.stack([b_y[1], b_yd[1]]))
    n2, dy_s, dyd_s, from_y_k[0], from_x[0] = after(n2, dy_s, dyd_s, from_y_k[0], from_x[0])
    y_k_sum, own_s_sum, n2 = after(y_k_sum, own_s_sum, n2)
    from_y_k.append(y_swap(y_k_sum[half:]))
    from_x.append(x_swap(own_s_sum[half:]))
    ryd_s = core_swap(dyd_s)
    sums4, (do_k, dc_k), fb4 = ff_call(n2, gm, (own_k, core_k), jnp.stack([b_own[0], b_core[0]]))
    sums4, do_k, dc_k, ryd_s, from_x[1], from_y_k[1] = after(sums4, do_k, dc_k, ryd_s, from_x[1], from_y_k[1])
    from_x, from_y_k = jnp.concatenate(from_x), jnp.concatenate(from_y_k)
    y_s_sum = total(dy_s, ryd_s)
    sums4, y_s_sum = after(sums4, y_s_sum)
    over_x = x_swap(y_s_sum[:half])
    over_y = y_swap(y_s_sum[half:])
    rc_k = core_swap(dc_k)

    four = (sums1, sums2, sums3, sums4)
    block_out, carry, gmix, gmix_far, d_out, d_out_far, vec2 = middle_call(
        [f[0] for f in four], [f[1] for f in four], hidden, attn, tokens, cotangent, live_own, sig, gm, mix_rows,
        out_all, vecs,
    )
    gmix, gmix_far, d_out_far, rc_k, vec2, over_x, over_y = after(
        gmix, gmix_far, d_out_far, rc_k, vec2, over_x, over_y
    )
    gmix_other = core_swap(gmix_far)
    rd_out = core_swap(d_out_far)

    join = lambda lo: jnp.where(
        core == 0,
        jnp.concatenate([gmix[:, lo : lo + width], gmix_other[:, lo : lo + width]]),
        jnp.concatenate([gmix_other[:, lo : lo + width], gmix[:, lo : lo + width]]),
    )
    gmix_a, gmix_b = after(join(0), join(width))
    rows_of = lambda v, s: lax.dynamic_slice_in_dim(v, s * rows, rows)

    over_xy = y_swap(over_x)
    over_yx = x_swap(over_y)
    gmix_b, rd_out = after(gmix_b, rd_out)
    d_out_half = total(d_out, rd_out)
    gmix_b, d_out_half = after(gmix_b, d_out_half)
    out_from_y = y_swap(d_out_half[width:])
    dy, gy, sy, vy = attend_back_call(qkv_b, mix_b, lse_b, gmix_b, live_chip, normed, qkv_y)
    gmix_a, dy, gy, over_xy, over_yx, out_from_y = after(gmix_a, dy, gy, over_xy, over_yx, out_from_y)
    ff_k = total(do_k, rc_k, from_y_k, from_x, jnp.concatenate([over_xy, over_yx]))
    gmix_a, ff_k = after(gmix_a, ff_k)
    ff_share = scatter_rest(ff_k, size, index)
    from_y = y_swap(dy)
    rgy = core_swap(rows_of(gy, 1 - core))

    do, go, so, vo = attend_back_call(qkv_a, mix_a, lse_a, gmix_a, live_chip, normed, qkv_own)
    do, go, so, vo, from_y, rgy, ff_share = after(do, go, so, vo, from_y, rgy, ff_share)
    ff_parts = gather_rest(ff_share, size)
    rgo = core_swap(rows_of(go, 1 - core))
    qo_own = jnp.concatenate([total(do, from_y), total(d_out_half[:width], out_from_y)])
    qo_keep = scatter_side(qo_own, side, size)
    fb_k, fb_s = jnp.stack([fb4[0], fb4[1], fb1[0], fb1[1]]), jnp.stack([fb2[0], fb2[1], fb3[0], fb3[1]])
    fb = unxor(jnp.stack([fb_k, fb_s]), side).transpose(1, 0, 2).reshape(4, dim)
    qv = lambda v: jnp.concatenate([v[0], v[2]])
    zero = jnp.zeros((2 * width,), F32)
    qv_rows = unxor(jnp.stack([qv(so), zero, qv(sy), zero]), tp_index).reshape(2, dim)
    lines = [vy + vo, vec2[:5], unxor(fb, tp_index), qv_rows, jnp.zeros((1, dim), F32)]
    ready = len(ff_parts) - 1
    lines, *early = after(jnp.concatenate(lines), *ff_parts[:ready])
    vec = sum_tp(lines)
    rgo, qo_keep, carry, vec = after(rgo, qo_keep, carry, vec)
    bits = rest_bits(size)
    ff_near = jnp.concatenate(early)
    ff_other = x_swap(ff_near)
    qo_share, vec = scatter_step(qo_keep, vec, size, index, bits[0])
    keep = lambda v: rows_of(v, core)
    input_grad = last_call(
        ((qkv_y, keep(gy)), (qkv_yd, rgy), (qkv_own, keep(go)), (qkv_core, rgo)), tokens, carry, vecs
    )
    input_grad, qo_share, vec, ff_far = after(input_grad, qo_share, vec, ff_parts[ready])
    for bit in bits[1:]:
        qo_share, vec = scatter_step(qo_share, vec, size, index, bit)
    qo_share, vec, ff_other = after(qo_share, vec, ff_other)
    qo_mine = qo_share
    for bit in reversed(bits):
        qo_mine = jnp.concatenate([qo_mine, dp_swap(qo_mine, size, bit)])
    swapped = x_swap(jnp.concatenate([ff_far, split_rows(vec)]))
    vec = vec + join_rows(swapped[ff_far.shape[0] :])
    ff_mine = jnp.concatenate([ff_near, ff_far])
    ff_other = jnp.concatenate([ff_other, swapped[: ff_far.shape[0]]])
    qo_both = unxor(jnp.stack([qo_mine, x_swap(qo_mine)]), side)
    qo_both = jax.vmap(lambda v: natural_bits(v, size, index))(qo_both).reshape(-1, dim)
    first = 3 * 128

    gain_one, shift_one = vecs[0], vecs[1]
    qv_grad = lax.dynamic_index_in_dim(vec[11:13].reshape(4, 2, width), tp_index, keepdims=False)
    fb_grad = lax.dynamic_index_in_dim(vec[:11], 7 + tp_index, keepdims=False)
    ff_both = unxor(jnp.stack([natural_rest(ff_mine, size, index), natural_rest(ff_other, size, index)]), side)
    ff_both = ff_both.astype(F32)
    fc1_grad = jnp.concatenate([ff_both[0, :, :half], ff_both[1, :, :half]], axis=1)
    second = lambda v: jnp.concatenate([v[:half, half:], v[half:, half:]], axis=1)
    fc2_grad = jnp.concatenate([second(ff_both[0]), second(ff_both[1])], axis=0)
    pair_part = qo_both[:first].reshape(3, 128, dim)
    last_part = qo_both[first : 3 * width].reshape(3, width - 128, dim)
    qkv_grad = jnp.concatenate([pair_part, last_part], axis=1).astype(F32)
    return (
        block_out,
        input_grad,
        (vec[0] - shift_one * vec[1]) / gain_one,
        vec[1],
        jnp.transpose(qkv_grad, (2, 0, 1)),
        qv_grad[0],
        qv_grad[1],
        qo_both[3 * width :].astype(F32),
        vec[4],
        vec[6],
        vec[2],
        vec[3],
        fc1_grad,
        fb_grad,
        fc2_grad,
        vec[5],
    )


def solution(mesh):
    return jax.shard_map(
        functools.partial(body, mesh.shape["dp"]),
        mesh=mesh,
        in_specs=(
            P(("dp", "tp"), None), P(("dp", "tp"), None), P("dp", None), P("dp"), P(), P(), P(None, None, "tp"),
            P("tp"), P("tp"), P("tp", None), P(), P(), P(), P(), P(None, "tp"), P("tp"), P("tp", None), P(),
        ),
        out_specs=(
            P(("dp", "tp"), None), P(("dp", "tp"), None), P(), P(), P(None, None, "tp"), P("tp"), P("tp"),
            P("tp", None), P(), P(), P(), P(), P(None, "tp"), P("tp"), P("tp", None), P(),
        ),
        check_vma=False,
    )
```

```python
import functools

import jax
import jax.numpy as jnp
from jax import lax
from jax.experimental import pallas as pl
from jax.experimental.pallas import tpu as pltpu
from jax.sharding import PartitionSpec as P

HEAD = 64
PATCHES = 577
SEQ = 592
EPS = 1e-06
F32 = jnp.float32
BF16 = jnp.bfloat16
MIB = 1024 * 1024
VMEM_BYTES = 44 * MIB
CORE_SWAP = [(0, 1), (1, 0), (2, 3), (3, 2)]
Y_SWAP = [(0, 2), (1, 3), (2, 0), (3, 1)]

NN = (((1,), (0,)), ((), ()))
NT = (((1,), (1,)), ((), ()))
TN = (((0,), (0,)), ((), ()))


def mm(left, right, dims):
    return lax.dot_general(left, right, dims, preferred_element_type=F32)


def params(size=VMEM_BYTES):
    return pltpu.CompilerParams(vmem_limit_bytes=size)


def cost(micros):
    return pl.CostEstimate(flops=int(micros * 0.11e9), bytes_accessed=int(micros * 1e5), transcendentals=0)


def whole(shape):
    rank = len(shape)
    return pl.BlockSpec(shape, lambda *ids: (0,) * rank)


def norm_parts(values):
    centre = values - jnp.mean(values, axis=-1, keepdims=True)
    inv = lax.rsqrt(jnp.mean(centre * centre, axis=-1, keepdims=True) + EPS)
    return centre * inv, inv


def split_three(column):
    high = column.astype(BF16).astype(F32)
    rest = column - high
    middle = rest.astype(BF16).astype(F32)
    return high, middle, (rest - middle).astype(BF16).astype(F32)


def pick(lane, base, columns, other):
    out = other
    for place, column in enumerate(columns):
        out = jnp.where(lane == base + place, column, out)
    return out


def lines_kernel(*refs):
    *ins, out_ref = refs
    lines = []
    for ref in ins:
        line = ref[...].astype(F32).reshape(1, -1)
        if line.shape[1] < out_ref.shape[1]:
            line = jnp.concatenate([line, jnp.zeros((1, out_ref.shape[1] - line.shape[1]), F32)], axis=1)
        lines.append(line)
    fill = jnp.zeros((out_ref.shape[0] - len(lines), out_ref.shape[1]), F32)
    out_ref[...] = jnp.concatenate(lines + [fill], axis=0)


def lines_call(vectors, dim):
    rows = -(-len(vectors) // 8) * 8
    return pl.pallas_call(
        lines_kernel,
        out_shape=jax.ShapeDtypeStruct((rows, dim), F32),
        cost_estimate=cost(1),
        name="lines",
    )(*vectors)


def attend_kernel(first, *refs):
    step = pl.program_id(0)
    if first:
        own_ref, other_ref, core_ref, vec_ref, w_ref, qb_ref, vb_ref, live_ref = refs[:8]
        normed_ref, qkv_ref, mix_ref, lse_ref = refs[8:]
        here = pl.ds(pl.multiple_of(step * SEQ, 16), SEQ)

        @pl.when(step == 0)
        def _():
            own, other = own_ref[...].astype(F32), other_ref[...].astype(F32)
            swap = core_ref[...] > 0
            blocks = [jnp.where(swap, other, own), jnp.where(swap, own, other)]
            rows = own.shape[0]
            for image in range(2 * rows // SEQ):
                pieces = []
                start, left = image * SEQ, SEQ
                while left:
                    block, at = start // rows, start % rows
                    take = min(left, rows - at)
                    pieces.append(blocks[block][at : at + take, :])
                    start, left = start + take, left - take
                x = pieces[0] if len(pieces) == 1 else jnp.concatenate(pieces, axis=0)
                scaled, _ = norm_parts(x)
                value = (scaled * vec_ref[0:1, :] + vec_ref[1:2, :]).astype(BF16)
                normed_ref[image * SEQ : (image + 1) * SEQ, :] = value

        normed = normed_ref[here, :]
    else:
        x_ref, w_ref, qb_ref, vb_ref, live_ref, qkv_ref, mix_ref, lse_ref = refs
        normed = x_ref[...]
    width = w_ref.shape[0] // 3
    rows = normed.shape[0]
    queries = (mm(normed, w_ref[:width, :], NT) + qb_ref[...]).astype(BF16)
    qkv_ref[:, :width] = (queries.astype(F32) * HEAD**-0.5).astype(BF16)
    qkv_ref[:, 256 : 256 + width] = mm(normed, w_ref[width : 2 * width, :], NT).astype(BF16)
    qkv_ref[:, 512 : 512 + width] = (mm(normed, w_ref[2 * width :, :], NT) + vb_ref[...]).astype(BF16)
    for i in range(3):
        qkv_ref[:, i * 256 + width : i * 256 + 256] = jnp.zeros((rows, 256 - width), BF16)
    lane = lax.broadcasted_iota(jnp.int32, (rows, 128), 1)
    key_bias = jnp.where(live_ref[...] > 0, 0.0, -1e30)
    lse_all = jnp.zeros((rows, 128), F32)
    heads = []
    for pair in range(2):
        base = pair * 128
        q_pair = qkv_ref[:, base : base + 128].astype(F32)
        k_pair = qkv_ref[:, 256 + base : 384 + base].astype(F32)
        v_pair = qkv_ref[:, 512 + base : 640 + base].astype(F32)
        for side in range(2 if pair == 0 else 1):
            inside = (lane >= side * 64) & (lane < side * 64 + 64)
            extra = 64 - side * 64
            q_ext = jnp.where(inside, q_pair, jnp.where(lane == extra, 1.0, 0.0)).astype(BF16)
            k_ext = jnp.where(inside, k_pair, jnp.where(lane == extra, key_bias, 0.0)).astype(BF16)
            v_own = jnp.where(inside, v_pair, 0.0).astype(BF16)
            heads.append((pair, side, mm(q_ext, k_ext, NT), v_own))
    mixed = [0.0, 0.0]
    for pair, side, scores, v_own in heads:
        top = jnp.max(scores, axis=-1, keepdims=True)
        weights = jnp.exp(scores - top)
        total = jnp.sum(weights, axis=-1, keepdims=True)
        mixed[pair] = mixed[pair] + mm(weights.astype(BF16), v_own, NN) * (1.0 / total)
        lse_all = jnp.where(lane == pair * 2 + side, top + jnp.log(total), lse_all)
    for pair in range(2):
        mix_ref[:, pair * 128 : pair * 128 + 128] = mixed[pair].astype(BF16)
    lse_ref[...] = lse_all


def attend_call(x, extras, weight, q_bias, v_bias, live_col):
    rows, dim = live_col.shape[0], x.shape[1]
    width = weight.shape[0] // 3
    block = lambda lanes: pl.BlockSpec((SEQ, lanes), lambda i: (i, 0))
    shapes = [((rows, 768), BF16), ((rows, 256), BF16), ((rows, 128), F32)]
    out_specs = [block(s[1]) for s, _ in shapes]
    kinds = [pltpu.HBM] * 3
    if extras:
        shapes = [((rows, dim), BF16)] + shapes
        kinds = [jax.ShapeDtypeStruct] + kinds
        out_specs = [whole((rows, dim))] + out_specs
    return pl.pallas_call(
        functools.partial(attend_kernel, bool(extras)),
        grid=(rows // SEQ,),
        in_specs=[whole(x.shape) if extras else block(dim)]
        + [whole(e.shape) for e in extras]
        + [whole(weight.shape), whole((1, width)), whole((1, width)), block(1)],
        out_specs=out_specs,
        out_shape=[kind(s, d) for kind, (s, d) in zip(kinds, shapes)],
        compiler_params=params(),
        cost_estimate=cost(13),
        name="attend",
    )(x, *extras, weight, q_bias, v_bias, live_col)


BLOCK = 224


def row_block(lanes):
    return pl.BlockSpec((BLOCK, lanes), lambda i: (i, 0))


def real_rows(rows):
    place = pl.program_id(0) * BLOCK + lax.broadcasted_iota(jnp.int32, (BLOCK, 1), 0)
    return place < rows


def hidden_kernel(rows, mix_ref, x_ref, cot_ref, live_ref, w_ref, vec_ref,
                  attn_ref, hidden_ref, normed_ref, gm_ref, sig_ref):
    x = x_ref[...].astype(F32)
    attention = mm(mix_ref[...], w_ref[...], NN) + vec_ref[2:3, :]
    sig = jax.nn.sigmoid(jnp.sum(x * vec_ref[3:4, :], axis=-1, keepdims=True))
    gate = live_ref[...] * sig
    hidden = x + gate * attention
    scaled, _ = norm_parts(hidden)
    real = real_rows(rows)
    attn_ref[...] = attention
    hidden_ref[...] = hidden
    normed_ref[...] = jnp.where(real, scaled * vec_ref[4:5, :] + vec_ref[5:6, :], 0.0).astype(BF16)
    gm_ref[...] = jnp.where(real, gate * cot_ref[...].astype(F32), 0.0).astype(BF16)
    sig_ref[...] = sig


def hidden_call(mix, x, cot, live_col, weight, vecs):
    rows, dim = x.shape
    steps = -(-rows // BLOCK)
    args = (mix, x, cot, live_col, weight, vecs)
    shapes = [((rows, dim), F32), ((rows, dim), F32), ((steps * BLOCK, dim), BF16), ((steps * BLOCK, dim), BF16),
              ((rows, 1), F32)]
    return pl.pallas_call(
        functools.partial(hidden_kernel, rows),
        in_specs=[row_block(a.shape[1]) for a in args[:4]] + [whole(a.shape) for a in args[4:]],
        out_specs=[row_block(s[1]) for s, _ in shapes],
        grid=(steps,),
        out_shape=[(pltpu.HBM if d == F32 and s[1] == dim else jax.ShapeDtypeStruct)(s, d) for s, d in shapes],
        compiler_params=params(),
        cost_estimate=cost(7),
        name="hidden",
    )(*args)


def ff_kernel(n2_ref, gm_ref, a_ref, b_ref, bias_ref, mlp_ref, gn2_ref, da_ref, db_ref, dbias_ref,
              w1, w2, act_all, pre_all):
    half = w1.shape[0] // 2
    for i, piece in enumerate((a_ref, b_ref)):
        at = i * half
        w1[:, at : at + half] = piece[:, :half]
        w2[at : at + half, :half] = piece[:half, half:]
        w2[at : at + half, half:] = piece[half:, half:]
    steps = 2
    size = n2_ref.shape[0] // steps
    sums = 0.0
    for step in range(steps):
        at = slice(step * size, (step + 1) * size)
        pre = mm(n2_ref[at, :], w1[...], NN) + bias_ref[...]
        grad_act = mm(gm_ref[at, :], w2[...], NT)
        cdf = 0.5 * (1.0 + lax.erf(pre * (0.5**0.5)))
        slope = cdf + pre * (jnp.exp(-0.5 * pre * pre) * (0.5 / jnp.pi) ** 0.5)
        grad_pre = (grad_act * slope).astype(BF16)
        act_all[at, :] = (pre * cdf).astype(BF16)
        pre_all[at, :] = grad_pre
        sums = sums + jnp.sum(grad_pre.astype(F32), axis=0, keepdims=True)
        mlp_ref[at, :] = mm(act_all[at, :], w2[...], NN).astype(BF16)
        gn2_ref[at, :] = mm(pre_all[at, :], w1[...], NT).astype(BF16)
    dbias_ref[...] = sums
    d2 = mm(act_all[...], gm_ref[...], TN).astype(BF16)
    d1 = mm(n2_ref[...], pre_all[...], TN).astype(BF16)
    for i, grad in enumerate((da_ref, db_ref)):
        at = i * half
        grad[:, :half] = d1[:, at : at + half]
        grad[:half, half:] = d2[at : at + half, :half]
        grad[half:, half:] = d2[at : at + half, half:]


def ff_call(n2, gm, pieces, bias):
    rows, dim = n2.shape
    tall, square, line = whole((rows, dim)), whole((dim, dim)), whole((1, dim))
    out = pl.pallas_call(
        ff_kernel,
        grid=(1,),
        in_specs=[tall, tall, square, square, line],
        out_specs=[tall, tall, square, square, line],
        out_shape=[pltpu.HBM((rows, dim), BF16)] * 2
        + [pltpu.HBM((dim, dim), BF16)] * 2
        + [jax.ShapeDtypeStruct((1, dim), F32)],
        scratch_shapes=[pltpu.VMEM((dim, dim), BF16)] * 2 + [pltpu.VMEM((rows, dim), BF16)] * 2,
        compiler_params=params(),
        cost_estimate=cost(12),
        name="feed",
    )(n2, gm, *pieces, bias.reshape(1, dim))
    return out[:2], out[2:4], out[4].reshape(2, dim // 2)


def middle_kernel(rows, parts, *refs):
    mlp_refs, gn2_refs = refs[:parts], refs[parts : 2 * parts]
    (hidden_ref, attn_ref, x_ref, cot_ref, live_ref, sig_ref, gm_ref, mix_ref, w_ref, vec_ref,
     block_ref, carry_ref, near_ref, far_ref, dw_near_ref, dw_far_ref, sum_ref, acc_ref) = refs[2 * parts :]
    step = pl.program_id(0)
    real = real_rows(rows)
    x = x_ref[...].astype(F32)
    cot = cot_ref[...].astype(F32)
    sig = sig_ref[...]
    gate = live_ref[...] * sig
    hidden = hidden_ref[...]
    mlp = vec_ref[6:7, :]
    gn2 = 0.0
    for ref in mlp_refs:
        mlp = mlp + ref[...].astype(F32)
    for ref in gn2_refs:
        gn2 = gn2 + ref[...].astype(F32)
    block_ref[...] = (hidden + gate * mlp).astype(BF16)
    scaled, inv = norm_parts(hidden)
    e = gn2 * vec_ref[4:5, :]
    grad_hidden = cot + inv * (
        e - jnp.mean(e, axis=-1, keepdims=True) - scaled * jnp.mean(e * scaled, axis=-1, keepdims=True)
    )
    gate_grad = jnp.sum(grad_hidden * attn_ref[...] + cot * mlp, axis=-1, keepdims=True)
    logit = live_ref[...] * gate_grad * sig * (1.0 - sig)
    carry_ref[...] = grad_hidden + logit * vec_ref[3:4, :]
    grad_attn = jnp.where(real, gate * grad_hidden, 0.0).astype(BF16)
    half = near_ref.shape[1]
    near_ref[...] = mm(grad_attn, w_ref[:half, :], NT).astype(BF16)
    far_ref[...] = mm(grad_attn, w_ref[half:, :], NT).astype(BF16)
    mix = jnp.where(real, mix_ref[...].astype(F32), 0.0).astype(BF16)
    update = mm(mix, grad_attn, TN)
    add = lambda v: jnp.sum(jnp.where(real, v, 0.0), axis=0, keepdims=True)
    sums = jnp.concatenate(
        [add(gn2 * scaled), add(gn2), add(grad_attn.astype(F32)), add(gm_ref[...].astype(F32)), add(x * logit),
         jnp.zeros((3, x.shape[1]), F32)], axis=0)

    @pl.when(step == 0)
    def _():
        acc_ref[...] = update
        sum_ref[...] = sums

    @pl.when(step > 0)
    def _():
        acc_ref[...] += update
        sum_ref[...] += sums

    @pl.when(step == pl.num_programs(0) - 1)
    def _():
        dw_near_ref[...] = acc_ref[:half, :].astype(BF16)
        dw_far_ref[...] = acc_ref[half:, :].astype(BF16)


def middle_call(mlp, gn2, *args):
    x, weight, vecs = args[2], args[8], args[9]
    rows, dim = x.shape
    half = dim // 2
    shapes = [((rows, dim), BF16), ((rows, dim), F32), ((rows, half), BF16), ((rows, half), BF16)]
    ins = (*mlp, *gn2, *args)
    return pl.pallas_call(
        functools.partial(middle_kernel, rows, len(mlp)),
        in_specs=[row_block(a.shape[1]) for a in ins[:-2]] + [whole(weight.shape), whole(vecs.shape)],
        out_specs=[row_block(s[1]) for s, _ in shapes] + [whole((half, dim))] * 2 + [whole((8, dim))],
        grid=(-(-rows // BLOCK),),
        out_shape=[pltpu.HBM(s, d) for s, d in shapes]
        + [pltpu.HBM((half, dim), BF16)] * 2
        + [jax.ShapeDtypeStruct((8, dim), F32)],
        scratch_shapes=[pltpu.VMEM((dim, dim), F32)],
        compiler_params=params(60 * MIB),
        cost_estimate=cost(11),
        name="middle",
    )(*ins)


def attend_back_kernel(*refs):
    qkv_ref, mix_ref, lse_ref, gmix_ref, live_ref, normed_ref, w_ref, dw_ref, gp_ref, bias_ref, vec_ref, gp_all = refs
    rows = qkv_ref.shape[0]
    third = w_ref.shape[0] // 3
    step = pl.program_id(0)
    lane = lax.broadcasted_iota(jnp.int32, (rows, 128), 1)
    key_bias = jnp.where(live_ref[...] > 0, 0.0, -1e30)
    lse_all = lse_ref[...]
    one = jnp.ones((rows, 1), F32)
    sums = []
    start = 0
    for pair in range(2):
        base = pair * 128
        width = min(128, third - base)
        q_pair = qkv_ref[:, base : base + 128].astype(F32)
        k_pair = qkv_ref[:, 256 + base : 384 + base].astype(F32)
        v_pair = qkv_ref[:, 512 + base : 640 + base].astype(F32)
        m_pair = mix_ref[:, base : base + 128].astype(F32)
        g_pair = gmix_ref[:, base : base + width].astype(F32)
        if width < 128:
            g_pair = jnp.concatenate([g_pair, jnp.zeros((rows, 128 - width), F32)], axis=1)
        gq = jnp.zeros((rows, 128), F32)
        gk = jnp.zeros((rows, 128), F32)
        gv = jnp.zeros((rows, 128), F32)
        for side in range(width // 64):
            inside = (lane >= side * 64) & (lane < side * 64 + 64)
            extra = 64 - side * 64
            lse = jnp.sum(jnp.where(lane == pair * 2 + side, lse_all, 0.0), axis=-1, keepdims=True)
            delta = jnp.sum(jnp.where(inside, g_pair * m_pair, 0.0), axis=-1, keepdims=True)
            l0, l1, l2 = split_three(lse)
            d0, d1, d2 = split_three(delta)
            q_ext = jnp.where(inside, q_pair, pick(lane, extra, (-l0, -l1, -l2, one), 0.0)).astype(BF16)
            k_ext = jnp.where(inside, k_pair, pick(lane, extra, (one, one, one, key_bias), 0.0)).astype(BF16)
            g_ext = jnp.where(inside, g_pair, pick(lane, extra, (-d0, -d1, -d2), 0.0)).astype(BF16)
            v_ext = jnp.where(inside, v_pair, pick(lane, extra, (one, one, one), 0.0)).astype(BF16)
            q_own = jnp.where(inside, q_pair, 0.0).astype(BF16)
            k_own = jnp.where(inside, k_pair, 0.0).astype(BF16)
            g_own = jnp.where(inside, g_pair, 0.0).astype(BF16)
            probs = jnp.exp(mm(k_ext, q_ext, NT))
            grad_scores = (probs * mm(v_ext, g_ext, NT)).astype(BF16)
            gv = gv + mm(probs.astype(BF16), g_own, NN)
            gk = gk + mm(grad_scores, q_own, NN)
            gq = gq + mm(grad_scores, k_own, TN)
        line = []
        for grad in (gq * HEAD**-0.5, gk, gv):
            piece = grad.astype(BF16)[:, :width]
            gp_ref[:, start : start + width] = piece
            line.append(jnp.sum(piece.astype(F32), axis=0, keepdims=True))
            start += width
        sums.append(jnp.concatenate(line, axis=0))
    gp_ref[:, start:] = jnp.zeros((rows, gp_ref.shape[1] - start), BF16)
    gp_all[pl.ds(pl.multiple_of(step * rows, 16), rows), :] = gp_ref[...]
    sums = jnp.concatenate(sums, axis=1)

    @pl.when(step == 0)
    def _():
        bias_ref[...] = sums

    @pl.when(step > 0)
    def _():
        bias_ref[...] += sums

    @pl.when(step == pl.num_programs(0) - 1)
    def _():
        update = mm(gp_all[...], normed_ref[...], TN)[: w_ref.shape[0], :]
        dw_ref[...] = update.astype(BF16)
        column = jnp.zeros((1, w_ref.shape[1]), F32)
        product = jnp.zeros((1, w_ref.shape[1]), F32)
        for part in range(3):
            terms = jnp.concatenate(split_three(bias_ref[part : part + 1, :]), axis=0).astype(BF16)
            rows_w = w_ref[part * third : (part + 1) * third, :]
            column = column + jnp.sum(mm(terms, rows_w, NN), axis=0, keepdims=True)
            lone = third - 128
            pair_rows = update[part * 128 : part * 128 + 128, :]
            lone_rows = update[3 * 128 + part * lone : 3 * 128 + (part + 1) * lone, :]
            own = jnp.concatenate([pair_rows, lone_rows], axis=0) * rows_w.astype(F32)
            product = product + jnp.sum(own, axis=0, keepdims=True)
        vec_ref[0:1, :] = product
        vec_ref[1:2, :] = column


def attend_back_call(qkv, mix, lse, gmix, live_col, normed, weight):
    rows, dim = normed.shape
    height = weight.shape[0]
    columns = -(-height // 128) * 128
    block = lambda lanes: pl.BlockSpec((SEQ, lanes), lambda i: (i, 0))
    ins = [qkv, mix, lse, gmix, live_col, normed, weight]
    return pl.pallas_call(
        attend_back_kernel,
        grid=(rows // SEQ,),
        in_specs=[block(a.shape[1]) for a in ins[:5]] + [whole(normed.shape), whole(weight.shape)],
        out_specs=[whole((height, dim)), block(columns), whole((3, height // 3)), whole((2, dim))],
        out_shape=[
            pltpu.HBM((height, dim), BF16),
            pltpu.HBM((rows, columns), BF16),
            jax.ShapeDtypeStruct((3, height // 3), F32),
            jax.ShapeDtypeStruct((2, dim), F32),
        ],
        scratch_shapes=[pltpu.VMEM((rows, columns), BF16)],
        compiler_params=params(),
        cost_estimate=cost(21),
        name="attend_back",
    )(*ins)


def last_kernel(groups, *refs):
    gp_refs, w_refs = refs[:groups], refs[groups : 2 * groups]
    x_ref, carry_ref, vec_ref, grad_ref = refs[2 * groups : 2 * groups + 4]
    scratch = refs[2 * groups + 4 :]

    @pl.when(pl.program_id(0) == 0)
    def _():
        for w_ref, to_ref in zip(w_refs, scratch):
            third = w_ref.shape[0] // 3
            start = 0
            base = 0
            for size in (128, third - 128):
                for part in range(3):
                    to_ref[start : start + size, :] = w_ref[part * third + base : part * third + base + size, :]
                    start += size
                base += size
            to_ref[start:, :] = jnp.zeros((to_ref.shape[0] - start, to_ref.shape[1]), BF16)

    gn = 0.0
    for gp_ref, to_ref in zip(gp_refs, scratch):
        gn = gn + mm(gp_ref[...], to_ref[...], NN)
    scaled, inv = norm_parts(x_ref[...].astype(F32))
    f = gn * vec_ref[0:1, :]
    grad_ref[...] = carry_ref[...] + inv * (
        f - jnp.mean(f, axis=-1, keepdims=True) - scaled * jnp.mean(f * scaled, axis=-1, keepdims=True)
    )


def last_call(groups, x, carry, vecs):
    rows, dim = x.shape
    gps = [g for _, g in groups]
    weights = [w for w, _ in groups]
    return pl.pallas_call(
        functools.partial(last_kernel, len(groups)),
        in_specs=[row_block(g.shape[1]) for g in gps]
        + [whole(w.shape) for w in weights]
        + [row_block(dim), row_block(dim), whole(vecs.shape)],
        out_specs=row_block(dim),
        grid=(-(-rows // BLOCK),),
        out_shape=jax.ShapeDtypeStruct((rows, dim), F32),
        scratch_shapes=[pltpu.VMEM((g.shape[1], dim), BF16) for g in gps],
        compiler_params=params(60 * MIB),
        cost_estimate=cost(9),
        name="last",
    )(*gps, *weights, x, carry, vecs)


def total(*terms):
    out = terms[0].astype(F32)
    for term in terms[1:]:
        out = out + term.astype(F32)
    return out.astype(BF16)


def after(first, *rest):
    return lax.optimization_barrier((first, *rest))


def unxor(value, index):
    count = value.shape[0]
    bit = 1
    while bit < count:
        split = value.reshape(count // (2 * bit), 2, bit, *value.shape[1:])
        value = jnp.where((index // bit) % 2 == 1, jnp.flip(split, 1), split).reshape(value.shape)
        bit *= 2
    return value


def stages(size):
    out = []
    stride = 2
    while stride < size:
        radix = 4 if size % (stride * 4) == 0 else 2
        out.append((stride, radix))
        stride *= radix
    return out


def dp_swap(value, size, offset):
    return lax.ppermute(value, "dp", [(i, i ^ offset) for i in range(size)])


def split_rows(value):
    high = value.astype(BF16)
    return jnp.concatenate([high, (value[:2] - high[:2].astype(F32)).astype(BF16)])


def join_rows(value):
    value = value.astype(F32)
    return jnp.concatenate([value[:2] + value[-2:], value[2:-2]])


def scatter_rest(value, size, index):
    for stride, radix in stages(size):
        digit = (index // stride) % radix
        share = value.shape[0] // radix
        cut = lambda o: lax.dynamic_slice_in_dim(value, (digit ^ o) * share, share)
        value = total(cut(0), *[dp_swap(cut(o), size, o * stride) for o in range(1, radix)])
    return value


def rest_bits(size):
    out = []
    bit = 2
    while bit < size:
        out.append(bit)
        bit *= 2
    return out


def scatter_step(value, vec, size, index, bit):
    share = value.shape[0] // 2
    place = (index // bit) % 2
    cut = lambda p: lax.dynamic_slice_in_dim(value, p * share, share)
    got = dp_swap(jnp.concatenate([cut(1 - place), split_rows(vec)]), size, bit)
    return total(cut(place), got[:share]), vec + join_rows(got[share:])


def natural_bits(value, size, index):
    order = 0
    for bit in rest_bits(size):
        order = order * 2 + (index // bit) % 2
    return unxor(value.reshape(size // 2, -1, value.shape[-1]), order).reshape(value.shape)


def gather_rest(value, size):
    parts = [value]
    for stride, radix in reversed(stages(size)):
        value = jnp.concatenate(parts)
        parts = [value] + [dp_swap(value, size, o * stride) for o in range(1, radix - 1)]
        parts.append(dp_swap(value, size, (radix - 1) * stride))
    return parts


def natural_rest(value, size, index):
    order = 0
    for stride, radix in stages(size):
        order = order * radix + (index // stride) % radix
    blocks = value.reshape(size // 2, -1, value.shape[-1])
    return unxor(blocks, order).reshape(value.shape)


def scatter_side(value, side, size):
    half = value.shape[0] // 2
    send = lax.dynamic_slice_in_dim(value, (1 - side) * half, half)
    keep = lax.dynamic_slice_in_dim(value, side * half, half)
    return total(keep, dp_swap(send, size, 1))


def sum_tp(value):
    return value + sum(lax.ppermute(value, "tp", [(i, i ^ o) for i in range(4)]) for o in range(1, 4))


def body(
    size,
    tokens, cotangent, patch_rank, kept_counts, norm1_gain, norm1_shift, qkv_weight, query_bias, value_bias,
    out_weight, out_bias, router_weight, norm2_gain, norm2_shift, fc1_weight, fc1_bias, fc2_weight, fc2_bias,
):
    rows, dim = tokens.shape
    half = dim // 2
    images = patch_rank.shape[0]
    tp_index = lax.axis_index("tp")
    index = lax.axis_index("dp")
    core = tp_index % 2
    chip = tp_index // 2
    side = index % 2
    core_swap = lambda v: lax.ppermute(v, "tp", CORE_SWAP)
    y_swap = lambda v: lax.ppermute(v, "tp", Y_SWAP)
    x_swap = lambda v: dp_swap(v, size, 1)
    row_vec = lambda v: v.astype(F32).reshape(1, -1)

    width = out_weight.shape[0]
    qkv_own = jnp.transpose(qkv_weight, (1, 2, 0)).reshape(-1, dim)
    tokens_other = core_swap(tokens)
    qkv_y = y_swap(qkv_own)
    out_y = y_swap(out_weight)
    vecs = lines_call([norm1_gain, norm1_shift, out_bias, router_weight, norm2_gain, norm2_shift, fc2_bias], dim)
    small_own = lines_call([query_bias, value_bias, fc1_bias], dim)
    small_y = y_swap(small_own)

    padded = jnp.concatenate([patch_rank, jnp.full((images, SEQ - PATCHES), PATCHES, jnp.int32)], axis=1)
    live_image = (padded < kept_counts[:, None]).astype(F32)
    live_chip = lax.dynamic_slice_in_dim(live_image, chip * (images // 2), images // 2).reshape(-1, 1)
    live_own = lax.dynamic_slice_in_dim(live_chip, core * rows, rows)

    def pack(s):
        w1 = lax.dynamic_slice_in_dim(fc1_weight, s * half, half, axis=1)
        w2 = lax.dynamic_slice_in_dim(fc2_weight, s * half, half)
        return jnp.concatenate([w1, jnp.concatenate([w2[:, :half], w2[:, half:]])], axis=1)

    own_k, own_s = pack(side), pack(1 - side)
    core_line = jnp.full((1, dim), core, jnp.int32)
    normed, qkv_a, mix_a, lse_a = attend_call(
        tokens, (tokens_other, core_line, vecs), qkv_own, small_own[0:1, :width], small_own[1:2, :width], live_chip
    )
    normed, qkv_y, small_y, own_k, own_s, out_y = after(normed, qkv_y, small_y, own_k, own_s, out_y)
    out_yd = core_swap(out_y)
    y_k = y_swap(own_k)
    core_k, core_s, out_core, qkv_core = [core_swap(v) for v in (own_k, own_s, out_weight, qkv_own)]
    small_far = core_swap(jnp.stack([small_own, small_y]))

    qkv_b, mix_b, lse_b = attend_call(normed, (), qkv_y, small_y[0:1, :width], small_y[1:2, :width], live_chip)
    part = lambda v, s: lax.dynamic_slice(v, (s * rows, 0), (rows, width))
    send_mix = jnp.concatenate([part(mix_a, 1 - core), part(mix_b, 1 - core)], axis=1)
    mix_rows = jnp.concatenate([part(mix_a, core), part(mix_b, core), core_swap(send_mix)], axis=1)
    out_all = jnp.concatenate([out_weight, out_y, out_core, out_yd], axis=0)

    attn, hidden, n2, gm, sig = hidden_call(mix_rows, tokens, cotangent, live_own, out_all, vecs)
    n2, y_k, qkv_core, small_far = after(n2, y_k, qkv_core, small_far)
    y_s = x_swap(y_k)
    yd_k = core_swap(y_k)
    qkv_yd = core_swap(qkv_y)
    halves = lambda v: unxor(v[2].reshape(2, half), side)
    b_own, b_y, b_core, b_yd = halves(small_own), halves(small_y), halves(small_far[0]), halves(small_far[1])

    sums1, (dy_k, dyd_k), fb1 = ff_call(n2, gm, (y_k, yd_k), jnp.stack([b_y[0], b_yd[0]]))
    n2, dyd_k, dy_k, qkv_yd = after(n2, dyd_k, dy_k, qkv_yd)
    ryd_k = core_swap(dyd_k)
    sums2, (do_s, dc_s), fb2 = ff_call(n2, gm, (own_s, core_s), jnp.stack([b_own[1], b_core[1]]))
    n2, do_s, dc_s, ryd_k, y_s = after(n2, do_s, dc_s, ryd_k, y_s)
    rc_s = core_swap(dc_s)
    yd_s = core_swap(y_s)
    y_k_sum = total(dy_k, ryd_k)
    own_s_sum = total(do_s, rc_s)
    n2, y_k_sum, own_s_sum, yd_s = after(n2, y_k_sum, own_s_sum, yd_s)
    from_y_k = [y_swap(y_k_sum[:half])]
    from_x = [x_swap(own_s_sum[:half])]
    sums3, (dy_s, dyd_s), fb3 = ff_call(n2, gm, (y_s, yd_s), jnp.stack([b_y[1], b_yd[1]]))
    n2, dy_s, dyd_s, from_y_k[0], from_x[0] = after(n2, dy_s, dyd_s, from_y_k[0], from_x[0])
    y_k_sum, own_s_sum, n2 = after(y_k_sum, own_s_sum, n2)
    from_y_k.append(y_swap(y_k_sum[half:]))
    from_x.append(x_swap(own_s_sum[half:]))
    ryd_s = core_swap(dyd_s)
    sums4, (do_k, dc_k), fb4 = ff_call(n2, gm, (own_k, core_k), jnp.stack([b_own[0], b_core[0]]))
    sums4, do_k, dc_k, ryd_s, from_x[1], from_y_k[1] = after(sums4, do_k, dc_k, ryd_s, from_x[1], from_y_k[1])
    from_x, from_y_k = jnp.concatenate(from_x), jnp.concatenate(from_y_k)
    y_s_sum = total(dy_s, ryd_s)
    sums4, y_s_sum = after(sums4, y_s_sum)
    over_x = x_swap(y_s_sum[:half])
    over_y = y_swap(y_s_sum[half:])
    rc_k = core_swap(dc_k)

    four = (sums1, sums2, sums3, sums4)
    block_out, carry, gmix, gmix_far, d_out, d_out_far, vec2 = middle_call(
        [f[0] for f in four], [f[1] for f in four], hidden, attn, tokens, cotangent, live_own, sig, gm, mix_rows,
        out_all, vecs,
    )
    gmix, gmix_far, d_out_far, rc_k, vec2, over_x, over_y = after(
        gmix, gmix_far, d_out_far, rc_k, vec2, over_x, over_y
    )
    gmix_other = core_swap(gmix_far)
    rd_out = core_swap(d_out_far)

    join = lambda lo: jnp.where(
        core == 0,
        jnp.concatenate([gmix[:, lo : lo + width], gmix_other[:, lo : lo + width]]),
        jnp.concatenate([gmix_other[:, lo : lo + width], gmix[:, lo : lo + width]]),
    )
    gmix_a, gmix_b = join(0), join(width)
    rows_of = lambda v, s: lax.dynamic_slice_in_dim(v, s * rows, rows)

    over_xy = y_swap(over_x)
    over_yx = x_swap(over_y)
    gmix_b, rd_out = after(gmix_b, rd_out)
    d_out_half = total(d_out, rd_out)
    gmix_b, d_out_half = after(gmix_b, d_out_half)
    out_from_y = y_swap(d_out_half[width:])
    dy, gy, sy, vy = attend_back_call(qkv_b, mix_b, lse_b, gmix_b, live_chip, normed, qkv_y)
    gmix_a, dy, gy, over_xy, over_yx, out_from_y = after(gmix_a, dy, gy, over_xy, over_yx, out_from_y)
    ff_k = total(do_k, rc_k, from_y_k, from_x, jnp.concatenate([over_xy, over_yx]))
    gmix_a, ff_k = after(gmix_a, ff_k)
    ff_share = scatter_rest(ff_k, size, index)
    from_y = y_swap(dy)
    rgy = core_swap(rows_of(gy, 1 - core))

    do, go, so, vo = attend_back_call(qkv_a, mix_a, lse_a, gmix_a, live_chip, normed, qkv_own)
    do, go, so, vo, from_y, rgy, ff_share = after(do, go, so, vo, from_y, rgy, ff_share)
    ff_parts = gather_rest(ff_share, size)
    rgo = core_swap(rows_of(go, 1 - core))
    qo_own = jnp.concatenate([total(do, from_y), total(d_out_half[:width], out_from_y)])
    qo_keep = scatter_side(qo_own, side, size)
    fb_k, fb_s = jnp.stack([fb4[0], fb4[1], fb1[0], fb1[1]]), jnp.stack([fb2[0], fb2[1], fb3[0], fb3[1]])
    fb = unxor(jnp.stack([fb_k, fb_s]), side).transpose(1, 0, 2).reshape(4, dim)
    qv = lambda v: jnp.concatenate([v[0], v[2]])
    zero = jnp.zeros((2 * width,), F32)
    qv_rows = unxor(jnp.stack([qv(so), zero, qv(sy), zero]), tp_index).reshape(2, dim)
    lines = [vy + vo, vec2[:5], unxor(fb, tp_index), qv_rows, jnp.zeros((1, dim), F32)]
    ready = len(ff_parts) - 1
    lines, *early = after(jnp.concatenate(lines), *ff_parts[:ready])
    vec = sum_tp(lines)
    rgo, qo_keep, carry, vec = after(rgo, qo_keep, carry, vec)
    bits = rest_bits(size)
    ff_near = jnp.concatenate(early)
    ff_other = x_swap(ff_near)
    qo_share, vec = scatter_step(qo_keep, vec, size, index, bits[0])
    keep = lambda v: rows_of(v, core)
    input_grad = last_call(
        ((qkv_y, keep(gy)), (qkv_yd, rgy), (qkv_own, keep(go)), (qkv_core, rgo)), tokens, carry, vecs
    )
    input_grad, qo_share, vec, ff_far = after(input_grad, qo_share, vec, ff_parts[ready])
    for bit in bits[1:]:
        qo_share, vec = scatter_step(qo_share, vec, size, index, bit)
    vec, ff_far, ff_other = after(vec, ff_far, ff_other)
    qo_mine = qo_share
    for bit in reversed(bits):
        qo_mine = jnp.concatenate([qo_mine, dp_swap(qo_mine, size, bit)])
    swapped = x_swap(jnp.concatenate([ff_far, split_rows(vec)]))
    vec = vec + join_rows(swapped[ff_far.shape[0] :])
    ff_mine = jnp.concatenate([ff_near, ff_far])
    ff_other = jnp.concatenate([ff_other, swapped[: ff_far.shape[0]]])
    qo_both = unxor(jnp.stack([qo_mine, x_swap(qo_mine)]), side)
    qo_both = jax.vmap(lambda v: natural_bits(v, size, index))(qo_both).reshape(-1, dim)
    first = 3 * 128

    gain_one, shift_one = vecs[0], vecs[1]
    qv_grad = lax.dynamic_index_in_dim(vec[11:13].reshape(4, 2, width), tp_index, keepdims=False)
    fb_grad = lax.dynamic_index_in_dim(vec[:11], 7 + tp_index, keepdims=False)
    ff_both = unxor(jnp.stack([natural_rest(ff_mine, size, index), natural_rest(ff_other, size, index)]), side)
    ff_both = ff_both.astype(F32)
    fc1_grad = jnp.concatenate([ff_both[0, :, :half], ff_both[1, :, :half]], axis=1)
    second = lambda v: jnp.concatenate([v[:half, half:], v[half:, half:]], axis=1)
    fc2_grad = jnp.concatenate([second(ff_both[0]), second(ff_both[1])], axis=0)
    pair_part = qo_both[:first].reshape(3, 128, dim)
    last_part = qo_both[first : 3 * width].reshape(3, width - 128, dim)
    qkv_grad = jnp.concatenate([pair_part, last_part], axis=1).astype(F32)
    return (
        block_out,
        input_grad,
        (vec[0] - shift_one * vec[1]) / gain_one,
        vec[1],
        jnp.transpose(qkv_grad, (2, 0, 1)),
        qv_grad[0],
        qv_grad[1],
        qo_both[3 * width :].astype(F32),
        vec[4],
        vec[6],
        vec[2],
        vec[3],
        fc1_grad,
        fb_grad,
        fc2_grad,
        vec[5],
    )


def solution(mesh):
    return jax.shard_map(
        functools.partial(body, mesh.shape["dp"]),
        mesh=mesh,
        in_specs=(
            P(("dp", "tp"), None), P(("dp", "tp"), None), P("dp", None), P("dp"), P(), P(), P(None, None, "tp"),
            P("tp"), P("tp"), P("tp", None), P(), P(), P(), P(), P(None, "tp"), P("tp"), P("tp", None), P(),
        ),
        out_specs=(
            P(("dp", "tp"), None), P(("dp", "tp"), None), P(), P(), P(None, None, "tp"), P("tp"), P("tp"),
            P("tp", None), P(), P(), P(), P(), P(None, "tp"), P("tp"), P("tp", None), P(),
        ),
        check_vma=False,
    )
```
